32 devices in a mesh: dp: 8 (over z, x), fsdp: 4 (over y, core).
Axes of the slice: x: 2, y: 2, z: 4, core: 2. Of those that a mesh axis runs over, the one named last changes fastest.
Arguments:
- x_now: float32 [32768, 78], P(('dp', 'fsdp'))
- x_next: float32 [32768, 78], P(('dp', 'fsdp'))
- node_counts: int32 [64], P(('dp', 'fsdp')), may hold values from 138 to 512, as said below
- border_flag: int32 [32768], P(('dp', 'fsdp')), may hold values 0 or 1
- source_vertex: int32 [64, 3072], P(('dp', 'fsdp')), may hold values from 0 to 511, as said below
- target_vertex: int32 [64, 3072], P(('dp', 'fsdp')), may hold values from 0 to 511, as said below
- link_features: float32 [64, 3072, 4], P(('dp', 'fsdp')), may hold values from -5 to 5
- level_ids: int32 [78], replicated, may hold values from 0 to 12
- encoder: float32 [78, 256], P(None, 'fsdp'), may hold values from -0.625 to 0.625
- edge_encoder: float32 [4, 256], P(None, 'fsdp'), may hold values from -3 to 3
- edge_first: float32 [3, 768, 256], P(None, 'fsdp'), may hold values from -0.21875 to 0.21875
- second_layers: float32 [3, 2, 256, 256], P(None, None, 'fsdp'), may hold values from -0.375 to 0.375
- node_first: float32 [3, 512, 256], P(None, 'fsdp'), may hold values from -0.25 to 0.25
- vectors: float32 [3, 2, 4, 256], P(None, None, None, 'fsdp'), as said below
- decoder: float32 [256, 78], P('fsdp'), may hold values from -0.375 to 0.375
- encoder_moment: float32 [78, 256], P(None, 'fsdp'), may hold values from -9.1552734e-05 to 9.1552734e-05
- edge_encoder_moment: float32 [4, 256], P(None, 'fsdp'), may hold values from -9.1552734e-05 to 9.1552734e-05
- edge_first_moment: float32 [3, 768, 256], P(None, 'fsdp'), may hold values from -9.1552734e-05 to 9.1552734e-05
- second_layers_moment: float32 [3, 2, 256, 256], P(None, None, 'fsdp'), may hold values from -9.1552734e-05 to 9.1552734e-05
- node_first_moment: float32 [3, 512, 256], P(None, 'fsdp'), may hold values from -9.1552734e-05 to 9.1552734e-05
- vectors_moment: float32 [3, 2, 4, 256], P(None, None, None, 'fsdp'), may hold values from -9.1552734e-05 to 9.1552734e-05
- decoder_moment: float32 [256, 78], P('fsdp'), may hold values from -9.1552734e-05 to 9.1552734e-05
- encoder_square: float32 [78, 256], P(None, 'fsdp'), may hold values from 9.155413e-12 to 1.4648661e-10
- edge_encoder_square: float32 [4, 256], P(None, 'fsdp'), may hold values from 3.6621653e-10 to 1.23598077e-07
- edge_first_square: float32 [3, 768, 256], P(None, 'fsdp'), may hold values from 9.155413e-12 to 1.4648661e-10
- second_layers_square: float32 [3, 2, 256, 256], P(None, None, 'fsdp'), may hold values from 9.155413e-12 to 1.4648661e-10
- node_first_square: float32 [3, 512, 256], P(None, 'fsdp'), may hold values from 9.155413e-12 to 1.4648661e-10
- vectors_square: float32 [3, 2, 4, 256], P(None, None, None, 'fsdp'), may hold values from 9.155413e-12 to 1.4648661e-10
- decoder_square: float32 [256, 78], P('fsdp'), may hold values from 9.155413e-12 to 1.4648661e-10
Outputs:
- loss_sum: float32 [], replicated
- loss_count: float32 [], replicated
- encoder_moment_new: float32 [78, 256], P(None, 'fsdp')
- encoder_square_new: float32 [78, 256], P(None, 'fsdp')
- encoder_new: float32 [78, 256], P(None, 'fsdp')
- edge_encoder_moment_new: float32 [4, 256], P(None, 'fsdp')
- edge_encoder_square_new: float32 [4, 256], P(None, 'fsdp')
- edge_encoder_new: float32 [4, 256], P(None, 'fsdp')
- edge_first_moment_new: float32 [3, 768, 256], P(None, 'fsdp')
- edge_first_square_new: float32 [3, 768, 256], P(None, 'fsdp')
- edge_first_new: float32 [3, 768, 256], P(None, 'fsdp')
- second_layers_moment_new: float32 [3, 2, 256, 256], P(None, None, 'fsdp')
- second_layers_square_new: float32 [3, 2, 256, 256], P(None, None, 'fsdp')
- second_layers_new: float32 [3, 2, 256, 256], P(None, None, 'fsdp')
- node_first_moment_new: float32 [3, 512, 256], P(None, 'fsdp')
- node_first_square_new: float32 [3, 512, 256], P(None, 'fsdp')
- node_first_new: float32 [3, 512, 256], P(None, 'fsdp')
- vectors_moment_new: float32 [3, 2, 4, 256], P(None, None, None, 'fsdp')
- vectors_square_new: float32 [3, 2, 4, 256], P(None, None, None, 'fsdp')
- vectors_new: float32 [3, 2, 4, 256], P(None, None, None, 'fsdp')
- decoder_moment_new: float32 [256, 78], P('fsdp')
- decoder_square_new: float32 [256, 78], P('fsdp')
- decoder_new: float32 [256, 78], P('fsdp')
The draws below stay inside these ranges and needn't reach their ends.
Inputs may be any that keep to these rules, and one draw needn't show every extreme that they name: `node_counts`: the last subgraph is full. `source_vertex`: every sender is a valid node of its subgraph. `target_vertex`: every receiver is a valid node of its subgraph. `vectors`: gains lie in 0.6 to 1.4.
All inputs are finite; a program needn't handle non-finite values. No bound on the sum of `border_flag` on one device may be relied on, other than what follows from the above.
Results may differ from the reference program's by a relative error of at most 0.0038.
The reference program's roundings to bfloat16 on the way count: a program that leaves them out, or rounds other values in their place, can miss the bound.
Values may be sent and summed in bfloat16 or wider, within the bound.
No kernel may reach another device: no remote copies, remote signals or barrier semaphores. Data moves between devices by JAX's collectives and lax.ppermute only.
A program may use at most 256 MiB of HBM per device.

```python
import math
import jax
import jax.numpy as jnp
from jax import lax

LATENT = 256
VARS = 6
LEVELS = 13
VERTEX_WIDTH = 78
LINK_SHAPE_DIM = 4
ROUNDS = 3
PATCH_VERTICES = 512
PATCH_LINKS = 3072
PATCH_AMOUNT = 64
NODES = 32768
STEP = 10


def base_state(key):
    return jnp.clip(jax.random.normal(key, (NODES, VERTEX_WIDTH), jnp.float32), -5.0, 5.0)


def draw_x_now(key, part):
    return base_state(key)


def draw_x_next(key, part):
    start = base_state(key)
    key = jax.random.fold_in(key, 7)
    key_var, key_noise, key_node, key_sign = jax.random.split(key, 4)
    position = jnp.arange(NODES, dtype=jnp.float32) / NODES
    signs = jnp.where(jax.random.uniform(key_sign, (VARS,), jnp.float32) < 0.5, -1.0, 1.0)
    var_scale = jnp.exp(jax.random.uniform(key_var, (VARS,), jnp.float32, -1.4, 1.4))
    noise = jnp.clip(jax.random.normal(key_noise, (NODES, VERTEX_WIDTH), jnp.float32), -4.0, 4.0)
    ramp = 0.5 + position
    offset = 1.0 + 2.0 * position
    noisy_jitter = jnp.exp(jax.random.uniform(key_node, (NODES, 1), jnp.float32, -0.35, 0.35))
    channel_scale = jnp.repeat(var_scale, LEVELS)
    channel_sign = jnp.repeat(signs, LEVELS)
    drift = offset[:, None] * (channel_scale * channel_sign)[None, :]
    return start + noise * channel_scale[None, :] * ramp[:, None] * noisy_jitter + drift


def graph_counts(key):
    key = jax.random.fold_in(key, 11)
    position_number = jnp.arange(PATCH_AMOUNT, dtype=jnp.int32)
    interval_length = max(PATCH_AMOUNT - 1, 1)
    minimum_level = PATCH_VERTICES // 3
    ascending_order = minimum_level + (PATCH_VERTICES - minimum_level) * position_number // interval_length
    noisy_jitter = jax.random.randint(key, (PATCH_AMOUNT,), -(PATCH_VERTICES // 16), PATCH_VERTICES // 16 + 1)
    tally_numbers = jnp.clip(ascending_order + noisy_jitter, 2, PATCH_VERTICES)
    return jnp.where(position_number == PATCH_AMOUNT - 1, PATCH_VERTICES, tally_numbers).astype(jnp.int32)


def draw_node_counts(key, part):
    return graph_counts(key)


def draw_source_vertex(key, part):
    tally_numbers = graph_counts(key)
    key = jax.random.fold_in(key, 21)
    picked_entries = jax.random.randint(key, (PATCH_AMOUNT, PATCH_LINKS), 0, tally_numbers[:, None])
    vertical_slice = jnp.arange(PATCH_LINKS, dtype=jnp.int32)[None, :]
    picked_entries = jnp.where(vertical_slice == 0, tally_numbers[:, None] - 1, picked_entries)
    return jnp.where(vertical_slice == 1, 0, picked_entries).astype(jnp.int32)


def draw_target_vertex(key, part):
    tally_numbers = graph_counts(key)
    key = jax.random.fold_in(key, 22)
    picked_entries = jax.random.randint(key, (PATCH_AMOUNT, PATCH_LINKS), 0, tally_numbers[:, None])
    vertical_slice = jnp.arange(PATCH_LINKS, dtype=jnp.int32)[None, :]
    picked_entries = jnp.where(vertical_slice == 0, 0, picked_entries)
    return jnp.where(vertical_slice == 1, tally_numbers[:, None] - 1, picked_entries).astype(jnp.int32)


def draw_vectors(key, part):
    key = jax.random.fold_in(key, 31)
    key_bias, key_gain = jax.random.split(key)
    shape = (ROUNDS, 2, 4, LATENT)
    biases = 0.3 * jnp.clip(jax.random.normal(key_bias, shape, jnp.float32), -4.0, 4.0)
    gains = jax.random.uniform(key_gain, shape, jnp.float32, 0.6, 1.4)
    row = jnp.arange(4, dtype=jnp.int32)[None, None, :, None]
    return jnp.where(row == 2, gains, biases)


def draw_edge_encoder_square(key, part):
    key = jax.random.fold_in(key, 41)
    inverse_count = 1.0 / (NODES * 2 // 3)
    lower_end = 1.3e-05
    upper_end = 0.0011
    fraction = jax.random.uniform(key, (LINK_SHAPE_DIM, LATENT), jnp.float32)
    return inverse_count * lower_end * jnp.exp(fraction * math.log(upper_end / lower_end))


def with_ends(values, rng, smallest, top_value):
    spot = [jax.random.randint(jax.random.fold_in(rng, axis), (), 0, length) for axis, length in enumerate(values.shape)]
    widest = values.shape.index(max(values.shape))
    beside = spot[:widest] + [(spot[widest] + 1) % values.shape[widest]] + spot[widest + 1:]
    return values.at[tuple(spot)].set(smallest).at[tuple(beside)].set(top_value)


def levels(stream_key, extent, pieces, least, high):
    def one(dim, shards_of):
        heights = jax.random.uniform(jax.random.fold_in(jax.random.fold_in(stream_key, 6), dim), (shards_of,), jnp.float32, least / len(pieces), high / len(pieces))
        return jnp.repeat(jnp.exp(heights), extent[dim] // shards_of).reshape((-1,) + (1,) * (len(extent) - dim - 1))

    level = one(*pieces[0])
    for cut in pieces[1:]:
        level = level * one(*cut)
    return level


def bell_draw(own_key, shape, width, bound, shards=(), held_as=jnp.bfloat16):
    array = jax.random.normal(own_key, shape, jnp.float32) * width
    if len(shards) > 0:
        array = levels(own_key, shape, shards, -0.22, 0.18) * array
    return jnp.clip(array, min=-bound, max=bound).astype(held_as)


def setup_inputs(seed: int = 0) -> dict:
    seeds = jax.random.split(jax.random.key(seed), 30)
    return {
        "x_now": draw_x_now(jax.random.fold_in(seeds[29], 71), 0),
        "x_next": draw_x_next(jax.random.fold_in(seeds[29], 71), 0),
        "node_counts": draw_node_counts(jax.random.fold_in(seeds[29], 71), 0),
        "border_flag": with_ends((jax.random.randint(seeds[3], (NODES,), 0, 6) < 1).astype(jnp.int32), jax.random.fold_in(seeds[3], 1), 0, 1),
        "source_vertex": draw_source_vertex(jax.random.fold_in(seeds[29], 71), 0),
        "target_vertex": draw_target_vertex(jax.random.fold_in(seeds[29], 71), 0),
        "link_features": bell_draw(seeds[6], (PATCH_AMOUNT, PATCH_LINKS, LINK_SHAPE_DIM), 1.0, 5.0, ((0, 32),), jnp.float32),
        "level_ids": with_ends(jax.random.randint(seeds[7], (VERTEX_WIDTH,), 0, LEVELS), jax.random.fold_in(seeds[7], 1), 0, LEVELS - 1).astype(jnp.int32),
        "encoder": bell_draw(seeds[8], (VERTEX_WIDTH, LATENT), VERTEX_WIDTH ** -0.5, 0.625, ((1, 4),), jnp.float32),
        "edge_encoder": bell_draw(seeds[9], (LINK_SHAPE_DIM, LATENT), LINK_SHAPE_DIM ** -0.5, 3.0, ((1, 4),), jnp.float32),
        "edge_first": bell_draw(seeds[10], (ROUNDS, 3 * LATENT, LATENT), (3 * LATENT) ** -0.5, 0.21875, ((1, 4),), jnp.float32),
        "second_layers": bell_draw(seeds[11], (ROUNDS, 2, LATENT, LATENT), LATENT ** -0.5, 0.375, ((2, 4),), jnp.float32),
        "node_first": bell_draw(seeds[12], (ROUNDS, 2 * LATENT, LATENT), (2 * LATENT) ** -0.5, 0.25, ((1, 4),), jnp.float32),
        "vectors": draw_vectors(jax.random.fold_in(seeds[29], 71), 0),
        "decoder": bell_draw(seeds[14], (LATENT, VERTEX_WIDTH), LATENT ** -0.5, 0.375, ((0, 4),), jnp.float32),
        "encoder_moment": bell_draw(seeds[15], (VERTEX_WIDTH, LATENT), (0.0022 * (NODES * 2 // 3) ** -0.5), 9.1552734375e-05, ((1, 4),), jnp.float32),
        "edge_encoder_moment": bell_draw(seeds[16], (LINK_SHAPE_DIM, LATENT), (0.0022 * (NODES * 2 // 3) ** -0.5), 9.1552734375e-05, ((1, 4),), jnp.float32),
        "edge_first_moment": bell_draw(seeds[17], (ROUNDS, 3 * LATENT, LATENT), (0.0022 * (NODES * 2 // 3) ** -0.5), 9.1552734375e-05, ((1, 4),), jnp.float32),
        "second_layers_moment": bell_draw(seeds[18], (ROUNDS, 2, LATENT, LATENT), (0.0022 * (NODES * 2 // 3) ** -0.5), 9.1552734375e-05, ((2, 4),), jnp.float32),
        "node_first_moment": bell_draw(seeds[19], (ROUNDS, 2 * LATENT, LATENT), (0.0022 * (NODES * 2 // 3) ** -0.5), 9.1552734375e-05, ((1, 4),), jnp.float32),
        "vectors_moment": bell_draw(seeds[20], (ROUNDS, 2, 4, LATENT), (0.0022 * (NODES * 2 // 3) ** -0.5), 9.1552734375e-05, ((3, 4),), jnp.float32),
        "decoder_moment": bell_draw(seeds[21], (LATENT, VERTEX_WIDTH), (0.0022 * (NODES * 2 // 3) ** -0.5), 9.1552734375e-05, ((0, 4),), jnp.float32),
        "encoder_square": jnp.clip(jnp.exp(math.log(1.464866145051147e-10) - 2.7725887 * jax.random.uniform(seeds[22], (VERTEX_WIDTH, LATENT), jnp.float32) ** levels(seeds[22], (VERTEX_WIDTH, LATENT), ((1, 4),), -0.2, 0.2)), 9.155413406569668e-12, 1.464866145051147e-10),
        "edge_encoder_square": draw_edge_encoder_square(jax.random.fold_in(seeds[29], 71), 0),
        "edge_first_square": jnp.clip(jnp.exp(math.log(1.464866145051147e-10) - 2.7725887 * jax.random.uniform(seeds[24], (ROUNDS, 3 * LATENT, LATENT), jnp.float32) ** levels(seeds[24], (ROUNDS, 3 * LATENT, LATENT), ((1, 4),), -0.2, 0.2)), 9.155413406569668e-12, 1.464866145051147e-10),
        "second_layers_square": jnp.clip(jnp.exp(math.log(1.464866145051147e-10) - 2.7725887 * jax.random.uniform(seeds[25], (ROUNDS, 2, LATENT, LATENT), jnp.float32) ** levels(seeds[25], (ROUNDS, 2, LATENT, LATENT), ((2, 4),), -0.2, 0.2)), 9.155413406569668e-12, 1.464866145051147e-10),
        "node_first_square": jnp.clip(jnp.exp(math.log(1.464866145051147e-10) - 2.7725887 * jax.random.uniform(seeds[26], (ROUNDS, 2 * LATENT, LATENT), jnp.float32) ** levels(seeds[26], (ROUNDS, 2 * LATENT, LATENT), ((1, 4),), -0.2, 0.2)), 9.155413406569668e-12, 1.464866145051147e-10),
        "vectors_square": jnp.clip(jnp.exp(math.log(1.464866145051147e-10) - 2.7725887 * jax.random.uniform(seeds[27], (ROUNDS, 2, 4, LATENT), jnp.float32) ** levels(seeds[27], (ROUNDS, 2, 4, LATENT), ((3, 4),), -0.2, 0.2)), 9.155413406569668e-12, 1.464866145051147e-10),
        "decoder_square": jnp.clip(jnp.exp(math.log(1.464866145051147e-10) - 2.7725887 * jax.random.uniform(seeds[28], (LATENT, VERTEX_WIDTH), jnp.float32) ** levels(seeds[28], (LATENT, VERTEX_WIDTH), ((0, 4),), -0.2, 0.2)), 9.155413406569668e-12, 1.464866145051147e-10),
    }


norm_eps = 1e-05
stat_eps = 1e-06
beta_one = 0.9
beta_two = 0.999
adam_eps = 1e-08
decay_rate = 0.01
rate_matrix = 0.03
rate_vector = 0.2

@jax.custom_vjp
def reduced_precision(v):
    return lax.optimization_barrier(v.astype(jnp.bfloat16)).astype(jnp.float32)

@jax.custom_vjp
def reduced_reverse(v):
    return v

def low_keep(v):
    return (reduced_precision(v), None)

def low_pass(kept, grad):
    return (grad,)

def back_keep(v):
    return (v, None)

def back_low(kept, grad):
    return (reduced_precision(grad),)
reduced_precision.defvjp(low_keep, low_pass)
reduced_reverse.defvjp(back_keep, back_low)

def matmul(left, right):
    return jnp.dot(left, right, precision=lax.Precision.HIGHEST, preferred_element_type=jnp.float32)

def block_forward(feed_quantities, first, second, vector_rows):
    pre_one = reduced_reverse(matmul(feed_quantities, first) + vector_rows[0])
    active = reduced_precision(jax.nn.silu(pre_one))
    pre_two = reduced_reverse(matmul(active, second) + vector_rows[1])
    centered = pre_two - lax.optimization_barrier(jnp.mean(pre_two, axis=-1, keepdims=True))
    variance = lax.optimization_barrier(jnp.mean(centered * centered, axis=-1, keepdims=True))
    return centered * lax.rsqrt(variance + norm_eps) * vector_rows[2] + vector_rows[3]

def graph_loss(params, item, scale, level_weight):
    encoder, edge_encoder, edge_first, second_layers, node_first, vectors, decoder = params
    feed_quantities, tendency_increment, genuine_flag, source_vertex, target_vertex, link_features = item
    state = reduced_reverse(matmul(reduced_precision(feed_quantities), encoder))
    edge_state = reduced_reverse(matmul(reduced_precision(link_features), edge_encoder))
    link_reduced = reduced_precision(edge_state)
    for index_round in range(ROUNDS):
        node_low = reduced_precision(state)
        from_send = reduced_reverse(jnp.take(node_low, source_vertex, axis=0))
        from_recv = reduced_reverse(jnp.take(node_low, target_vertex, axis=0))
        edge_in = jnp.concatenate([from_send, from_recv, link_reduced], axis=-1)
        edge_state = edge_state + block_forward(edge_in, edge_first[index_round], second_layers[index_round, 0], vectors[index_round, 0])
        link_reduced = reduced_precision(edge_state)
        arriving_messages = reduced_precision(reduced_reverse(jax.ops.segment_sum(link_reduced, target_vertex, num_segments=PATCH_VERTICES)))
        node_in = jnp.concatenate([node_low, arriving_messages], axis=-1)
        state = state + block_forward(node_in, node_first[index_round], second_layers[index_round, 1], vectors[index_round, 1])
    predicted = reduced_reverse(matmul(reduced_precision(state), decoder))
    misfit = (predicted - tendency_increment) * scale[None, :]
    return jnp.sum(level_weight[None, :] * genuine_flag[:, None] * misfit * misfit)

def adam_update(weight, moment, square, gradient, rate):
    moment_new = beta_one * moment + (1.0 - beta_one) * gradient
    square_new = beta_two * square + (1.0 - beta_two) * gradient * gradient
    direction = moment_new / (1.0 - beta_one ** STEP) / (jnp.sqrt(square_new / (1.0 - beta_two ** STEP)) + adam_eps)
    return (moment_new, square_new, weight - rate * (direction + decay_rate * weight))

def reference(x_now, x_next, node_counts, border_flag, source_vertex, target_vertex, link_features, level_ids, encoder, edge_encoder, edge_first, second_layers, node_first, vectors, decoder, encoder_moment, edge_encoder_moment, edge_first_moment, second_layers_moment, node_first_moment, vectors_moment, decoder_moment, encoder_square, edge_encoder_square, edge_first_square, second_layers_square, node_first_square, vectors_square, decoder_square):
    tendency_increment = x_next - x_now
    placeholder_places = jnp.arange(PATCH_VERTICES, dtype=jnp.int32)
    valid = placeholder_places[None, :] < node_counts[:, None]
    driver_vector = border_flag.reshape(PATCH_AMOUNT, PATCH_VERTICES) == 1
    genuine_flag = jnp.where(valid & jnp.logical_not(driver_vector), 1.0, 0.0).astype(jnp.float32).reshape(-1)
    feed_quantities = jnp.where(driver_vector.reshape(-1, 1), x_next, x_now)
    grouped = tendency_increment.reshape(-1, VARS, LEVELS)
    count = jnp.sum(genuine_flag)
    average = lax.optimization_barrier(jnp.sum(grouped * genuine_flag[:, None, None], axis=(0, 2))) / (count * LEVELS)
    centered = (grouped - average[None, :, None]) * genuine_flag[:, None, None]
    variance = lax.optimization_barrier(jnp.sum(centered * centered, axis=(0, 2))) / (count * LEVELS)
    scale = jnp.repeat(lax.rsqrt(variance + stat_eps), LEVELS)
    level_weight = (level_ids.astype(jnp.float32) + 1.0) / LEVELS
    loss_count = count * VERTEX_WIDTH
    drawn_example = (feed_quantities.reshape(PATCH_AMOUNT, PATCH_VERTICES, VERTEX_WIDTH), tendency_increment.reshape(PATCH_AMOUNT, PATCH_VERTICES, VERTEX_WIDTH), genuine_flag.reshape(PATCH_AMOUNT, PATCH_VERTICES), source_vertex, target_vertex, link_features)
    params = (encoder, edge_encoder, edge_first, second_layers, node_first, vectors, decoder)

    def objective(weights):
        low_params = tuple((reduced_precision(weight) for weight in weights))

        def one_graph(total, item):
            return (total + graph_loss(low_params, item, scale, level_weight), None)
        total, unused = lax.scan(jax.checkpoint(one_graph), jnp.zeros((), jnp.float32), drawn_example)
        return (total / loss_count, total)
    unused_value, pullback, loss_sum = jax.vjp(objective, params, has_aux=True)
    gradients = pullback(jnp.ones((), jnp.float32))[0]
    moments = (encoder_moment, edge_encoder_moment, edge_first_moment, second_layers_moment, node_first_moment, vectors_moment, decoder_moment)
    squares = (encoder_square, edge_encoder_square, edge_first_square, second_layers_square, node_first_square, vectors_square, decoder_square)
    rates = (rate_matrix, rate_matrix, rate_matrix, rate_matrix, rate_matrix, rate_vector, rate_matrix)
    results = [adam_update(params[k], moments[k], squares[k], gradients[k], rates[k]) for k in range(7)]
    return (loss_sum, loss_count, results[0][0], results[0][1], results[0][2], results[1][0], results[1][1], results[1][2], results[2][0], results[2][1], results[2][2], results[3][0], results[3][1], results[3][2], results[4][0], results[4][1], results[4][2], results[5][0], results[5][1], results[5][2], results[6][0], results[6][1], results[6][2])
```

```python
import functools

import jax
import jax.numpy as jnp
from jax import lax
from jax.experimental import pallas as pl
from jax.experimental.pallas import tpu as pltpu
from jax.sharding import PartitionSpec as P

VARS = 6
LEVELS = 13
ROUNDS = 3
STEP = 10

norm_eps = 1e-05
stat_eps = 1e-06
beta_one = 0.9
beta_two = 0.999
adam_eps = 1e-08
decay_rate = 0.01
rate_matrix = 0.03
rate_vector = 0.2

BF = jnp.bfloat16
F32 = jnp.float32
VMEM_LIMIT = 56 * 1024 * 1024
EDGE_TILE = 512


def contract(a, b, da, db):
    return lax.dot_general(a, b, (((da,), (db,)), ((), ())), preferred_element_type=F32)


def nn(a, b):
    return contract(a, b, 1, 0)


def nt(a, b):
    return contract(a, b, 1, 1)


def tn(a, b):
    return contract(a, b, 0, 0)


def sigmoid(v):
    return 0.5 * jnp.tanh(0.5 * v) + 0.5


def round_up(v, m):
    return (v + m - 1) // m * m


class Plan:
    def __init__(self, latent, dp_size, fsdp_size):
        self.latent = latent
        self.dp = dp_size
        self.fsdp = fsdp_size
        self.width = latent // fsdp_size
        self.half = self.width // 2
        sizes = (
            ("edge_first", 3 * self.width),
            ("edge_second", self.width),
            ("node_second", self.width),
            ("node_first", 2 * self.width),
            ("rows", 16),
            ("outer", self.half),
        )
        offset = 0
        self.at = {}
        for name, size in sizes:
            self.at[name] = (offset, size)
            offset += size
        self.piece = round_up((offset + dp_size - 1) // dp_size, 16)
        self.used = offset
        self.total = self.piece * dp_size

    def pieces(self, name):
        start, size = self.at[name]
        done = 0
        while done < size:
            at = start + done
            count = min(size - done, self.piece - at % self.piece)
            yield at // self.piece, at % self.piece, done, count
            done += count


def params(**kw):
    return pltpu.CompilerParams(vmem_limit_bytes=VMEM_LIMIT, **kw)


def live_row(border, count):
    place = lax.broadcasted_iota(jnp.int32, border.shape, 1)
    return jnp.where((place < count) & (border != 1), 1.0, 0.0).astype(F32)


def group_matrix(rows, cols, flip):
    var = lax.broadcasted_iota(jnp.int32, (rows, cols), 1 if flip else 0)
    chan = lax.broadcasted_iota(jnp.int32, (rows, cols), 0 if flip else 1)
    inside = (chan >= var * LEVELS) & (chan < (var + 1) * LEVELS)
    return jnp.where(inside, 1.0, 0.0).astype(F32)


def exact(a, b):
    return lax.dot_general(
        a, b, (((1,), (0,)), ((), ())), precision=lax.Precision.HIGHEST, preferred_element_type=F32
    )


def pack_round(plan, out, r, edge_first, second_layers, node_first, vectors, edge_encoder, outer):
    width = plan.width
    at = plan.at

    def put(name, value):
        start, size = at[name]
        out[start : start + size, :] = value.astype(BF)

    put("edge_first", edge_first[r])
    put("edge_second", second_layers[r, 0])
    put("node_second", second_layers[r, 1])
    put("node_first", node_first[r])
    rows = jnp.concatenate([vectors[r, 0], vectors[r, 1]], axis=0)
    if edge_encoder is None:
        low = jnp.zeros((8, width), F32)
    else:
        low = jnp.concatenate([edge_encoder[...], jnp.zeros((4, width), F32)], axis=0)
    rows = jnp.concatenate([rows, low], axis=0)
    rows = jnp.concatenate([rows, jnp.zeros((16, plan.latent - width), F32)], axis=1)
    put("rows", rows)
    start, size = at["outer"]
    if outer is None:
        out[start : start + size, :] = jnp.zeros((size, plan.latent), BF)
    else:
        channels = outer.shape[1]
        wide = jnp.concatenate(
            [outer[...], jnp.zeros((width, plan.latent // 2 - channels), F32)], axis=1
        )
        put("outer", jnp.concatenate([wide[: plan.half], wide[plan.half :]], axis=1))
    if plan.total > plan.used:
        out[plan.used : plan.total, :] = jnp.zeros((plan.total - plan.used, plan.latent), BF)


def pack_first_kernel(plan, ef, sl, nf, vec, ee, enc, out):
    pack_round(plan, out, 0, ef, sl, nf, vec, ee, enc)


def pack_rest_kernel(plan, graphs, counts, ef, sl, nf, vec, dec, x_now, x_next, border, out1, out2, stats):
    pack_round(plan, out1, 1, ef, sl, nf, vec, None, None)
    pack_round(plan, out2, 2, ef, sl, nf, vec, None, dec)
    nodes = x_now.shape[1] // graphs
    channels = x_now.shape[0]
    lives = []
    for g in range(graphs):
        lives.append(live_row(border[:, g * nodes : (g + 1) * nodes], counts[g]))
    live = jnp.concatenate(lives, axis=1)
    delta = x_next[...] - x_now[...]
    count = jnp.sum(live)
    sums = jnp.sum(delta * live, axis=1, keepdims=True)
    to_var = group_matrix(8, channels, False)
    to_chan = group_matrix(channels, 8, True)
    var_sum = exact(to_var, jnp.broadcast_to(sums, (channels, 128)))
    mean = var_sum / (jnp.maximum(count, 1.0) * LEVELS)
    centered = (delta - exact(to_chan, mean)[:, 0:1]) * live
    square = jnp.sum(centered * centered, axis=1, keepdims=True)
    var_square = exact(to_var, jnp.broadcast_to(square, (channels, 128)))
    lane = lax.broadcasted_iota(jnp.int32, (8, 128), 1)
    value = jnp.where(lane == 0, var_sum, jnp.where(lane == 1, var_square, count))
    stats[...] = jnp.broadcast_to(value[None], stats.shape)


def assemble(plan, me, packs, edge_first, edge_second, node_second, node_first, cols, outer):
    width = plan.width
    latent = plan.latent
    total = jnp.zeros((latent, 16), F32)
    rowid = lax.broadcasted_iota(jnp.int32, (latent, width), 0)
    colid = lax.broadcasted_iota(jnp.int32, (latent, width), 1)
    for k, pack in enumerate(packs):
        owner = jnp.bitwise_xor(me, k)

        def put(ref, name, step):
            start, size = plan.at[name]
            ref[pl.ds(pl.multiple_of(owner * step, 16), size), :] = pack[start : start + size, :]

        put(edge_first, "edge_first", 3 * width)
        put(edge_second, "edge_second", width)
        put(node_second, "node_second", width)
        put(node_first, "node_first", 2 * width)
        start, size = plan.at["rows"]
        place = jnp.where(rowid == owner * width + colid, 1.0, 0.0).astype(BF)
        total = total + nt(place, pack[start : start + size, 0:width])
        if outer is not None:
            start, size = plan.at["outer"]
            half = latent // 2
            first = pl.multiple_of(owner * width, 16)
            second = pl.multiple_of(owner * width + plan.half, 16)
            outer[pl.ds(first, size), :] = pack[start : start + size, 0:half]
            outer[pl.ds(second, size), :] = pack[start : start + size, half : 2 * half]
    cols[...] = total


def fill_tables(u_ref, src, dst, nodes, tile):
    place = lax.broadcasted_iota(jnp.int32, (nodes, tile), 0).astype(jnp.int16)
    one = jnp.ones((nodes, tile), BF)
    zero = jnp.zeros((nodes, tile), BF)
    u_ref[0:nodes, :] = jnp.where(place == src.astype(jnp.int16), one, zero)
    u_ref[nodes : 2 * nodes, :] = jnp.where(place == dst.astype(jnp.int16), one, zero)


def norm_forward(z2, count):
    mean = jnp.sum(z2, axis=0, keepdims=True) * (1.0 / count)
    centered = z2 - mean
    var = jnp.sum(centered * centered, axis=0, keepdims=True) * (1.0 / count)
    inverse = lax.rsqrt(var + norm_eps)
    return centered * inverse, inverse


def forward_kernel(plan, first, last, graphs, tiles, me_ref, *refs):
    packs = refs[: plan.fsdp]
    refs = list(refs[plan.fsdp :])
    src_ref, dst_ref = refs[0:2]
    refs = refs[2:]
    if first:
        x_now, x_next, border, link = refs[0:4]
        refs = refs[4:]
    else:
        h_in, e_in = refs[0:2]
        refs = refs[2:]
    h_out, hb_out, agg_out, zn_out, xn_out, in_out, z1_out, xh_out, iv_out = refs[0:9]
    refs = refs[9:]
    if not last:
        e_out = refs[0]
        refs = refs[1:]
    wa, wb, wbn, wan, cols, outer, a_t, b_t, pcat, u, agg, h = refs[0:12]
    link8 = refs[12] if first else None
    latent = plan.latent
    nodes = h_out.shape[-1]
    tile = z1_out.shape[-1]
    g = pl.program_id(0)
    t = pl.program_id(1)

    @pl.when((g == 0) & (t == 0))
    def _():
        assemble(plan, me_ref[0], packs, wa, wb, wbn, wan, cols, outer if first else None)
        a_t[...] = wa[2 * latent :, :].astype(F32).T.astype(BF)
        b_t[...] = wb[...].astype(F32).T.astype(BF)
        pcat[:, 2 * nodes :] = a_t[...]
        if first:
            link8[...] = jnp.zeros_like(link8)

    @pl.when(t == 0)
    def _():
        if first:
            chosen = jnp.where(border[...] == 1, x_next[...], x_now[...]).astype(BF)
            h[...] = nn(outer[:, 0 : x_now.shape[0]], chosen)
        else:
            h[...] = h_in[0]
        low = h[...].astype(BF)
        hb_out[0] = low
        pcat[:, 0:nodes] = tn(wa[0:latent, :], low).astype(BF)
        pcat[:, nodes : 2 * nodes] = tn(wa[latent : 2 * latent, :], low).astype(BF)
        agg[...] = jnp.zeros_like(agg)

    fill_tables(u, src_ref[pl.ds(g, 1), :], dst_ref[pl.ds(g, 1), :], nodes, tile)
    if first:
        link8[0:4, :] = link[0]
        e = nn(cols[:, 8:16].astype(BF), link8[...].astype(BF))
    else:
        e = e_in[0]
    u[2 * nodes :, :] = e.astype(BF)
    z1 = nn(pcat[...], u[...]) + cols[:, 0:1]
    active = (z1 * sigmoid(z1)).astype(BF)
    z1_out[0] = z1.astype(BF)
    z2 = nn(b_t[...], active) + cols[:, 1:2]
    normed, inverse = norm_forward(z2, latent)
    xh_out[0] = normed.astype(BF)
    iv_out[0] = inverse
    e = e + (normed * cols[:, 2:3] + cols[:, 3:4])
    if not last:
        e_out[0] = e
    agg[...] += nt(e.astype(BF), u[nodes : 2 * nodes, :])

    @pl.when(t == tiles - 1)
    def _():
        arriving = agg[...].astype(BF)
        agg_out[0] = arriving
        low = h[...].astype(BF)
        z1n = tn(wan[0:latent, :], low) + tn(wan[latent:, :], arriving) + cols[:, 4:5]
        zn_out[0] = z1n
        actn = (z1n * sigmoid(z1n)).astype(BF)
        z2n = tn(wbn[...], actn) + cols[:, 5:6]
        normn, invn = norm_forward(z2n, latent)
        xn_out[0] = normn
        in_out[0] = invn
        h_out[0] = h[...] + (normn * cols[:, 6:7] + cols[:, 7:8])


def norm_backward(grad, gain, normed, inverse, count):
    scaled = grad * gain
    mean = jnp.sum(scaled, axis=0, keepdims=True) * (1.0 / count)
    cross = jnp.sum(scaled * normed, axis=0, keepdims=True) * (1.0 / count)
    return (inverse * (scaled - mean - normed * cross)).astype(BF)


def lane_sum(value):
    total = value[:, 0:128]
    for k in range(1, value.shape[1] // 128):
        total = total + value[:, 128 * k : 128 * (k + 1)]
    return total


def backward_kernel(plan, first, last, graphs, tiles, me_ref, counts, *refs):
    packs = refs[: plan.fsdp]
    refs = list(refs[plan.fsdp :])

    def take(k):
        out = refs[:k]
        del refs[:k]
        return out

    src_ref, dst_ref, hb, aggl, zn, xn, iv_n, z1_ref, xh_ref, iv_ref = take(10)
    if first:
        (link,) = take(1)
    else:
        (e_in,) = take(1)
    if last:
        h_fin, level, stats = take(3)
    else:
        gh_in, ge_in = take(2)
    if first or last:
        x_now, x_next, border = take(3)
    (out,) = take(1)
    if not first:
        gh_out, ge_out = take(2)
    if last:
        (count_out,) = take(1)
    wa, wb, wbn, wan, cols, outer = take(6)
    u, act, low_e, gh, gagg, q, d_ae, d_as, d_b, d_bn, d_an, v_e, v_n, loss = take(14)
    if first or last:
        d_outer, d_ee, link8, aux = take(4)
    latent = plan.latent
    nodes = hb.shape[-1]
    tile = z1_ref.shape[-1]
    channels = x_now.shape[0] if (first or last) else 0
    g = pl.program_id(0)
    t = pl.program_id(1)

    @pl.when((g == 0) & (t == 0))
    def _():
        assemble(plan, me_ref[0], packs, wa, wb, wbn, wan, cols, outer if (first or last) else None)
        for ref in (d_ae, d_as, d_b, d_bn, d_an, v_e, v_n, loss):
            ref[...] = jnp.zeros_like(ref)
        act[latent:, :] = jnp.ones((16, tile), BF)
        low_e[latent:, :] = jnp.ones((16, tile), BF)
        if first or last:
            d_outer[...] = jnp.zeros_like(d_outer)
            d_ee[...] = jnp.zeros_like(d_ee)
            link8[...] = jnp.zeros_like(link8)
        if last:
            total = jnp.sum(stats[...], axis=0)
            count = total[0:1, 2:3]
            mean = total[:, 0:1] / (count * LEVELS)
            spread = jnp.zeros((8, 1), F32)
            for k in range(stats.shape[0]):
                own = stats[k]
                own_count = own[:, 2:3]
                own_mean = own[:, 0:1] / (jnp.maximum(own_count, 1.0) * LEVELS)
                shift = own_mean - mean
                spread = spread + own[:, 1:2] + own_count * LEVELS * shift * shift
            variance = spread / (count * LEVELS)
            scale = jnp.broadcast_to(lax.rsqrt(variance + stat_eps), (8, 128))
            aux[:, 0:128] = exact(group_matrix(channels, 8, True), scale)
            aux[:, 128:256] = jnp.broadcast_to(count * channels, (channels, 128))
            count_out[0, 0] = jnp.sum(count) * channels

    @pl.when(t == 0)
    def _():
        if last:
            final_low = h_fin[0].astype(BF)
            delta = x_next[...] - x_now[...]
            scale = aux[:, 0:1]
            norm_count = aux[:, 128:129]
            predicted = tn(outer[...], final_low)[0:channels]
            misfit = (predicted - delta) * scale
            weighting = (level[...].astype(F32) + 1.0) / LEVELS * live_row(border[...], counts[g])
            piece = weighting * misfit * misfit
            loss[...] += jnp.broadcast_to(jnp.sum(piece), loss.shape)
            grad_pred = (2.0 * weighting * misfit * scale / norm_count).astype(BF)
            d_outer[:, 0:channels] += nt(final_low, grad_pred)
            gh_now = nn(outer[:, 0:channels], grad_pred)
        else:
            gh_now = gh_in[0]
        z1n = zn[0]
        normn = xn[0]
        v_n[:, 0:128] += lane_sum(gh_now * normn)
        v_n[:, 128:256] += lane_sum(gh_now)
        low_two = norm_backward(gh_now, cols[:, 6:7], normn, iv_n[0], latent)
        gate = sigmoid(z1n)
        soft = z1n * gate
        d_bn[0:latent] += nt(soft.astype(BF), low_two)
        d_active = nn(wbn[...], low_two)
        low_one = (d_active * (soft - soft * gate + gate)).astype(BF)
        v_n[:, 256:384] += lane_sum(low_one.astype(F32))
        v_n[:, 384:512] += lane_sum(low_two.astype(F32))
        low_h = hb[0]
        d_an[0:latent, :] += nt(low_h, low_one)
        d_an[latent:, :] += nt(aggl[0], low_one)
        gagg[...] = nn(wan[latent:, :], low_one).astype(BF)
        gh[...] = gh_now + nn(wan[0:latent, :], low_one)
        q[...] = jnp.zeros_like(q)

    fill_tables(u, src_ref[pl.ds(g, 1), :], dst_ref[pl.ds(g, 1), :], nodes, tile)
    if first:
        link8[0:4, :] = link[0]
        link_low = link8[...].astype(BF)
        low_e[0:latent, :] = nn(cols[:, 8:16].astype(BF), link_low).astype(BF)
    else:
        low_e[0:latent, :] = e_in[0].astype(BF)
    ge = nn(gagg[...], u[nodes : 2 * nodes, :])
    if not last:
        ge = ge + ge_in[0]
    normed = xh_ref[0].astype(F32)
    z1 = z1_ref[0].astype(F32)
    v_e[:, 0:128] += lane_sum(ge * normed)
    v_e[:, 128:256] += lane_sum(ge)
    low_two = norm_backward(ge, cols[:, 2:3], normed, iv_ref[0], latent)
    gate = sigmoid(z1)
    soft = z1 * gate
    act[0:latent, :] = soft.astype(BF)
    d_b[...] += nt(act[...], low_two)
    d_active = nn(wb[...], low_two)
    low_one = (d_active * (soft - soft * gate + gate)).astype(BF)
    d_ae[...] += nt(low_e[...], low_one)
    ge = ge + nn(wa[2 * latent :, :], low_one)
    q[...] += nt(low_one, u[...])
    if first:
        d_ee[...] += nt(ge.astype(BF), link_low)
    else:
        ge_out[0] = ge

    @pl.when(t == tiles - 1)
    def _():
        low_h = hb[0]
        total = gh[...]
        for side in range(2):
            sums = q[:, side * nodes : (side + 1) * nodes]
            high = sums.astype(BF)
            rest = (sums - high.astype(F32)).astype(BF)
            d_as[side * latent : (side + 1) * latent, :] += nt(low_h, high) + nt(low_h, rest)
            side_weights = wa[side * latent : (side + 1) * latent, :]
            total = total + nn(side_weights, high) + nn(side_weights, rest)
        if first:
            chosen = jnp.where(border[...] == 1, x_next[...], x_now[...]).astype(BF)
            d_outer[:, 0:channels] += nt(total.astype(BF), chosen)
        else:
            gh_out[0] = total

    @pl.when((g == graphs - 1) & (t == tiles - 1))
    def _():
        width = plan.width

        def emit(name, owner, value):
            for piece, row, at, count in plan.pieces(name):
                out[piece, owner, row : row + count, :] = value[at : at + count, :].astype(BF)

        def row_of(cols128):
            return jnp.sum(cols128.T, axis=0, keepdims=True)

        rows = [
            d_ae[latent : latent + 1, :],
            d_b[latent : latent + 1, :],
            row_of(v_e[:, 0:128]),
            row_of(v_e[:, 128:256]),
            row_of(v_n[:, 256:384]),
            row_of(v_n[:, 384:512]),
            row_of(v_n[:, 0:128]),
            row_of(v_n[:, 128:256]),
        ]
        top = jnp.concatenate(rows, axis=0)
        if first:
            low = d_ee[...].T
        else:
            whole = loss[0:1, 0:1]
            high = whole.astype(BF).astype(F32)
            mid = (whole - high).astype(BF).astype(F32)
            rest = whole - high - mid
            lane = lax.broadcasted_iota(jnp.int32, (8, latent), 1) % width
            low = jnp.where(lane == 0, high, jnp.where(lane == 1, mid, jnp.where(lane == 2, rest, 0.0)))
        all_rows = jnp.concatenate([top, low], axis=0)
        out[...] = jnp.zeros_like(out)
        pad = jnp.zeros((16, latent - width), F32)
        for j in range(plan.fsdp):
            block = 3 * width * j
            pieces = []
            if block < 2 * latent:
                stop = min(2 * latent, block + 3 * width)
                pieces.append(d_as[block:stop, :])
            if block + 3 * width > 2 * latent:
                begin = max(block, 2 * latent)
                pieces.append(d_ae[begin - 2 * latent : block + 3 * width - 2 * latent, :])
            emit("edge_first", j, pieces[0] if len(pieces) == 1 else jnp.concatenate(pieces, axis=0))
            emit("edge_second", j, d_b[width * j : width * (j + 1), :])
            emit("node_second", j, d_bn[width * j : width * (j + 1), :])
            emit("node_first", j, d_an[2 * width * j : 2 * width * (j + 1), :])
            emit(
                "rows", j, jnp.concatenate([all_rows[:, width * j : width * (j + 1)], pad], axis=1)
            )
            if first or last:
                own = d_outer[width * j : width * (j + 1), :]
                emit("outer", j, jnp.concatenate([own[: plan.half], own[plan.half :]], axis=1))


def adam_math(weight, moment, square, gradient, rate):
    moment_new = beta_one * moment + (1.0 - beta_one) * gradient
    square_new = beta_two * square + (1.0 - beta_two) * gradient * gradient
    direction = (
        moment_new
        * (1.0 / (1.0 - beta_one**STEP))
        / (jnp.sqrt(square_new * (1.0 / (1.0 - beta_two**STEP))) + adam_eps)
    )
    return (moment_new, square_new, weight - rate * (direction + decay_rate * weight))


def adam_kernel(plan, grads, *refs):
    ins = [refs[7 * k : 7 * k + 7] for k in range(3)]
    outs = [refs[21 + 3 * k : 24 + 3 * k] for k in range(7)]
    loss = refs[42]
    r = pl.program_id(0)
    block = grads[0]
    width = plan.width

    def part(name):
        start, size = plan.at[name]
        return block[start : start + size, :]

    def apply(k, index, gradient, rate):
        new = adam_math(ins[0][k][index], ins[1][k][index], ins[2][k][index], gradient, rate)
        for ref, value in zip(outs[k], new):
            ref[index] = value

    apply(2, 0, part("edge_first"), rate_matrix)
    apply(3, (0, 0), part("edge_second"), rate_matrix)
    apply(3, (0, 1), part("node_second"), rate_matrix)
    apply(4, 0, part("node_first"), rate_matrix)
    rows = part("rows")
    apply(5, (0, 0), rows[0:4, 0:width], rate_vector)
    apply(5, (0, 1), rows[4:8, 0:width], rate_vector)
    half = plan.latent // 2
    wide = part("outer")
    outer = jnp.concatenate([wide[:, 0:half], wide[:, half:]], axis=0)

    @pl.when(r == 0)
    def _():
        apply(0, Ellipsis, outer[:, 0 : ins[0][0].shape[1]], rate_matrix)
        apply(1, Ellipsis, rows[8:12, 0:width], rate_matrix)

    @pl.when(r == ROUNDS - 1)
    def _():
        apply(6, Ellipsis, outer[:, 0 : ins[0][6].shape[1]], rate_matrix)
        loss[0, 0] = jnp.sum(rows[8:9, 0:3])


def body(plan, *args):
    x_now, x_next, node_counts, border_flag, source_vertex, target_vertex, link_features, level_ids = args[:8]
    weights = args[8:15]
    moments = args[15:22]
    squares = args[22:29]
    encoder, edge_encoder, edge_first, second_layers, node_first, vectors, decoder = weights
    graphs, edge_count = source_vertex.shape
    nodes = x_now.shape[0] // graphs
    channels = x_now.shape[1]
    latent = plan.latent
    tile = EDGE_TILE
    tiles = edge_count // tile
    x_now_t = x_now.T
    x_next_t = x_next.T
    border = border_flag.reshape(1, -1)
    link_t = jnp.transpose(link_features, (0, 2, 1))
    level = level_ids.reshape(-1, 1)
    me = lax.axis_index("fsdp").astype(jnp.int32).reshape(1)
    devices = plan.dp * plan.fsdp

    vm = pl.BlockSpec(memory_space=pltpu.VMEM)
    sm = pl.BlockSpec(memory_space=pltpu.SMEM)
    sds = jax.ShapeDtypeStruct
    pack_shape = sds((plan.total, latent), BF)

    pack0 = pl.pallas_call(
        functools.partial(pack_first_kernel, plan),
        out_shape=pack_shape,
        in_specs=[vm] * 6,
        out_specs=vm,
        compiler_params=params(),
        name="pack_first",
    )(edge_first, second_layers, node_first, vectors, edge_encoder, encoder.T)

    def swap(value, mask):
        pairs = [(j, j ^ mask) for j in range(plan.fsdp)]
        return lax.ppermute(value, "fsdp", pairs)

    def spread_chain(own):
        got = [own]
        for k in range(1, plan.fsdp):
            low = k & -k
            got.append(swap(got[k & (k - 1)], low))
        return got

    def spread_direct(own):
        return [own] + [swap(own, k) for k in range(1, plan.fsdp)]

    packs = [spread_chain(pack0)]
    pack1, pack2, stats = pl.pallas_call(
        functools.partial(pack_rest_kernel, plan, graphs),
        out_shape=(pack_shape, pack_shape, sds((devices, 8, 128), F32)),
        in_specs=[sm] + [vm] * 8,
        out_specs=(vm,) * 3,
        compiler_params=params(),
        name="pack_rest",
    )(node_counts, edge_first, second_layers, node_first, vectors, decoder, x_now_t, x_next_t, border)
    packs.append(spread_direct(pack1))
    packs.append(spread_direct(pack2))
    stats = lax.all_to_all(stats, ("dp", "fsdp"), 0, 0, tiled=True)

    def const(shape):
        return pl.BlockSpec(shape, lambda g, t, *_: (0,) * len(shape))

    pack_spec = const((plan.total, latent))
    ids_spec = pl.BlockSpec((graphs, tile), lambda g, t, *_: (0, t))
    x_spec = pl.BlockSpec((channels, nodes), lambda g, t, *_: (0, g))
    border_spec = pl.BlockSpec((1, nodes), lambda g, t, *_: (0, g))
    link_spec = pl.BlockSpec((1, 4, tile), lambda g, t, *_: (g, 0, t))
    node_spec = pl.BlockSpec((1, latent, nodes), lambda g, t, *_: (g, 0, 0))
    node_row = pl.BlockSpec((1, 1, nodes), lambda g, t, *_: (g, 0, 0))
    edge_spec = pl.BlockSpec((1, latent, tile), lambda g, t, *_: (g * tiles + t, 0, 0))
    edge_row = pl.BlockSpec((1, 1, tile), lambda g, t, *_: (g * tiles + t, 0, 0))

    node_f32 = sds((graphs, latent, nodes), F32)
    node_bf = sds((graphs, latent, nodes), BF)
    node_row_f32 = sds((graphs, 1, nodes), F32)
    edge_f32 = sds((graphs * tiles, latent, tile), F32)
    edge_bf = sds((graphs * tiles, latent, tile), BF)
    edge_row_f32 = sds((graphs * tiles, 1, tile), F32)

    weight_scratch = [
        pltpu.VMEM((3 * latent, latent), BF),
        pltpu.VMEM((latent, latent), BF),
        pltpu.VMEM((latent, latent), BF),
        pltpu.VMEM((2 * latent, latent), BF),
        pltpu.VMEM((latent, 16), F32),
        pltpu.VMEM((latent, latent // 2), BF),
    ]
    row_flops = 2 * latent * latent
    forward_cost = pl.CostEstimate(
        flops=graphs * edge_count * row_flops * 8, bytes_accessed=24_000_000, transcendentals=0
    )
    backward_cost = pl.CostEstimate(
        flops=graphs * edge_count * row_flops * 11, bytes_accessed=30_000_000, transcendentals=0
    )

    stored = []
    state = None
    edge_state = None
    for r in range(ROUNDS):
        first = r == 0
        last = r == ROUNDS - 1
        ins = [*packs[r], source_vertex, target_vertex]
        specs = [pack_spec] * plan.fsdp + [ids_spec, ids_spec]
        if first:
            ins += [x_now_t, x_next_t, border, link_t]
            specs += [x_spec, x_spec, border_spec, link_spec]
        else:
            ins += [state, edge_state]
            specs += [node_spec, edge_spec]
        outs = [node_f32, node_bf, node_bf, node_f32, node_f32, node_row_f32, edge_bf, edge_bf, edge_row_f32]
        out_specs = [node_spec] * 5 + [node_row, edge_spec, edge_spec, edge_row]
        if not last:
            outs.append(edge_f32)
            out_specs.append(edge_spec)
        scratch = weight_scratch + [
            pltpu.VMEM((latent, latent), BF),
            pltpu.VMEM((latent, latent), BF),
            pltpu.VMEM((latent, 2 * nodes + latent), BF),
            pltpu.VMEM((2 * nodes + latent, tile), BF),
            pltpu.VMEM((latent, nodes), F32),
            pltpu.VMEM((latent, nodes), F32),
        ]
        if first:
            scratch = scratch + [pltpu.VMEM((8, tile), F32)]
        result = pl.pallas_call(
            functools.partial(forward_kernel, plan, first, last, graphs, tiles),
            out_shape=outs,
            grid_spec=pltpu.PrefetchScalarGridSpec(
                num_scalar_prefetch=1,
                grid=(graphs, tiles),
                in_specs=specs,
                out_specs=out_specs,
                scratch_shapes=scratch,
            ),
            compiler_params=params(),
            cost_estimate=forward_cost,
            name=f"forward_round{r}",
        )(me, *ins)
        stored.append((*result[1:9], edge_state))
        state = result[0]
        if not last:
            edge_state = result[9]

    blocks = [None] * ROUNDS
    loss_count = None
    grad_state = None
    grad_edge = None
    for r in reversed(range(ROUNDS)):
        first = r == 0
        last = r == ROUNDS - 1
        hb, aggl, zn, xn, ivn, z1, xh, iv, e_in = stored[r]
        ins = [*packs[r], source_vertex, target_vertex, hb, aggl, zn, xn, ivn, z1, xh, iv]
        specs = [pack_spec] * plan.fsdp + [ids_spec, ids_spec] + [node_spec] * 4
        specs += [node_row, edge_spec, edge_spec, edge_row]
        if first:
            ins += [link_t]
            specs += [link_spec]
        else:
            ins += [e_in]
            specs += [edge_spec]
        if last:
            ins += [state, level, stats]
            specs += [node_spec, const((channels, 1)), const((devices, 8, 128))]
        else:
            ins += [grad_state, grad_edge]
            specs += [node_spec, edge_spec]
        if first or last:
            ins += [x_now_t, x_next_t, border]
            specs += [x_spec, x_spec, border_spec]
        out_block = (plan.dp, plan.fsdp, plan.piece, latent)
        outs = [sds(out_block, BF)]
        out_specs = [const(out_block)]
        if not first:
            outs += [node_f32, edge_f32]
            out_specs += [node_spec, edge_spec]
        if last:
            outs += [sds((1, 1), F32)]
            out_specs += [sm]
        scratch = weight_scratch + [
            pltpu.VMEM((2 * nodes, tile), BF),
            pltpu.VMEM((latent + 16, tile), BF),
            pltpu.VMEM((latent + 16, tile), BF),
            pltpu.VMEM((latent, nodes), F32),
            pltpu.VMEM((latent, nodes), BF),
            pltpu.VMEM((latent, 2 * nodes), F32),
            pltpu.VMEM((latent + 16, latent), F32),
            pltpu.VMEM((2 * latent, latent), F32),
            pltpu.VMEM((latent + 16, latent), F32),
            pltpu.VMEM((latent, latent), F32),
            pltpu.VMEM((2 * latent, latent), F32),
            pltpu.VMEM((latent, 256), F32),
            pltpu.VMEM((latent, 512), F32),
            pltpu.VMEM((8, 128), F32),
        ]
        if first or last:
            scratch = scratch + [
                pltpu.VMEM((latent, latent // 2), F32),
                pltpu.VMEM((latent, 8), F32),
                pltpu.VMEM((8, tile), F32),
                pltpu.VMEM((channels, 256), F32),
            ]
        result = pl.pallas_call(
            functools.partial(backward_kernel, plan, first, last, graphs, tiles),
            out_shape=outs,
            grid_spec=pltpu.PrefetchScalarGridSpec(
                num_scalar_prefetch=2,
                grid=(graphs, tiles),
                in_specs=specs,
                out_specs=out_specs,
                scratch_shapes=scratch,
            ),
            compiler_params=params(),
            cost_estimate=backward_cost,
            name=f"backward_round{r}",
        )(me, node_counts, *ins)
        if not first:
            grad_state, grad_edge = result[1:3]
        if last:
            loss_count = result[3].reshape(())
        send = result[0].reshape(devices, plan.piece, latent)
        got = lax.all_to_all(send, ("dp", "fsdp"), 0, 0, tiled=True)
        total = jnp.sum(got.astype(F32), axis=0)
        shared = jnp.broadcast_to(total[None], (plan.dp, plan.piece, latent))
        whole = lax.all_to_all(shared, "dp", 0, 0, tiled=True)
        blocks[r] = whole.reshape(1, plan.total, latent)

    grads = jnp.concatenate(blocks, axis=0)

    def turned(group):
        return (group[0].T, *group[1:])

    groups = (turned(weights), turned(moments), turned(squares))

    def by_round(shape):
        if len(shape) == 2:
            return pl.BlockSpec(shape, lambda r: (0, 0))
        rest = (0,) * (len(shape) - 1)
        return pl.BlockSpec((1, *shape[1:]), lambda r: (r, *rest))

    shapes = [w.shape for w in groups[0]]
    each = [by_round(s) for s in shapes]
    out_specs = []
    out_shapes = []
    for s in shapes:
        out_specs += [by_round(s)] * 3
        out_shapes += [sds(s, F32)] * 3
    out_specs.append(sm)
    out_shapes.append(sds((1, 1), F32))
    new = pl.pallas_call(
        functools.partial(adam_kernel, plan),
        out_shape=out_shapes,
        grid=(ROUNDS,),
        in_specs=[pl.BlockSpec((1, plan.total, latent), lambda r: (r, 0, 0))] + each * 3,
        out_specs=out_specs,
        compiler_params=params(),
        name="update",
    )(grads, *groups[0], *groups[1], *groups[2])
    encoder_new = [v.T for v in new[0:3]]
    return (new[21].reshape(()), loss_count, *encoder_new, *new[3:21])


def solution(mesh):
    rows = P(("dp", "fsdp"), None)
    row = P(("dp", "fsdp"))
    weight_specs = (
        P(None, "fsdp"),
        P(None, "fsdp"),
        P(None, "fsdp", None),
        P(None, None, "fsdp", None),
        P(None, "fsdp", None),
        P(None, None, None, "fsdp"),
        P("fsdp", None),
    )
    placed = (rows, rows, row, row, rows, rows, P(("dp", "fsdp"), None, None), P(), *weight_specs * 3)
    out_specs = [P(), P()]
    for spec in weight_specs:
        out_specs += [spec] * 3

    def step(*args):
        plan = Plan(args[10].shape[2], mesh.shape["dp"], mesh.shape["fsdp"])
        return body(plan, *args)

    return jax.shard_map(
        step, mesh=mesh, in_specs=placed, out_specs=tuple(out_specs), check_vma=False
    )
```

```python
import functools

import jax
import jax.numpy as jnp
from jax import lax
from jax.experimental import pallas as pl
from jax.experimental.pallas import tpu as pltpu
from jax.sharding import PartitionSpec as P

VARS = 6
LEVELS = 13
ROUNDS = 3
STEP = 10

norm_eps = 1e-05
stat_eps = 1e-06
beta_one = 0.9
beta_two = 0.999
adam_eps = 1e-08
decay_rate = 0.01
rate_matrix = 0.03
rate_vector = 0.2

BF = jnp.bfloat16
F32 = jnp.float32
VMEM_LIMIT = 56 * 1024 * 1024
EDGE_TILE = 1536
CHUNK = 256


def contract(a, b, da, db):
    return lax.dot_general(a, b, (((da,), (db,)), ((), ())), preferred_element_type=F32)


def nn(a, b):
    return contract(a, b, 1, 0)


def nt(a, b):
    return contract(a, b, 1, 1)


def tn(a, b):
    return contract(a, b, 0, 0)


def sigmoid(v):
    return 0.5 * jnp.tanh(0.5 * v) + 0.5


def round_up(v, m):
    return (v + m - 1) // m * m


class Plan:
    def __init__(self, latent, dp_size, fsdp_size):
        self.latent = latent
        self.dp = dp_size
        self.fsdp = fsdp_size
        self.width = latent // fsdp_size
        self.half = self.width // 2
        sizes = (
            ("edge_first", 3 * self.width),
            ("edge_second", self.width),
            ("node_second", self.width),
            ("node_first", 2 * self.width),
            ("rows", 16),
            ("outer", self.half),
        )
        offset = 0
        self.at = {}
        for name, size in sizes:
            self.at[name] = (offset, size)
            offset += size
        self.piece = round_up((offset + dp_size - 1) // dp_size, 16)
        self.used = offset
        self.total = self.piece * dp_size


class Block:
    def __init__(self, plan, edge, node_parts):
        width = plan.width
        sizes = []
        if edge:
            sizes += [("edge_first", 3 * width), ("edge_second", width), ("rows", 16), ("outer", plan.half)]
        for k in range(node_parts):
            sizes += [(f"node_first{k}", 2 * width), (f"node_second{k}", width), (f"node_rows{k}", 16)]
        offset = 0
        self.at = {}
        for name, size in sizes:
            self.at[name] = (offset, size)
            offset += size
        self.used = offset
        self.piece = round_up((offset + plan.dp - 1) // plan.dp, 8)
        self.total = self.piece * plan.dp


def params(**kw):
    return pltpu.CompilerParams(vmem_limit_bytes=VMEM_LIMIT, **kw)


def live_row(border, count):
    place = lax.broadcasted_iota(jnp.int32, border.shape, 1)
    return jnp.where((place < count) & (border != 1), 1.0, 0.0).astype(F32)


def group_matrix(rows, cols, flip):
    var = lax.broadcasted_iota(jnp.int32, (rows, cols), 1 if flip else 0)
    chan = lax.broadcasted_iota(jnp.int32, (rows, cols), 0 if flip else 1)
    inside = (chan >= var * LEVELS) & (chan < (var + 1) * LEVELS)
    return jnp.where(inside, 1.0, 0.0).astype(F32)


def exact(a, b):
    return lax.dot_general(
        a, b, (((1,), (0,)), ((), ())), precision=lax.Precision.HIGHEST, preferred_element_type=F32
    )


class Refs:
    pass


def kernel_call(kernel, name, ins, outs, scratch=(), grid=(), prefetch=(), cost=None, aliases=None):
    names = [n for n, _ in prefetch] + [n for n, _, _ in ins] + [n for n, _, _ in outs]
    names += [n for n, _ in scratch]
    whole = pl.BlockSpec(memory_space=pltpu.VMEM)

    def spec(given, value):
        if given is not None:
            return given
        if not grid:
            return whole
        rank = len(value.shape)
        return pl.BlockSpec(value.shape, lambda *_: (0,) * rank)

    def run(*refs):
        bag = Refs()
        for n, ref in zip(names, refs):
            setattr(bag, n, ref)
        kernel(bag)

    result = pl.pallas_call(
        run,
        out_shape=[v for _, v, _ in outs],
        grid_spec=pltpu.PrefetchScalarGridSpec(
            num_scalar_prefetch=len(prefetch),
            grid=grid,
            in_specs=[spec(s, v) for _, v, s in ins],
            out_specs=[spec(s, v) for _, v, s in outs],
            scratch_shapes=[v for _, v in scratch],
        ),
        compiler_params=params(),
        input_output_aliases=aliases or {},
        cost_estimate=cost,
        name=name,
    )(*[v for _, v in prefetch], *[v for _, v, _ in ins])
    bag = Refs()
    for (n, _, _), value in zip(outs, result):
        setattr(bag, n, value)
    return bag


def listed(bag, name, count):
    return [getattr(bag, f"{name}{k}") for k in range(count)]


def pack_round(plan, out, r, edge_first, second_layers, node_first, vectors, edge_encoder, outer):
    width = plan.width
    at = plan.at

    def put(name, value):
        start, size = at[name]
        out[start : start + size, :] = value.astype(BF)

    put("edge_first", edge_first[r])
    put("edge_second", second_layers[r, 0])
    put("node_second", second_layers[r, 1])
    put("node_first", node_first[r])
    rows = jnp.concatenate([vectors[r, 0], vectors[r, 1]], axis=0)
    if edge_encoder is None:
        low = jnp.zeros((8, width), F32)
    else:
        low = jnp.concatenate([edge_encoder[...], jnp.zeros((4, width), F32)], axis=0)
    rows = jnp.concatenate([rows, low], axis=0)
    rows = jnp.concatenate([rows, jnp.zeros((16, plan.latent - width), F32)], axis=1)
    put("rows", rows)
    start, size = at["outer"]
    if outer is None:
        out[start : start + size, :] = jnp.zeros((size, plan.latent), BF)
    else:
        channels = outer.shape[1]
        wide = jnp.concatenate(
            [outer[...], jnp.zeros((width, plan.latent // 2 - channels), F32)], axis=1
        )
        put("outer", jnp.concatenate([wide[: plan.half], wide[plan.half :]], axis=1))
    if plan.total > plan.used:
        out[plan.used : plan.total, :] = jnp.zeros((plan.total - plan.used, plan.latent), BF)


def pack_first_kernel(plan, b):
    pack_round(plan, b.pack, 0, b.ef, b.sl, b.nf, b.vec, b.ee, b.enc)


def merge_stats(parts):
    total = parts[0]
    for part in parts[1:]:
        total = total + part
    count = total[:, 2:3]
    mean = total[:, 0:1] / (jnp.maximum(count, 1.0) * LEVELS)
    spread = jnp.zeros((8, 1), F32)
    for own in parts:
        own_count = own[:, 2:3]
        own_mean = own[:, 0:1] / (jnp.maximum(own_count, 1.0) * LEVELS)
        shift = own_mean - mean
        spread = spread + own[:, 1:2] + own_count * LEVELS * shift * shift
    lane = lax.broadcasted_iota(jnp.int32, (8, 128), 1)
    return jnp.where(lane == 1, spread, total)


def pack_rest_kernel(plan, graphs, b):
    pack_round(plan, b.pack.at[0], 1, b.ef, b.sl, b.nf, b.vec, None, None)
    pack_round(plan, b.pack.at[1], 2, b.ef, b.sl, b.nf, b.vec, None, b.dec)
    nodes = b.x_now.shape[1] // graphs
    channels = b.x_now.shape[0]
    lives = []
    for g in range(graphs):
        lives.append(live_row(b.border[:, g * nodes : (g + 1) * nodes], b.counts[g]))
    live = jnp.concatenate(lives, axis=1)
    delta = b.x_next[...] - b.x_now[...]
    count = jnp.sum(live)
    sums = jnp.sum(delta * live, axis=1, keepdims=True)
    to_var = group_matrix(8, channels, False)
    to_chan = group_matrix(channels, 8, True)
    var_sum = exact(to_var, jnp.broadcast_to(sums, (channels, 128)))
    mean = var_sum / (jnp.maximum(count, 1.0) * LEVELS)
    centered = (delta - exact(to_chan, mean)[:, 0:1]) * live
    square = jnp.sum(centered * centered, axis=1, keepdims=True)
    var_square = exact(to_var, jnp.broadcast_to(square, (channels, 128)))
    lane = lax.broadcasted_iota(jnp.int32, (8, 128), 1)
    value = jnp.where(lane == 0, var_sum, jnp.where(lane == 1, var_square, count))
    b.stats[...] = jnp.broadcast_to(value[None], b.stats.shape)


def assemble(plan, me, packs, edge_first=None, edge_second=None, node_second=None, node_first=None, cols=None, outer=None):
    width = plan.width
    latent = plan.latent
    total = jnp.zeros((latent, 16), F32)
    rowid = lax.broadcasted_iota(jnp.int32, (latent, width), 0)
    colid = lax.broadcasted_iota(jnp.int32, (latent, width), 1)
    for k, pack in enumerate(packs):
        owner = jnp.bitwise_xor(me, k)

        def put(ref, name, step):
            if ref is not None:
                start, size = plan.at[name]
                ref[pl.ds(pl.multiple_of(owner * step, 16), size), :] = pack[start : start + size, :]

        put(edge_first, "edge_first", 3 * width)
        put(edge_second, "edge_second", width)
        put(node_second, "node_second", width)
        put(node_first, "node_first", 2 * width)
        start, size = plan.at["rows"]
        place = jnp.where(rowid == owner * width + colid, 1.0, 0.0).astype(BF)
        total = total + nt(place, pack[start : start + size, 0:width])
        if outer is not None:
            start, size = plan.at["outer"]
            half = latent // 2
            first = pl.multiple_of(owner * width, 16)
            second = pl.multiple_of(owner * width + plan.half, 16)
            outer[pl.ds(first, size), :] = pack[start : start + size, 0:half]
            outer[pl.ds(second, size), :] = pack[start : start + size, half : 2 * half]
    cols[...] = total


def assemble_all(plan, b, packs, outer):
    assemble(plan, b.ids[0], packs, b.wa, b.wb, b.wbn, b.wan, b.cols, b.outer if outer else None)


def turn_weights(plan, b, nodes):
    latent = plan.latent
    b.b_t[...] = b.wb[...].astype(F32).T.astype(BF)
    b.pcat[:, 2 * nodes :] = b.wa[2 * latent :, :].astype(F32).T.astype(BF)


def fill_tables(u_ref, src, dst, nodes, lanes):
    count = lanes.stop - lanes.start
    place = lax.broadcasted_iota(jnp.int32, (nodes, count), 0).astype(jnp.int16)
    one = jnp.ones((nodes, count), BF)
    zero = jnp.zeros((nodes, count), BF)
    u_ref[0:nodes, lanes] = jnp.where(place == src[:, lanes].astype(jnp.int16), one, zero)
    u_ref[nodes : 2 * nodes, lanes] = jnp.where(place == dst[:, lanes].astype(jnp.int16), one, zero)


def skew(chunks):
    live = []
    waiting = list(chunks)
    while live or waiting:
        if waiting:
            live.append(waiting.pop(0))
        for item in list(reversed(live)):
            if next(item, 1) == 1:
                live.remove(item)


def norm_forward(z2, count):
    mean = jnp.sum(z2, axis=0, keepdims=True) * (1.0 / count)
    centered = z2 - mean
    var = jnp.sum(centered * centered, axis=0, keepdims=True) * (1.0 / count)
    inverse = lax.rsqrt(var + norm_eps)
    return centered * inverse, inverse


def forward_nodes_in(plan, b, state):
    latent = plan.latent
    nodes = state.shape[-1]
    low = state.astype(BF)
    b.pcat[:, 0:nodes] = tn(b.wa[0:latent, :], low).astype(BF)
    b.pcat[:, nodes : 2 * nodes] = tn(b.wa[latent : 2 * latent, :], low).astype(BF)
    b.agg[...] = jnp.zeros_like(b.agg)
    return low


def forward_edges(plan, b, src, dst, tile, get, put, keep):
    nodes = b.agg.shape[-1]

    def chunk(at):
        lanes = slice(at, at + CHUNK)
        fill_tables(b.u, src, dst, nodes, lanes)
        low = get(lanes).astype(BF)
        b.u[2 * nodes :, lanes] = low
        yield
        z1 = nn(b.pcat[...], b.u[:, lanes])
        yield
        z1 = z1 + b.cols[:, 0:1]
        active = (z1 * sigmoid(z1)).astype(BF)
        keep("z1", lanes, z1.astype(BF))
        yield
        z2 = nn(b.b_t[...], active)
        yield
        z2 = z2 + b.cols[:, 1:2]
        normed, inverse = norm_forward(z2, plan.latent)
        keep("xh", lanes, normed.astype(BF))
        keep("iv", lanes, inverse)
        e = get(lanes) + (normed * b.cols[:, 2:3] + b.cols[:, 3:4])
        if put is not None:
            put(lanes, e)
        b.new_low[:, lanes] = e.astype(BF)
        yield

    skew([chunk(at) for at in range(0, tile, CHUNK)])
    b.agg[...] += nt(b.new_low[...], b.u[nodes : 2 * nodes, :])


def forward_nodes_out(plan, b, state, low):
    latent = plan.latent
    arriving = b.agg[...].astype(BF)
    z1 = tn(b.wan[0:latent, :], low) + tn(b.wan[latent:, :], arriving) + b.cols[:, 4:5]
    active = (z1 * sigmoid(z1)).astype(BF)
    z2 = tn(b.wbn[...], active) + b.cols[:, 5:6]
    normed, inverse = norm_forward(z2, latent)
    return arriving, z1, normed, inverse, state + (normed * b.cols[:, 6:7] + b.cols[:, 7:8])


def norm_backward(grad, gain, normed, inverse, count):
    scaled = grad * gain
    mean = jnp.sum(scaled, axis=0, keepdims=True) * (1.0 / count)
    cross = jnp.sum(scaled * normed, axis=0, keepdims=True) * (1.0 / count)
    return (inverse * (scaled - mean - normed * cross)).astype(BF)


def lane_sum(value):
    total = value[:, 0:128]
    for k in range(1, value.shape[1] // 128):
        total = total + value[:, 128 * k : 128 * (k + 1)]
    return total


def backward_reset(plan, b, tile, names):
    for name in names:
        ref = getattr(b, name)
        ref[...] = jnp.zeros_like(ref)
    b.act[plan.latent :, :] = jnp.ones((16, tile), BF)


def backward_nodes_in(plan, weights, sums, grad, low_h, arriving, z1, normed, inverse):
    latent = plan.latent
    wan, wbn, cols = weights
    d_an, d_bn, v_n = sums
    v_n[:, 0:128] += lane_sum(grad * normed)
    v_n[:, 128:256] += lane_sum(grad)
    low_two = norm_backward(grad, cols[:, 6:7], normed, inverse, latent)
    gate = sigmoid(z1)
    soft = z1 * gate
    d_bn[...] += nt(soft.astype(BF), low_two)
    d_active = nn(wbn[...], low_two)
    low_one = (d_active * (soft - soft * gate + gate)).astype(BF)
    v_n[:, 256:384] += lane_sum(low_one.astype(F32))
    v_n[:, 384:512] += lane_sum(low_two.astype(F32))
    d_an[0:latent, :] += nt(low_h, low_one)
    d_an[latent:, :] += nt(arriving, low_one)
    return grad + nn(wan[0:latent, :], low_one), nn(wan[latent:, :], low_one).astype(BF)


def backward_edges(plan, b, src, dst, tile, get, fetch, low_e, put):
    latent = plan.latent
    nodes = b.gagg.shape[-1]

    def chunk(at):
        lanes = slice(at, at + CHUNK)
        fill_tables(b.u, src, dst, nodes, lanes)
        yield
        ge = nn(b.gagg[...], b.u[nodes : 2 * nodes, lanes])
        yield
        if get is not None:
            ge = ge + get(lanes)
        normed = fetch("xh", lanes).astype(F32)
        b.v_e[:, 0:128] += lane_sum(ge * normed)
        b.v_e[:, 128:256] += lane_sum(ge)
        low_two = norm_backward(ge, b.cols[:, 2:3], normed, fetch("iv", lanes), latent)
        b.two[:, lanes] = low_two
        yield
        d_active = nn(b.wb[...], low_two)
        yield
        z1 = fetch("z1", lanes).astype(F32)
        gate = sigmoid(z1)
        soft = z1 * gate
        b.act[0:latent, lanes] = soft.astype(BF)
        low_one = (d_active * (soft - soft * gate + gate)).astype(BF)
        b.one[:, lanes] = low_one
        yield
        put(lanes, ge + nn(b.wa[2 * latent :, :], low_one))
        yield

    skew([chunk(at) for at in range(0, tile, CHUNK)])
    b.d_b[...] += nt(b.act[...], b.two[...])
    b.d_first[2 * latent :, :] += nt(low_e[...], b.one[...])
    b.q[...] += nt(b.one[...], b.u[0 : 2 * nodes, :])


def backward_nodes_out(plan, b, low_h):
    latent = plan.latent
    nodes = b.gagg.shape[-1]
    total = b.gh[...]
    for side in range(2):
        sums = b.q[:, side * nodes : (side + 1) * nodes]
        high = sums.astype(BF)
        rest = (sums - high.astype(F32)).astype(BF)
        rows = slice(side * latent, (side + 1) * latent)
        b.d_first[rows, :] += nt(low_h, high) + nt(low_h, rest)
        total = total + nn(b.wa[rows, :], high) + nn(b.wa[rows, :], rest)
    return total


def row_of(cols128):
    return jnp.sum(cols128.T, axis=0, keepdims=True)


def backward_emit(plan, block, b, low, outer, node_sums, before):
    latent = plan.latent
    width = plan.width
    rows = [
        b.d_first[3 * latent : 3 * latent + 1, :],
        b.d_b[latent : latent + 1, :],
        row_of(b.v_e[:, 0:128]),
        row_of(b.v_e[:, 128:256]),
        jnp.zeros((4, latent), F32),
        jnp.zeros((8, latent), F32) if low is None else low,
    ]
    groups = [("rows", jnp.concatenate(rows, axis=0).astype(BF))]
    for k, (_, _, v_n) in enumerate(node_sums):
        rows = [
            row_of(v_n[:, 256:384]),
            row_of(v_n[:, 384:512]),
            row_of(v_n[:, 0:128]),
            row_of(v_n[:, 128:256]),
            jnp.zeros((12, latent), F32),
        ]
        groups.append((f"node_rows{k}", jnp.concatenate(rows, axis=0).astype(BF)))
    rowid = lax.broadcasted_iota(jnp.int32, (latent, latent), 0)
    colid = lax.broadcasted_iota(jnp.int32, (latent, latent), 1)
    for k, out in enumerate(listed(b, "grad", plan.fsdp)):
        owner = jnp.bitwise_xor(b.ids[0], k)

        def put(name, value):
            start, size = block.at[name]
            rows = slice(start, start + size)
            if before is not None:
                value = value + before[k][rows, :].astype(F32)
            out[rows, :] = value.astype(BF)

        def take(ref, step):
            return ref[pl.ds(pl.multiple_of(owner * step, 8), step), :]

        put("edge_first", take(b.d_first, 3 * width))
        put("edge_second", take(b.d_b, width))
        inside = (rowid == owner * width + colid) & (colid < width)
        place = jnp.where(inside, 1.0, 0.0).astype(BF)
        for name, value in groups:
            put(name, nn(value, place))
        if outer is not None:
            own = take(outer, width)
            put("outer", jnp.concatenate([own[: plan.half], own[plan.half :]], axis=1))
        else:
            put("outer", jnp.zeros((plan.half, latent), F32))
        for k2, (d_an, d_bn, _) in enumerate(node_sums):
            put(f"node_first{k2}", take(d_an, 2 * width))
            put(f"node_second{k2}", take(d_bn, width))
        if block.total > block.used:
            out[block.used :, :] = jnp.zeros((block.total - block.used, latent), BF)


def split_three(whole, lanes, period, place):
    high = whole.astype(BF).astype(F32)
    mid = (whole - high).astype(BF).astype(F32)
    rest = whole - high - mid
    lane = lax.broadcasted_iota(jnp.int32, (8, lanes), 1) % period - 3 * place
    top = lax.broadcasted_iota(jnp.int32, (8, lanes), 0) == 0
    value = jnp.where(lane == 0, high, jnp.where(lane == 1, mid, jnp.where(lane == 2, rest, 0.0)))
    return jnp.where(top, value, 0.0)


def first_kernel(plan, tiles, b):
    g = pl.program_id(0)
    t = pl.program_id(1)
    nodes = b.h_out.shape[-1]
    tile = b.z1.shape[-1]

    @pl.when((g == 0) & (t == 0))
    def _():
        assemble_all(plan, b, listed(b, "pack", plan.fsdp), True)
        turn_weights(plan, b, nodes)
        b.link8[...] = jnp.zeros_like(b.link8)

    @pl.when(t == 0)
    def _():
        chosen = jnp.where(b.border[...] == 1, b.x_next[...], b.x_now[...]).astype(BF)
        b.h[...] = nn(b.outer[:, 0 : b.x_now.shape[0]], chosen)
        b.hb[0] = forward_nodes_in(plan, b, b.h[...])

    b.link8[0:4, :] = b.link[0]

    def get(lanes):
        return nn(b.cols[:, 8:16].astype(BF), b.link8[:, lanes].astype(BF))

    def put(lanes, value):
        b.e_out[0, :, lanes] = value

    def keep(name, lanes, value):
        getattr(b, name)[0, :, lanes] = value

    forward_edges(plan, b, b.src[pl.ds(g, 1), :], b.dst[pl.ds(g, 1), :], tile, get, put, keep)

    @pl.when(t == tiles - 1)
    def _():
        state = b.h[...]
        b.aggl[0], b.zn[0], b.xn[0], b.ivn[0], b.h_out[0] = forward_nodes_out(plan, b, state, state.astype(BF))


def middle_kernel(plan, block, graphs, tiles, b):
    p = pl.program_id(0)
    g = pl.program_id(1)
    t = pl.program_id(2)
    nodes = b.gh_out.shape[-1]
    tile = b.z1.shape[-1]
    latent = plan.latent
    channels = b.x_now.shape[0]
    at = g * tiles + t
    start = (g == 0) & (t == 0)
    src = b.src[pl.ds(g, 1), :]
    dst = b.dst[pl.ds(g, 1), :]

    @pl.when((p == 0) & start)
    def _():
        assemble_all(plan, b, [r.at[0] for r in listed(b, "pack", plan.fsdp)], False)
        turn_weights(plan, b, nodes)
        b.wan1[...] = b.wan[...]
        b.wbn1[...] = b.wbn[...]
        b.cols1[...] = b.cols[...]
        names = ("d_first", "d_b", "v_e", "d_bn", "d_an", "v_n", "d_bn1", "d_an1", "v_n1", "d_outer", "loss")
        backward_reset(plan, b, tile, names)
        merged = merge_stats([b.stats[k] for k in range(b.stats.shape[0])])
        count = merged[:, 2:3]
        scale = lax.rsqrt(merged[:, 1:2] / (count * LEVELS) + stat_eps)
        b.aux[:, 0:128] = exact(group_matrix(channels, 8, True), jnp.broadcast_to(scale, (8, 128)))
        b.aux[:, 128:256] = jnp.broadcast_to(count[0:1] * channels, (channels, 128))
        b.count_out[0, 0] = jnp.sum(count[0:1]) * channels

    @pl.when((p == 1) & start)
    def _():
        assemble_all(plan, b, [r.at[1] for r in listed(b, "pack", plan.fsdp)], True)
        turn_weights(plan, b, nodes)

    @pl.when((p == 0) & (t == 0))
    def _():
        b.hb[0] = forward_nodes_in(plan, b, b.h_in[0])

    @pl.when(p == 0)
    def _():
        def get(lanes):
            return b.e_in[0, :, lanes]

        def put(lanes, value):
            b.e_all[at, :, lanes] = value

        def keep(name, lanes, value):
            getattr(b, name)[0, :, lanes] = value

        forward_edges(plan, b, src, dst, tile, get, put, keep)

    @pl.when((p == 0) & (t == tiles - 1))
    def _():
        state = b.h_in[0]
        b.hb1[g] = state.astype(BF)
        b.aggl1[g], b.zn1[g], b.xn1[g], b.ivn1[g], b.h_all[g] = forward_nodes_out(plan, b, state, b.hb1[g])

    @pl.when((p == 1) & (t == 0))
    def _():
        b.hb2[g] = forward_nodes_in(plan, b, b.h_all[g])

    @pl.when(p == 1)
    def _():
        b.low2[at, latent:, :] = jnp.ones((16, tile), BF)

        def get(lanes):
            return b.e_all[at, :, lanes]

        def keep(name, lanes, value):
            getattr(b, name + "2")[at, :, lanes] = value

        forward_edges(plan, b, src, dst, tile, get, None, keep)
        b.low2[at, 0:latent, :] = b.u[2 * nodes :, :]

    @pl.when((p == 1) & (t == tiles - 1))
    def _():
        b.aggl2[g], b.zn2[g], b.xn2[g], b.ivn2[g], b.h_all[g] = forward_nodes_out(
            plan, b, b.h_all[g], b.hb2[g]
        )

    @pl.when((p == 2) & (t == 0))
    def _():
        final_low = b.h_all[g].astype(BF)
        delta = b.x_next[...] - b.x_now[...]
        scale = b.aux[:, 0:1]
        norm_count = b.aux[:, 128:129]
        predicted = tn(b.outer[...], final_low)[0:channels]
        misfit = (predicted - delta) * scale
        weighting = (b.level[...].astype(F32) + 1.0) / LEVELS * live_row(b.border[...], b.counts[g])
        b.loss[...] += jnp.broadcast_to(jnp.sum(weighting * misfit * misfit), b.loss.shape)
        grad_pred = (2.0 * weighting * misfit * scale / norm_count).astype(BF)
        b.d_outer[:, 0:channels] += nt(final_low, grad_pred)
        grad = nn(b.outer[:, 0:channels], grad_pred)
        b.gh[...], b.gagg[...] = backward_nodes_in(
            plan,
            (b.wan, b.wbn, b.cols),
            (b.d_an, b.d_bn, b.v_n),
            grad,
            b.hb2[g],
            b.aggl2[g],
            b.zn2[g],
            b.xn2[g],
            b.ivn2[g],
        )
        b.q[...] = jnp.zeros_like(b.q)

    @pl.when(p == 2)
    def _():
        def fetch(name, lanes):
            return getattr(b, name + "2")[at, :, lanes]

        def put(lanes, value):
            b.ge_out[0, :, lanes] = value

        backward_edges(plan, b, src, dst, tile, None, fetch, b.low2.at[at], put)

    @pl.when((p == 2) & (t == tiles - 1))
    def _():
        grad = backward_nodes_out(plan, b, b.hb2[g])
        b.gh_out[0], b.gagg_out[0] = backward_nodes_in(
            plan,
            (b.wan1, b.wbn1, b.cols1),
            (b.d_an1, b.d_bn1, b.v_n1),
            grad,
            b.hb1[g],
            b.aggl1[g],
            b.zn1[g],
            b.xn1[g],
            b.ivn1[g],
        )

    @pl.when((p == 2) & (g == graphs - 1) & (t == tiles - 1))
    def _():
        low = split_three(b.loss[0:1, 0:1], latent, plan.width, b.ids[0])
        sums = ((b.d_an, b.d_bn, b.v_n), (b.d_an1, b.d_bn1, b.v_n1))
        backward_emit(plan, block, b, low, b.d_outer, sums, None)


def back_kernel(plan, block, first, g, tiles, b):
    tile = b.u.shape[-1]
    latent = plan.latent
    names = ["z1", "xh", "iv", "ge"] + ([] if first else ["e"])

    def fetch_copy(name, t):
        source = getattr(b, name + "_in")
        place = t if source.shape[0] == tiles else g * tiles + t
        return pltpu.make_async_copy(
            source.at[place], getattr(b, name).at[t], b.sems.at[names.index(name), t]
        )

    for t in range(tiles):
        for name in names:
            fetch_copy(name, t).start()
    packs = listed(b, "pack", plan.fsdp)
    if first:
        assemble(plan, b.ids[0], packs, b.wa, b.wb, cols=b.cols)
    else:
        assemble(plan, b.ids[0], [r.at[0] for r in packs], b.wa, b.wb, cols=b.cols)
        assemble(
            plan, b.ids[0], listed(b, "before", plan.fsdp), node_second=b.wbn, node_first=b.wan, cols=b.cols1
        )
    sums = ["d_first", "d_b", "v_e", "q"]
    sums += ["d_outer", "d_ee", "link8"] if first else ["d_bn", "d_an", "v_n"]
    backward_reset(plan, b, tile, sums)
    b.low_e[latent:, :] = jnp.ones((16, tile), BF)
    b.gagg[...] = b.gagg_in[0]
    b.gh[...] = b.gh_in[0]

    @pl.loop(0, tiles)
    def _(t):
        for name in names:
            fetch_copy(name, t).wait()
        lanes = pl.ds(pl.multiple_of(t * tile, 128), tile)

        def get(lanes):
            return b.ge[t, :, lanes]

        def fetch(name, lanes):
            return getattr(b, name)[t, :, lanes]

        if first:
            b.link8[0:4, :] = b.link[0, :, lanes]
            b.low_e[0:latent, :] = nn(b.cols[:, 8:16].astype(BF), b.link8[...].astype(BF)).astype(BF)

            def put(lanes, value):
                b.ge_low[:, lanes] = value.astype(BF)
        else:
            b.low_e[0:latent, :] = b.e[t].astype(BF)

            def put(lanes, value):
                b.ge[t, :, lanes] = value

        backward_edges(
            plan, b, b.src[g : g + 1, lanes], b.dst[g : g + 1, lanes], tile, get, fetch, b.low_e, put
        )
        if first:
            b.d_ee[...] += nt(b.ge_low[...], b.link8[...].astype(BF))
        else:
            pltpu.make_async_copy(b.ge.at[t], b.ge_out.at[t], b.sems.at[len(names), t]).start()

    total = backward_nodes_out(plan, b, b.hb[0])
    before = listed(b, "other", plan.fsdp) if g > 0 else None
    if first:
        chosen = jnp.where(b.border[...] == 1, b.x_next[...], b.x_now[...]).astype(BF)
        b.d_outer[:, 0 : b.x_now.shape[0]] += nt(total.astype(BF), chosen)
        backward_emit(plan, block, b, b.d_ee[...].T, b.d_outer, (), before)
    else:
        b.gh_out[0], b.gagg_out[0] = backward_nodes_in(
            plan,
            (b.wan, b.wbn, b.cols1),
            (b.d_an, b.d_bn, b.v_n),
            total,
            b.hb0[0],
            b.aggl[0],
            b.zn[0],
            b.xn[0],
            b.ivn[0],
        )
        backward_emit(plan, block, b, None, None, ((b.d_an, b.d_bn, b.v_n),), before)
        for t in range(tiles):
            pltpu.make_async_copy(b.ge.at[t], b.ge_out.at[t], b.sems.at[len(names), t]).wait()


def adam_math(weight, moment, square, gradient, rate):
    moment_new = beta_one * moment + (1.0 - beta_one) * gradient
    square_new = beta_two * square + (1.0 - beta_two) * gradient * gradient
    direction = (
        moment_new
        * (1.0 / (1.0 - beta_one**STEP))
        / (jnp.sqrt(square_new * (1.0 / (1.0 - beta_two**STEP))) + adam_eps)
    )
    return (moment_new, square_new, weight - rate * (direction + decay_rate * weight))


def apply_update(b, k, index, gradient, rate):
    old = [getattr(b, f"{kind}{k}")[index] for kind in ("weight", "moment", "square")]
    new = adam_math(*old, gradient, rate)
    for kind, value in zip(("moment_new", "square_new", "weight_new"), new):
        getattr(b, f"{kind}{k}")[index] = value


def part_of(ref, block, name):
    start, size = block.at[name]
    return ref[start : start + size, :]


def update_edge(plan, b, ref, block, r, at):
    apply_update(b, 2, at, part_of(ref, block, "edge_first"), rate_matrix)
    apply_update(b, 3, (at, 0), part_of(ref, block, "edge_second"), rate_matrix)
    rows = part_of(ref, block, "rows")
    apply_update(b, 5, (at, 0), rows[0:4, 0 : plan.width], rate_vector)
    half = plan.latent // 2
    wide = part_of(ref, block, "outer")
    return rows, jnp.concatenate([wide[:, 0:half], wide[:, half:]], axis=0)


def update_early_kernel(plan, blocks, b):
    width = plan.width
    rows, outer = update_edge(plan, b, b.grads2, blocks[2], 2, 2)
    apply_update(b, 6, Ellipsis, outer[:, 0 : b.weight6.shape[1]], rate_matrix)
    lane = lax.broadcasted_iota(jnp.int32, (1, plan.latent), 1)
    b.loss[0, 0] = jnp.sum(jnp.where(lane < width, rows[8:9, :], 0.0))
    update_edge(plan, b, b.grads1, blocks[1], 1, 1)
    for r, ref, block, k in ((2, b.grads2, blocks[2], 0), (1, b.grads2, blocks[2], 1), (0, b.grads1, blocks[1], 0)):
        apply_update(b, 4, r, part_of(ref, block, f"node_first{k}"), rate_matrix)
        apply_update(b, 3, (r, 1), part_of(ref, block, f"node_second{k}"), rate_matrix)
        node_rows = part_of(ref, block, f"node_rows{k}")
        apply_update(b, 5, (r, 1), node_rows[0:4, 0:width], rate_vector)


def update_late_kernel(plan, blocks, b):
    rows, outer = update_edge(plan, b, b.grads0, blocks[0], 0, 0)
    apply_update(b, 0, Ellipsis, outer[:, 0 : b.weight0.shape[1]], rate_matrix)
    apply_update(b, 1, Ellipsis, rows[8:12, 0 : plan.width], rate_matrix)


def body(plan, *args):
    x_now, x_next, node_counts, border_flag, source_vertex, target_vertex, link_features, level_ids = args[:8]
    weights = args[8:15]
    moments = args[15:22]
    squares = args[22:29]
    encoder, edge_encoder, edge_first, second_layers, node_first, vectors, decoder = weights
    graphs, edge_count = source_vertex.shape
    nodes = x_now.shape[0] // graphs
    channels = x_now.shape[1]
    latent = plan.latent
    tile = EDGE_TILE
    tiles = edge_count // tile
    x_now_t = x_now.T
    x_next_t = x_next.T
    border = border_flag.reshape(1, -1)
    link_t = jnp.transpose(link_features, (0, 2, 1))
    level = level_ids.reshape(-1, 1)
    ids = jnp.stack([lax.axis_index("fsdp"), lax.axis_index("dp")]).astype(jnp.int32)

    sm = pl.BlockSpec(memory_space=pltpu.SMEM)
    sds = jax.ShapeDtypeStruct
    pack_shape = sds((plan.total, latent), BF)
    devices = plan.dp * plan.fsdp

    def across(value, axis, size, mask):
        return lax.ppermute(value, axis, [(j, j ^ mask) for j in range(size)])

    def spread_chain(own, beside):
        got = [own]
        for k in range(1, plan.fsdp):
            source = got[k & (k - 1)]
            if k & (k - 1):
                source, _ = lax.optimization_barrier((source, beside))
            got.append(across(source, "fsdp", plan.fsdp, k & -k))
        return got

    def spread_direct(own, axis, size):
        return [own] + [across(own, axis, size, k) for k in range(1, size)]

    def exchange(parts, axis, size):
        return [parts[0]] + [across(parts[k], axis, size, k) for k in range(1, size)]

    def several(name, values, spec=None):
        return [(f"{name}{k}", v, spec) for k, v in enumerate(values)]

    raw = [("ef", edge_first, None), ("sl", second_layers, None), ("nf", node_first, None), ("vec", vectors, None)]
    start = kernel_call(
        functools.partial(pack_first_kernel, plan),
        "pack_first",
        [*raw, ("ee", edge_encoder, None), ("enc", encoder.T, None)],
        [("pack", pack_shape, None)],
        cost=pl.CostEstimate(flops=1000, bytes_accessed=3_000_000, transcendentals=0),
    )
    rest = kernel_call(
        functools.partial(pack_rest_kernel, plan, graphs),
        "pack_rest",
        [("counts", node_counts, sm), *raw, ("dec", decoder, None)]
        + [("x_now", x_now_t, None), ("x_next", x_next_t, None), ("border", border, None)],
        [("pack", sds((2, plan.total, latent), BF), None), ("stats", sds((devices, 8, 128), F32), None)],
        cost=pl.CostEstimate(flops=1000, bytes_accessed=8_000_000, transcendentals=0),
    )
    pack_first = spread_chain(start.pack, rest.pack)
    pack_rest = spread_direct(rest.pack, "fsdp", plan.fsdp)
    stats = lax.all_to_all(rest.stats, ("dp", "fsdp"), 0, 0, tiled=True)

    ids_spec = pl.BlockSpec((graphs, tile), lambda g, t, *_: (0, t))
    x_spec = pl.BlockSpec((channels, nodes), lambda g, t, *_: (0, g))
    border_spec = pl.BlockSpec((1, nodes), lambda g, t, *_: (0, g))
    link_spec = pl.BlockSpec((1, 4, tile), lambda g, t, *_: (g, 0, t))
    node_spec = pl.BlockSpec((1, latent, nodes), lambda g, t, *_: (g, 0, 0))
    node_row = pl.BlockSpec((1, 1, nodes), lambda g, t, *_: (g, 0, 0))
    edge_spec = pl.BlockSpec((1, latent, tile), lambda g, t, *_: (g * tiles + t, 0, 0))
    edge_row = pl.BlockSpec((1, 1, tile), lambda g, t, *_: (g * tiles + t, 0, 0))

    node_f32 = sds((graphs, latent, nodes), F32)
    node_bf = sds((graphs, latent, nodes), BF)
    node_row_f32 = sds((graphs, 1, nodes), F32)
    edge_f32 = sds((graphs * tiles, latent, tile), F32)
    edge_bf = sds((graphs * tiles, latent, tile), BF)
    edge_row_f32 = sds((graphs * tiles, 1, tile), F32)

    def vmem(shape, kind=F32):
        return pltpu.VMEM(shape, kind)

    weight_scratch = [
        ("wa", vmem((3 * latent, latent), BF)),
        ("wb", vmem((latent, latent), BF)),
        ("wbn", vmem((latent, latent), BF)),
        ("wan", vmem((2 * latent, latent), BF)),
        ("cols", vmem((latent, 16))),
        ("outer", vmem((latent, latent // 2), BF)),
        ("u", vmem((2 * nodes + latent, tile), BF)),
    ]
    forward_scratch = [
        ("b_t", vmem((latent, latent), BF)),
        ("pcat", vmem((latent, 2 * nodes + latent), BF)),
        ("new_low", vmem((latent, tile), BF)),
        ("agg", vmem((latent, nodes))),
    ]
    backward_scratch = [
        ("act", vmem((latent + 16, tile), BF)),
        ("one", vmem((latent, tile), BF)),
        ("two", vmem((latent, tile), BF)),
        ("gh", vmem((latent, nodes))),
        ("gagg", vmem((latent, nodes), BF)),
        ("q", vmem((latent, 2 * nodes))),
        ("d_first", vmem((3 * latent + 16, latent))),
        ("d_b", vmem((latent + 16, latent))),
        ("d_bn", vmem((latent, latent))),
        ("d_an", vmem((2 * latent, latent))),
        ("v_e", vmem((latent, 256))),
        ("v_n", vmem((latent, 512))),
        ("d_outer", vmem((latent, latent // 2))),
        ("d_ee", vmem((latent, 8))),
        ("loss", vmem((8, 128))),
    ]
    link_scratch = [("link8", vmem((8, tile)))]
    row_flops = 2 * latent * latent * graphs * edge_count

    def cost(passes, size):
        return pl.CostEstimate(flops=row_flops * passes, bytes_accessed=size, transcendentals=0)

    names = ("hb", "aggl", "zn", "xn", "ivn", "z1", "xh", "iv")
    kinds = (node_bf, node_bf, node_f32, node_f32, node_row_f32, edge_bf, edge_bf, edge_row_f32)
    specs = (node_spec,) * 4 + (node_row, edge_spec, edge_spec, edge_row)
    kept0 = list(zip(names, kinds, specs))
    node_inputs = [("x_now", x_now_t, x_spec), ("x_next", x_next_t, x_spec), ("border", border, border_spec)]
    edges = [("src", source_vertex, ids_spec), ("dst", target_vertex, ids_spec)]

    zero = kernel_call(
        functools.partial(first_kernel, plan, tiles),
        "forward_round0",
        [*several("pack", pack_first), *edges, *node_inputs, ("link", link_t, link_spec)],
        [("h_out", node_f32, node_spec), *kept0, ("e_out", edge_f32, edge_spec)],
        [*weight_scratch, *forward_scratch, *link_scratch, ("h", vmem((latent, nodes)))],
        grid=(graphs, tiles),
        prefetch=[("ids", ids)],
        cost=cost(8, 20_000_000),
    )

    last_at = graphs * tiles - 1

    def early_edge(p, g, t, *_):
        return (jnp.where(p == 0, g * tiles + t, last_at), 0, 0)

    def late_edge(p, g, t, *_):
        return (jnp.where(p == 2, g * tiles + t, 0), 0, 0)

    def early_node(p, g, t, *_):
        return (jnp.where(p == 0, g, graphs - 1), 0, 0)

    def late_node(p, g, t, *_):
        return (jnp.where(p == 2, g, 0), 0, 0)

    def late_x(p, g, t, *_):
        return (0, jnp.where(p == 2, g, 0))

    early_node_spec = pl.BlockSpec((1, latent, nodes), early_node)
    early_edge_spec = pl.BlockSpec((1, latent, tile), early_edge)
    late_node_spec = pl.BlockSpec((1, latent, nodes), late_node)
    late_edge_spec = pl.BlockSpec((1, latent, tile), late_edge)
    tile_ids = pl.BlockSpec((graphs, tile), lambda p, g, t, *_: (0, t))
    kept1 = [
        ("hb", node_bf, early_node_spec),
        ("z1", edge_bf, early_edge_spec),
        ("xh", edge_bf, early_edge_spec),
        ("iv", edge_row_f32, pl.BlockSpec((1, 1, tile), early_edge)),
    ]
    blocks = (Block(plan, True, 0), Block(plan, True, 1), Block(plan, True, 2))

    def grad_outs(r):
        return [(f"grad{k}", sds((blocks[r].total, latent), BF), None) for k in range(plan.fsdp)]

    held = [
        ("hb1", vmem((graphs, latent, nodes), BF)),
        ("aggl1", vmem((graphs, latent, nodes), BF)),
        ("zn1", vmem((graphs, latent, nodes))),
        ("xn1", vmem((graphs, latent, nodes))),
        ("ivn1", vmem((graphs, 1, nodes))),
        ("wan1", vmem((2 * latent, latent), BF)),
        ("wbn1", vmem((latent, latent), BF)),
        ("cols1", vmem((latent, 16))),
        ("d_an1", vmem((2 * latent, latent))),
        ("d_bn1", vmem((latent, latent))),
        ("v_n1", vmem((latent, 512))),
        ("hb2", vmem((graphs, latent, nodes), BF)),
        ("aggl2", vmem((graphs, latent, nodes), BF)),
        ("zn2", vmem((graphs, latent, nodes))),
        ("xn2", vmem((graphs, latent, nodes))),
        ("ivn2", vmem((graphs, 1, nodes))),
        ("h_all", vmem((graphs, latent, nodes))),
        ("e_all", vmem((graphs * tiles, latent, tile))),
        ("low2", vmem((graphs * tiles, latent + 16, tile), BF)),
        ("z12", vmem((graphs * tiles, latent, tile), BF)),
        ("xh2", vmem((graphs * tiles, latent, tile), BF)),
        ("iv2", vmem((graphs * tiles, 1, tile))),
        ("aux", vmem((channels, 256))),
    ]
    mid = kernel_call(
        functools.partial(middle_kernel, plan, blocks[2], graphs, tiles),
        "rounds_middle",
        several("pack", pack_rest)
        + [("src", source_vertex, tile_ids), ("dst", target_vertex, tile_ids)]
        + [("h_in", zero.h_out, early_node_spec), ("e_in", zero.e_out, early_edge_spec)]
        + [("x_now", x_now_t, pl.BlockSpec((channels, nodes), late_x))]
        + [("x_next", x_next_t, pl.BlockSpec((channels, nodes), late_x))]
        + [("border", border, pl.BlockSpec((1, nodes), late_x)), ("level", level, None)]
        + [("stats", stats, None)],
        [*kept1, *grad_outs(2)]
        + [("gh_out", node_f32, late_node_spec), ("gagg_out", node_bf, late_node_spec)]
        + [("ge_out", edge_f32, late_edge_spec)]
        + [("count_out", sds((1, 1), F32), sm)],
        [*weight_scratch, *forward_scratch, *backward_scratch, *held],
        grid=(3, graphs, tiles),
        prefetch=[("ids", ids), ("counts", node_counts)],
        cost=cost(27, 40_000_000),
    )

    anywhere = pl.BlockSpec(memory_space=pl.ANY)

    def graph_spec(value, g):
        rest = (0,) * (len(value.shape) - 1)
        return pl.BlockSpec((1, *value.shape[1:]), lambda *_: (g, *rest))

    def back(r, g, kept, grads, other):
        first = r == 0

        def one(name, value):
            return (name, value, graph_spec(value, g if value.shape[0] > 1 else 0))

        if first:
            ins = several("pack", pack_first)
        else:
            half = pl.BlockSpec((1, plan.total, latent), lambda *_: (0, 0, 0))
            ins = several("pack", pack_rest, half) + several("before", pack_first)
        if other is not None:
            ins += several("other", listed(other, "grad", plan.fsdp))
        ins += [("src", source_vertex, None), ("dst", target_vertex, None), one("hb", kept.hb)]
        ins += [("z1_in", kept.z1, anywhere), ("xh_in", kept.xh, anywhere), ("iv_in", kept.iv, anywhere)]
        ins += [one("gh_in", grads.gh_out), one("gagg_in", grads.gagg_out), ("ge_in", grads.ge_out, anywhere)]
        outs = grad_outs(r)
        scratch = [item for item in weight_scratch if item[0] in ("wa", "wb", "cols")]
        scratch += [("u", vmem((2 * nodes, tile), BF)), ("low_e", vmem((latent + 16, tile), BF))]
        unused = ("d_bn", "d_an", "v_n") if first else ("d_outer", "d_ee")
        scratch += [item for item in backward_scratch if item[0] not in (*unused, "loss")]
        scratch += [
            ("z1", vmem((tiles, latent, tile), BF)),
            ("xh", vmem((tiles, latent, tile), BF)),
            ("iv", vmem((tiles, 1, tile))),
            ("ge", vmem((tiles, latent, tile))),
            ("sems", pltpu.SemaphoreType.DMA((6, tiles))),
        ]
        if first:
            ins += [
                ("x_now", x_now_t, pl.BlockSpec((channels, nodes), lambda *_: (0, g))),
                ("x_next", x_next_t, pl.BlockSpec((channels, nodes), lambda *_: (0, g))),
                ("border", border, pl.BlockSpec((1, nodes), lambda *_: (0, g))),
                one("link", link_t),
            ]
            scratch += [*link_scratch, ("ge_low", vmem((latent, tile), BF))]
        else:
            ins += [("e_in", zero.e_out, anywhere), one("hb0", zero.hb), one("aggl", zero.aggl)]
            ins += [one("zn", zero.zn), one("xn", zero.xn), one("ivn", zero.ivn)]
            outs += [
                ("gh_out", sds((1, latent, nodes), F32), None),
                ("gagg_out", sds((1, latent, nodes), BF), None),
                ("ge_out", sds((tiles, latent, tile), F32), anywhere),
            ]
            scratch += [
                ("e", vmem((tiles, latent, tile))),
                ("wbn", vmem((latent, latent), BF)),
                ("wan", vmem((2 * latent, latent), BF)),
                ("cols1", vmem((latent, 16))),
            ]
        return kernel_call(
            functools.partial(back_kernel, plan, blocks[r], first, g, tiles),
            f"backward_round{r}_graph{g}",
            ins,
            outs,
            scratch,
            grid=(1,),
            prefetch=[("ids", ids)],
            cost=pl.CostEstimate(flops=row_flops * 11 // graphs, bytes_accessed=15_000_000, transcendentals=0),
        )

    def total_of(parts):
        total = parts[0].astype(F32)
        for part in parts[1:]:
            total = total + part.astype(F32)
        return total

    def exchange_grads(bag):
        return exchange(listed(bag, "grad", plan.fsdp), "fsdp", plan.fsdp)

    def owned(got, r):
        return total_of(got).astype(BF).reshape(plan.dp, blocks[r].piece, latent)

    def reduce_owner(value):
        return lax.all_to_all(value, "dp", 0, 0, tiled=True)

    def share(parts):
        total = jnp.sum(parts.astype(F32), axis=0)
        wide = jnp.broadcast_to(total[None], (plan.dp, *total.shape))
        return lax.all_to_all(wide, "dp", 0, 0, tiled=True)

    def after(bag, names, *others):
        values, held = lax.optimization_barrier(([getattr(bag, n) for n in names], others))
        for n, v in zip(names, values):
            setattr(bag, n, v)
        return held

    grad_names = [f"grad{k}" for k in range(plan.fsdp)]
    got2 = exchange_grads(mid)
    one_a = back(1, 0, mid, mid, None)
    owned2 = owned(got2, 2)
    (owned2,) = after(one_a, grad_names, owned2)
    parts2 = reduce_owner(owned2)
    last = one_a
    chain = [one_a]
    for g in range(1, graphs):
        last = back(1, g, mid, mid, last)
        chain.append(last)
    (parts2,) = after(last, grad_names + ["gh_out"], parts2)
    got1 = exchange_grads(last)
    whole2 = share(parts2)
    zero_a = back(0, 0, zero, chain[0], None)
    owned1 = owned(got1, 1)
    owned1, whole2 = after(zero_a, grad_names, owned1, whole2)
    parts1 = reduce_owner(owned1)
    last = zero_a
    for g in range(1, graphs):
        last = back(0, g, zero, chain[g], last)
    (parts1,) = after(last, grad_names, parts1)
    got0 = exchange_grads(last)
    whole1 = share(parts1)
    owned0, whole1 = lax.optimization_barrier((owned(got0, 0), whole1))
    parts0 = reduce_owner(owned0)
    whole0 = share(parts0)

    def turned(group):
        return (group[0].T, *group[1:])

    groups = list(zip(("weight", "moment", "square"), (turned(weights), turned(moments), turned(squares))))
    kinds_new = ("moment_new", "square_new", "weight_new")

    def flat(whole, r):
        return whole.reshape(blocks[r].total, latent)

    def operands(numbers):
        return [(f"{kind}{k}", group[k], None) for kind, group in groups for k in numbers]

    def products(numbers):
        return [(f"{kind}{k}", sds(groups[0][1][k].shape, F32), None) for k in numbers for kind in kinds_new]

    early = kernel_call(
        functools.partial(update_early_kernel, plan, blocks),
        "update_early",
        [("grads2", flat(whole2, 2), None), ("grads1", flat(whole1, 1), None), *operands((2, 3, 4, 5, 6))],
        [*products((2, 3, 4, 5, 6)), ("loss", sds((1, 1), F32), sm)],
        cost=pl.CostEstimate(flops=1000, bytes_accessed=9_000_000, transcendentals=0),
    )

    def slot(value):
        shape = value.shape
        cut = (1, 1, *shape[2:]) if len(shape) == 4 else (1, *shape[1:])
        return pl.BlockSpec(cut, lambda *_: (0,) * len(shape))

    ins = [("grads0", flat(whole0, 0), None)]
    for kind, group in groups:
        ins += [(f"{kind}{k}", group[k], slot(group[k]) if k in (2, 3, 5) else None) for k in (0, 1, 2, 3, 5)]
    outs = [(n, v, None) for n, v, _ in products((0, 1))]
    aliases = {}
    for n, v, _ in products((2, 3, 5)):
        aliases[len(ins)] = len(outs)
        ins.append((f"{n}_early", getattr(early, n), anywhere))
        outs.append((n, v, slot(v)))
    late = kernel_call(
        functools.partial(update_late_kernel, plan, blocks),
        "update_late",
        ins,
        outs,
        grid=(1,),
        aliases=aliases,
    )
    new = Refs()
    for k in range(7):
        for kind in kinds_new:
            setattr(new, f"{kind}{k}", getattr(late if k in (0, 1, 2, 3, 5) else early, f"{kind}{k}"))
    new.loss = early.loss
    results = []
    for k in range(7):
        for kind in ("moment_new", "square_new", "weight_new"):
            value = getattr(new, f"{kind}{k}")
            results.append(value.T if k == 0 else value)
    return (new.loss.reshape(()), mid.count_out.reshape(()), *results)


def solution(mesh):
    rows = P(("dp", "fsdp"), None)
    row = P(("dp", "fsdp"))
    weight_specs = (
        P(None, "fsdp"),
        P(None, "fsdp"),
        P(None, "fsdp", None),
        P(None, None, "fsdp", None),
        P(None, "fsdp", None),
        P(None, None, None, "fsdp"),
        P("fsdp", None),
    )
    placed = (rows, rows, row, row, rows, rows, P(("dp", "fsdp"), None, None), P(), *weight_specs * 3)
    out_specs = [P(), P()]
    for spec in weight_specs:
        out_specs += [spec] * 3

    def step(*args):
        plan = Plan(args[10].shape[2], mesh.shape["dp"], mesh.shape["fsdp"])
        return body(plan, *args)

    return jax.shard_map(
        step, mesh=mesh, in_specs=placed, out_specs=tuple(out_specs), check_vma=False
    )
```

```python
import functools

import jax
import jax.numpy as jnp
from jax import lax
from jax.experimental import pallas as pl
from jax.experimental.pallas import tpu as pltpu
from jax.sharding import PartitionSpec as P

VARS = 6
LEVELS = 13
ROUNDS = 3
STEP = 10

norm_eps = 1e-05
stat_eps = 1e-06
beta_one = 0.9
beta_two = 0.999
adam_eps = 1e-08
decay_rate = 0.01
rate_matrix = 0.03
rate_vector = 0.2

EDGE_FIRST, EDGE_SECOND, NODE_FIRST, NODE_SECOND, ROWS, OUTER = range(6)

BF = jnp.bfloat16
F32 = jnp.float32
VMEM_LIMIT = 56 * 1024 * 1024
EDGE_TILE = 1536
CHUNK = 256


def contract(a, b, da, db):
    return lax.dot_general(a, b, (((da,), (db,)), ((), ())), preferred_element_type=F32)


def nn(a, b):
    return contract(a, b, 1, 0)


def nt(a, b):
    return contract(a, b, 1, 1)


def tn(a, b):
    return contract(a, b, 0, 0)


def sigmoid(v):
    return 0.5 * jnp.tanh(0.5 * v) + 0.5


def silu(v):
    half = 0.5 * v
    return half * jnp.tanh(half) + half


def round_up(v, m):
    return (v + m - 1) // m * m


def stacked(sizes):
    offset = 0
    at = {}
    for name, size in sizes:
        at[name] = (offset, size)
        offset += size
    return at, offset


class Plan:
    def __init__(self, latent, dp_size, fsdp_size):
        self.latent = latent
        self.dp = dp_size
        self.fsdp = fsdp_size
        self.width = latent // fsdp_size
        self.half = self.width // 2
        width = self.width
        sizes = (
            (EDGE_FIRST, 3 * width),
            (EDGE_SECOND, width),
            (NODE_SECOND, width),
            (NODE_FIRST, 2 * width),
            (ROWS, 16),
            (OUTER, self.half),
        )
        self.at, self.total = stacked(sizes)


class Block:
    def __init__(self, plan, node_parts):
        width = plan.width
        sizes = [(EDGE_FIRST, 3 * width), (EDGE_SECOND, width), (ROWS, 16), (OUTER, plan.half)]
        for k in range(node_parts):
            sizes += [((NODE_FIRST, k), 2 * width), ((NODE_SECOND, k), width), ((ROWS, k), 16)]
        self.at, self.used = stacked(sizes)
        self.piece = round_up((self.used + plan.dp - 1) // plan.dp, 8)
        self.total = self.piece * plan.dp


def live_row(border, count):
    place = lax.broadcasted_iota(jnp.int32, border.shape, 1)
    return jnp.where((place < count) & (border != 1), 1.0, 0.0).astype(F32)


def group_matrix(rows, cols, flip):
    var = lax.broadcasted_iota(jnp.int32, (rows, cols), 1 if flip else 0)
    chan = lax.broadcasted_iota(jnp.int32, (rows, cols), 0 if flip else 1)
    inside = (chan >= var * LEVELS) & (chan < (var + 1) * LEVELS)
    return jnp.where(inside, 1.0, 0.0).astype(F32)


def exact(a, b):
    return lax.dot_general(
        a, b, (((1,), (0,)), ((), ())), precision=lax.Precision.HIGHEST, preferred_element_type=F32
    )


class Bag:
    pass


def kernel_call(kernel, name, ins, outs, scratch=None, grid=(), prefetch=None, cost=None, alias=None):
    scratch = scratch or {}
    prefetch = prefetch or {}
    whole = pl.BlockSpec(memory_space=pltpu.VMEM)

    def flat(group):
        return [(n, v) for n, vs in group.items() for v in (vs if isinstance(vs, list) else [vs])]

    def fill(groups, values):
        bag = Bag()
        at = 0
        for group in groups:
            for n, vs in group.items():
                count = len(vs) if isinstance(vs, list) else None
                if count is None:
                    setattr(bag, n, values[at])
                    at += 1
                else:
                    setattr(bag, n, list(values[at : at + count]))
                    at += count
        return bag

    def split(item):
        if isinstance(item, tuple):
            return item
        if not grid:
            return item, whole
        rank = len(item.shape)
        return item, pl.BlockSpec(item.shape, lambda *_: (0,) * rank)

    def run(*refs):
        kernel(fill((prefetch, ins, outs, scratch), refs))

    sources = [split(v) for _, v in flat(ins)]
    products = [split(v) for _, v in flat(outs)]
    aliases = {}
    if alias:
        first_in = [n for n, _ in flat(ins)].index(alias[0]) + len(prefetch)
        first_out = [n for n, _ in flat(outs)].index(alias[1])
        aliases = {first_in + k: first_out + k for k in range(len(ins[alias[0]]))}
    result = pl.pallas_call(
        run,
        out_shape=[v for v, _ in products],
        grid_spec=pltpu.PrefetchScalarGridSpec(
            num_scalar_prefetch=len(prefetch),
            grid=grid,
            in_specs=[spec for _, spec in sources],
            out_specs=[spec for _, spec in products],
            scratch_shapes=list(scratch.values()),
        ),
        compiler_params=pltpu.CompilerParams(vmem_limit_bytes=VMEM_LIMIT),
        input_output_aliases=aliases,
        cost_estimate=pl.CostEstimate(flops=cost[0], bytes_accessed=cost[1], transcendentals=0),
        name=name,
    )(*prefetch.values(), *[v for v, _ in sources])
    return fill((outs,), result)


def pack_round(plan, out, r, edge_first, second_layers, node_first, vectors, edge_encoder, outer):
    width = plan.width
    at = plan.at

    def put(name, value):
        start, size = at[name]
        out[start : start + size, :] = value.astype(BF)

    put(EDGE_FIRST, edge_first[r])
    put(EDGE_SECOND, second_layers[r, 0])
    put(NODE_SECOND, second_layers[r, 1])
    put(NODE_FIRST, node_first[r])
    rows = jnp.concatenate([vectors[r, 0], vectors[r, 1]], axis=0)
    if edge_encoder is None:
        low = jnp.zeros((8, width), F32)
    else:
        low = jnp.concatenate([edge_encoder[...], jnp.zeros((4, width), F32)], axis=0)
    rows = jnp.concatenate([rows, low], axis=0)
    rows = jnp.concatenate([rows, jnp.zeros((16, plan.latent - width), F32)], axis=1)
    put(ROWS, rows)
    start, size = at[OUTER]
    if outer is None:
        out[start : start + size, :] = jnp.zeros((size, plan.latent), BF)
    else:
        channels = outer.shape[1]
        wide = jnp.concatenate(
            [outer[...], jnp.zeros((width, plan.latent // 2 - channels), F32)], axis=1
        )
        put(OUTER, jnp.concatenate([wide[: plan.half], wide[plan.half :]], axis=1))


def pack_first_kernel(plan, b):
    pack_round(plan, b.pack, 0, b.ef, b.sl, b.nf, b.vec, b.ee, b.enc)


def merge_stats(stats):
    total = jnp.sum(stats, axis=0)
    count = total[:, 2:3]
    mean = total[:, 0:1] / (count * LEVELS)
    own_count = stats[:, :, 2:3] * LEVELS
    shift = stats[:, :, 0:1] / jnp.maximum(own_count, 1.0) - mean[None]
    spread = jnp.sum(stats[:, :, 1:2] + own_count * shift * shift, axis=0)
    return count, spread


def pack_rest_kernel(plan, graphs, b):
    pack_round(plan, b.pack.at[0], 1, b.ef, b.sl, b.nf, b.vec, None, None)
    pack_round(plan, b.pack.at[1], 2, b.ef, b.sl, b.nf, b.vec, None, b.dec)
    nodes = b.x_now.shape[1] // graphs
    channels = b.x_now.shape[0]
    lives = []
    for g in range(graphs):
        lives.append(live_row(b.border[:, g * nodes : (g + 1) * nodes], b.counts[g]))
    live = jnp.concatenate(lives, axis=1)
    delta = b.x_next[...] - b.x_now[...]
    count = jnp.sum(live)
    sums = jnp.sum(delta * live, axis=1, keepdims=True)
    to_var = group_matrix(8, channels, False)
    to_chan = group_matrix(channels, 8, True)
    var_sum = exact(to_var, jnp.broadcast_to(sums, (channels, 128)))
    mean = var_sum / (jnp.maximum(count, 1.0) * LEVELS)
    centered = (delta - exact(to_chan, mean)[:, 0:1]) * live
    square = jnp.sum(centered * centered, axis=1, keepdims=True)
    var_square = exact(to_var, jnp.broadcast_to(square, (channels, 128)))
    lane = lax.broadcasted_iota(jnp.int32, (8, 128), 1)
    value = jnp.where(lane == 0, var_sum, jnp.where(lane == 1, var_square, count))
    b.stats[...] = jnp.broadcast_to(value[None], b.stats.shape)


def assemble(plan, me, packs, edge_first=None, edge_second=None, node_second=None, node_first=None, cols=None, outer=None):
    width = plan.width
    latent = plan.latent
    total = jnp.zeros((latent, 16), F32)
    rowid = lax.broadcasted_iota(jnp.int32, (latent, width), 0)
    colid = lax.broadcasted_iota(jnp.int32, (latent, width), 1)
    for k, pack in enumerate(packs):
        owner = jnp.bitwise_xor(me, k)

        def put(ref, name, step):
            if ref is not None:
                start, size = plan.at[name]
                ref[pl.ds(pl.multiple_of(owner * step, 16), size), :] = pack[start : start + size, :]

        put(edge_first, EDGE_FIRST, 3 * width)
        put(edge_second, EDGE_SECOND, width)
        put(node_second, NODE_SECOND, width)
        put(node_first, NODE_FIRST, 2 * width)
        start, size = plan.at[ROWS]
        place = jnp.where(rowid == owner * width + colid, 1.0, 0.0).astype(BF)
        total = total + nt(place, pack[start : start + size, 0:width])
        if outer is not None:
            start, size = plan.at[OUTER]
            half = latent // 2
            first = pl.multiple_of(owner * width, 16)
            second = pl.multiple_of(owner * width + plan.half, 16)
            outer[pl.ds(first, size), :] = pack[start : start + size, 0:half]
            outer[pl.ds(second, size), :] = pack[start : start + size, half : 2 * half]
    cols[...] = total


def assemble_all(plan, b, packs, outer):
    assemble(plan, b.ids[0], packs, b.wa, b.wb, b.wbn, b.wan, b.cols, b.outer if outer else None)


def turn_weights(plan, b, nodes):
    latent = plan.latent
    b.b_t[...] = b.wb[...].astype(F32).T.astype(BF)
    b.pcat[:, 2 * nodes :] = b.wa[2 * latent :, :].astype(F32).T.astype(BF)


def fill_tables(u_ref, src, dst, nodes, lanes):
    count = lanes.stop - lanes.start
    place = lax.broadcasted_iota(jnp.int32, (nodes, count), 0).astype(jnp.int16)
    one = jnp.ones((nodes, count), BF)
    zero = jnp.zeros((nodes, count), BF)
    u_ref[0:nodes, lanes] = jnp.where(place == src[:, lanes].astype(jnp.int16), one, zero)
    u_ref[nodes : 2 * nodes, lanes] = jnp.where(place == dst[:, lanes].astype(jnp.int16), one, zero)


def skew(chunks):
    live = []
    waiting = list(chunks)
    while live or waiting:
        if waiting:
            live.append(waiting.pop(0))
        for item in list(reversed(live)):
            if next(item, 1) == 1:
                live.remove(item)


def norm_forward(z2, count):
    mean = jnp.sum(z2, axis=0, keepdims=True) * (1.0 / count)
    centered = z2 - mean
    var = jnp.sum(centered * centered, axis=0, keepdims=True) * (1.0 / count)
    inverse = lax.rsqrt(var + norm_eps)
    return centered * inverse, inverse


def forward_nodes_in(plan, b, state):
    latent = plan.latent
    nodes = state.shape[-1]
    low = state.astype(BF)
    b.pcat[:, 0:nodes] = tn(b.wa[0:latent, :], low).astype(BF)
    b.pcat[:, nodes : 2 * nodes] = tn(b.wa[latent : 2 * latent, :], low).astype(BF)
    b.agg[...] = jnp.zeros_like(b.agg)
    return low


def forward_edges(plan, b, src, dst, tile, get, put, kept):
    nodes = b.agg.shape[-1]
    z1_ref, xh_ref, iv_ref = kept

    def chunk(at):
        lanes = slice(at, at + CHUNK)
        fill_tables(b.u, src, dst, nodes, lanes)
        b.u[2 * nodes :, lanes] = get(lanes).astype(BF)
        yield
        z1 = nn(b.pcat[...], b.u[:, lanes])
        yield
        z1 = z1 + b.cols[:, 0:1]
        active = silu(z1).astype(BF)
        z1_ref[:, lanes] = z1.astype(BF)
        yield
        z2 = nn(b.b_t[...], active)
        yield
        z2 = z2 + b.cols[:, 1:2]
        normed, inverse = norm_forward(z2, plan.latent)
        xh_ref[:, lanes] = normed.astype(BF)
        iv_ref[:, lanes] = inverse
        e = get(lanes) + (normed * b.cols[:, 2:3] + b.cols[:, 3:4])
        if put is not None:
            put(lanes, e)
        b.new_low[:, lanes] = e.astype(BF)
        yield

    skew([chunk(at) for at in range(0, tile, CHUNK)])
    b.agg[...] += nt(b.new_low[...], b.u[nodes : 2 * nodes, :])


def forward_nodes_out(plan, b, state, low):
    latent = plan.latent
    arriving = b.agg[...].astype(BF)
    z1 = tn(b.wan[0:latent, :], low) + tn(b.wan[latent:, :], arriving) + b.cols[:, 4:5]
    active = silu(z1).astype(BF)
    z2 = tn(b.wbn[...], active) + b.cols[:, 5:6]
    normed, inverse = norm_forward(z2, latent)
    return arriving, z1, normed, inverse, state + (normed * b.cols[:, 6:7] + b.cols[:, 7:8])


def norm_backward(grad, gain, normed, inverse, count):
    scaled = grad * gain
    mean = jnp.sum(scaled, axis=0, keepdims=True) * (1.0 / count)
    cross = jnp.sum(scaled * normed, axis=0, keepdims=True) * (1.0 / count)
    return (inverse * (scaled - mean - normed * cross)).astype(BF)


def lane_sum(value):
    total = value[:, 0:128]
    for k in range(1, value.shape[1] // 128):
        total = total + value[:, 128 * k : 128 * (k + 1)]
    return total


def backward_reset(plan, b, tile, refs):
    for ref in refs:
        ref[...] = jnp.zeros_like(ref)
    b.act[plan.latent :, :] = jnp.ones((16, tile), BF)


def backward_nodes_in(plan, weights, sums, grad, low_h, arriving, z1, normed, inverse):
    latent = plan.latent
    wan, wbn, cols = weights
    z1 = z1.astype(F32)
    normed = normed.astype(F32)
    d_an, d_bn, v_n = sums
    v_n[:, 0:128] += lane_sum(grad * normed)
    v_n[:, 128:256] += lane_sum(grad)
    low_two = norm_backward(grad, cols[:, 6:7], normed, inverse, latent)
    gate = sigmoid(z1)
    soft = z1 * gate
    d_bn[...] += nt(soft.astype(BF), low_two)
    d_active = nn(wbn[...], low_two)
    low_one = (d_active * (soft - soft * gate + gate)).astype(BF)
    v_n[:, 256:384] += lane_sum(low_one.astype(F32))
    v_n[:, 384:512] += lane_sum(low_two.astype(F32))
    d_an[0:latent, :] += nt(low_h, low_one)
    d_an[latent:, :] += nt(arriving, low_one)
    return grad + nn(wan[0:latent, :], low_one), nn(wan[latent:, :], low_one).astype(BF)


def backward_edges(plan, b, src, dst, tile, get, kept, low_e, put):
    z1_ref, xh_ref, iv_ref = kept
    latent = plan.latent
    nodes = b.gagg.shape[-1]

    def chunk(at):
        lanes = slice(at, at + CHUNK)
        fill_tables(b.u, src, dst, nodes, lanes)
        yield
        ge = nn(b.gagg[...], b.u[nodes : 2 * nodes, lanes])
        yield
        if get is not None:
            ge = ge + get(lanes)
        normed = xh_ref[:, lanes].astype(F32)
        b.v_e[:, 0:128] += lane_sum(ge * normed)
        b.v_e[:, 128:256] += lane_sum(ge)
        low_two = norm_backward(ge, b.cols[:, 2:3], normed, iv_ref[:, lanes], latent)
        b.two[:, lanes] = low_two
        yield
        d_active = nn(b.wb[...], low_two)
        yield
        z1 = z1_ref[:, lanes].astype(F32)
        gate = sigmoid(z1)
        soft = z1 * gate
        b.act[0:latent, lanes] = soft.astype(BF)
        low_one = (d_active * (soft - soft * gate + gate)).astype(BF)
        b.one[:, lanes] = low_one
        yield
        put(lanes, ge + nn(b.wa[2 * latent :, :], low_one))
        yield

    skew([chunk(at) for at in range(0, tile, CHUNK)])
    b.d_b[...] += nt(b.act[...], b.two[...])
    b.d_first[2 * latent :, :] += nt(low_e[...], b.one[...])
    b.q[...] += nt(b.one[...], b.u[0 : 2 * nodes, :])


def backward_nodes_out(plan, b, low_h):
    latent = plan.latent
    nodes = b.gagg.shape[-1]
    total = b.gh[...]
    for side in range(2):
        sums = b.q[:, side * nodes : (side + 1) * nodes]
        high = sums.astype(BF)
        rest = (sums - high.astype(F32)).astype(BF)
        rows = slice(side * latent, (side + 1) * latent)
        b.d_first[rows, :] += nt(low_h, high) + nt(low_h, rest)
        total = total + nn(b.wa[rows, :], high) + nn(b.wa[rows, :], rest)
    return total


def row_of(cols128):
    return jnp.sum(cols128.T, axis=0, keepdims=True)


def backward_emit(plan, block, b, low, outer, node_sums, before):
    latent = plan.latent
    width = plan.width
    rows = [
        b.d_first[3 * latent : 3 * latent + 1, :],
        b.d_b[latent : latent + 1, :],
        row_of(b.v_e[:, 0:128]),
        row_of(b.v_e[:, 128:256]),
        jnp.zeros((4, latent), F32),
        jnp.zeros((8, latent), F32) if low is None else low,
    ]
    groups = [(ROWS, jnp.concatenate(rows, axis=0).astype(BF))]
    for k, (_, _, v_n) in enumerate(node_sums):
        rows = [
            row_of(v_n[:, 256:384]),
            row_of(v_n[:, 384:512]),
            row_of(v_n[:, 0:128]),
            row_of(v_n[:, 128:256]),
            jnp.zeros((12, latent), F32),
        ]
        groups.append(((ROWS, k), jnp.concatenate(rows, axis=0).astype(BF)))
    rowid = lax.broadcasted_iota(jnp.int32, (latent, latent), 0)
    colid = lax.broadcasted_iota(jnp.int32, (latent, latent), 1)
    for k, out in enumerate(b.grad):
        owner = jnp.bitwise_xor(b.ids[0], k)

        def put(name, value):
            start, size = block.at[name]
            rows = slice(start, start + size)
            if before is not None:
                value = value + before[k][rows, :].astype(F32)
            out[rows, :] = value.astype(BF)

        def take(ref, step):
            return ref[pl.ds(pl.multiple_of(owner * step, 8), step), :]

        put(EDGE_FIRST, take(b.d_first, 3 * width))
        put(EDGE_SECOND, take(b.d_b, width))
        inside = (rowid == owner * width + colid) & (colid < width)
        place = jnp.where(inside, 1.0, 0.0).astype(BF)
        for name, value in groups:
            put(name, nn(value, place))
        if outer is not None:
            own = take(outer, width)
            put(OUTER, jnp.concatenate([own[: plan.half], own[plan.half :]], axis=1))
        else:
            put(OUTER, jnp.zeros((plan.half, latent), F32))
        for k2, (d_an, d_bn, _) in enumerate(node_sums):
            put((NODE_FIRST, k2), take(d_an, 2 * width))
            put((NODE_SECOND, k2), take(d_bn, width))
        if block.total > block.used:
            out[block.used :, :] = jnp.zeros((block.total - block.used, latent), BF)


def split_three(whole, lanes, period, place):
    high = whole.astype(BF).astype(F32)
    mid = (whole - high).astype(BF).astype(F32)
    rest = whole - high - mid
    lane = lax.broadcasted_iota(jnp.int32, (8, lanes), 1) % period - 3 * place
    top = lax.broadcasted_iota(jnp.int32, (8, lanes), 0) == 0
    value = jnp.where(lane == 0, high, jnp.where(lane == 1, mid, jnp.where(lane == 2, rest, 0.0)))
    return jnp.where(top, value, 0.0)


def first_kernel(plan, tiles, b):
    g = pl.program_id(0)
    t = pl.program_id(1)
    nodes = b.h_out.shape[-1]
    tile = b.z1.shape[-1]

    @pl.when((g == 0) & (t == 0))
    def _():
        assemble_all(plan, b, b.pack, True)
        turn_weights(plan, b, nodes)
        b.link8[...] = jnp.zeros_like(b.link8)

    @pl.when(t == 0)
    def _():
        chosen = jnp.where(b.border[...] == 1, b.x_next[...], b.x_now[...]).astype(BF)
        b.h[...] = nn(b.outer[:, 0 : b.x_now.shape[0]], chosen)
        b.hb[0] = forward_nodes_in(plan, b, b.h[...])

    b.link8[0:4, :] = b.link[0]

    def get(lanes):
        return nn(b.cols[:, 8:16].astype(BF), b.link8[:, lanes].astype(BF))

    def put(lanes, value):
        b.e_out[0, :, lanes] = value

    kept = (b.z1.at[0], b.xh.at[0], b.iv.at[0])
    forward_edges(plan, b, b.src[pl.ds(g, 1), :], b.dst[pl.ds(g, 1), :], tile, get, put, kept)

    @pl.when(t == tiles - 1)
    def _():
        state = b.h[...]
        b.aggl[0], z1, normed, b.ivn[0], b.h_out[0] = forward_nodes_out(plan, b, state, state.astype(BF))
        b.zn[0] = z1.astype(BF)
        b.xn[0] = normed.astype(BF)


def middle_kernel(plan, block, graphs, tiles, b):
    p = pl.program_id(0)
    g = pl.program_id(1)
    t = pl.program_id(2)
    nodes = b.gh_out.shape[-1]
    tile = b.z1.shape[-1]
    latent = plan.latent
    channels = b.x_now.shape[0]
    at = g * tiles + t
    start = (g == 0) & (t == 0)
    src = b.src[pl.ds(g, 1), :]
    dst = b.dst[pl.ds(g, 1), :]

    @pl.when((p == 0) & start)
    def _():
        assemble_all(plan, b, [r.at[0] for r in b.pack], False)
        turn_weights(plan, b, nodes)
        b.wan1[...] = b.wan[...]
        b.wbn1[...] = b.wbn[...]
        b.cols1[...] = b.cols[...]
        refs = (b.d_first, b.d_b, b.v_e, b.d_bn, b.d_an, b.v_n, b.d_bn1, b.d_an1, b.v_n1, b.d_outer, b.loss)
        backward_reset(plan, b, tile, refs)
        count, spread = merge_stats(b.stats[...])
        scale = lax.rsqrt(spread / (count * LEVELS) + stat_eps)
        b.aux[:, 0:128] = exact(group_matrix(channels, 8, True), jnp.broadcast_to(scale, (8, 128)))
        b.aux[:, 128:256] = jnp.broadcast_to(count[0:1] * channels, (channels, 128))
        b.count_out[0, 0] = jnp.sum(count[0:1]) * channels

    @pl.when((p == 1) & start)
    def _():
        assemble_all(plan, b, [r.at[1] for r in b.pack], True)
        turn_weights(plan, b, nodes)

    @pl.when((p == 0) & (t == 0))
    def _():
        b.hb[0] = forward_nodes_in(plan, b, b.h_in[0])

    @pl.when(p == 0)
    def _():
        def get(lanes):
            return b.e_in[0, :, lanes]

        def put(lanes, value):
            b.e_all[at, :, lanes] = value

        forward_edges(plan, b, src, dst, tile, get, put, (b.z1.at[0], b.xh.at[0], b.iv.at[0]))

    @pl.when((p == 0) & (t == tiles - 1))
    def _():
        state = b.h_in[0]
        b.hb1[g] = state.astype(BF)
        b.aggl1[g], b.zn1[g], b.xn1[g], b.ivn1[g], b.h_all[g] = forward_nodes_out(plan, b, state, b.hb1[g])

    @pl.when((p == 1) & (t == 0))
    def _():
        b.hb2[g] = forward_nodes_in(plan, b, b.h_all[g])

    @pl.when(p == 1)
    def _():
        b.low2[at, latent:, :] = jnp.ones((16, tile), BF)

        def get(lanes):
            return b.e_all[at, :, lanes]

        forward_edges(plan, b, src, dst, tile, get, None, (b.z12.at[at], b.xh2.at[at], b.iv2.at[at]))
        b.low2[at, 0:latent, :] = b.u[2 * nodes :, :]

    @pl.when((p == 1) & (t == tiles - 1))
    def _():
        b.aggl2[g], b.zn2[g], b.xn2[g], b.ivn2[g], b.h_all[g] = forward_nodes_out(
            plan, b, b.h_all[g], b.hb2[g]
        )

    @pl.when((p == 2) & (t == 0))
    def _():
        final_low = b.h_all[g].astype(BF)
        delta = b.x_next[...] - b.x_now[...]
        scale = b.aux[:, 0:1]
        norm_count = b.aux[:, 128:129]
        predicted = tn(b.outer[...], final_low)[0:channels]
        misfit = (predicted - delta) * scale
        weighting = (b.level[...].astype(F32) + 1.0) / LEVELS * live_row(b.border[...], b.counts[g])
        b.loss[...] += jnp.broadcast_to(jnp.sum(weighting * misfit * misfit), b.loss.shape)
        grad_pred = (2.0 * weighting * misfit * scale / norm_count).astype(BF)
        b.d_outer[:, 0:channels] += nt(final_low, grad_pred)
        grad = nn(b.outer[:, 0:channels], grad_pred)
        b.gh[...], b.gagg[...] = backward_nodes_in(
            plan,
            (b.wan, b.wbn, b.cols),
            (b.d_an, b.d_bn, b.v_n),
            grad,
            b.hb2[g],
            b.aggl2[g],
            b.zn2[g],
            b.xn2[g],
            b.ivn2[g],
        )
        b.q[...] = jnp.zeros_like(b.q)

    @pl.when(p == 2)
    def _():
        def put(lanes, value):
            b.ge_out[0, :, lanes] = value

        kept = (b.z12.at[at], b.xh2.at[at], b.iv2.at[at])
        backward_edges(plan, b, src, dst, tile, None, kept, b.low2.at[at], put)

    @pl.when((p == 2) & (t == tiles - 1))
    def _():
        grad = backward_nodes_out(plan, b, b.hb2[g])
        b.gh_out[0], b.gagg_out[0] = backward_nodes_in(
            plan,
            (b.wan1, b.wbn1, b.cols1),
            (b.d_an1, b.d_bn1, b.v_n1),
            grad,
            b.hb1[g],
            b.aggl1[g],
            b.zn1[g],
            b.xn1[g],
            b.ivn1[g],
        )

    @pl.when((p == 2) & (g == graphs - 1) & (t == tiles - 1))
    def _():
        low = split_three(b.loss[0:1, 0:1], latent, plan.width, b.ids[0])
        sums = ((b.d_an, b.d_bn, b.v_n), (b.d_an1, b.d_bn1, b.v_n1))
        backward_emit(plan, block, b, low, b.d_outer, sums, None)


def back_kernel(plan, block, first, places, tiles, b):
    tile = b.u.shape[-1]
    latent = plan.latent

    def copies(pairs, row):
        return [pltpu.make_async_copy(x, y, b.sems.at[row, k]) for k, (x, y) in enumerate(pairs)]

    picked = b.pack_in if first else [r.at[0] for r in b.pack_in]
    weights = copies([(x, b.pack.at[k]) for k, x in enumerate(picked)], 0)
    early = []
    late = []
    moves = []
    ends = []
    for k, g in enumerate(places):
        own = g if b.gh_in.shape[0] > 1 else 0
        pairs = [(b.gagg_in.at[own], b.gagg_all.at[k]), (b.gh_in.at[own], b.gh_all.at[k])]
        early.append(copies(pairs, 1 + k))
        pairs = [(b.hb_in.at[g], b.hb.at[k])]
        if not first:
            nodes_in = ((b.hb0_in, b.hb0), (b.aggl_in, b.aggl), (b.zn_in, b.zn), (b.xn_in, b.xn), (b.ivn_in, b.ivn))
            pairs += [(x.at[g], y.at[k]) for x, y in nodes_in]
        late.append(copies(pairs, 3 + k))
        for t in range(tiles):
            at = k * tiles + t
            place = g * tiles + t
            source = place if b.ge_in.shape[0] > tiles else t
            pairs = [(b.z1_in.at[place], b.z1.at[at]), (b.xh_in.at[place], b.xh.at[at])]
            pairs += [(b.iv_in.at[place], b.iv.at[at]), (b.ge_in.at[source], b.ge.at[at])]
            if not first:
                pairs.append((b.e_in.at[place], b.e.at[at]))
                ends.append(pltpu.make_async_copy(b.ge.at[at], b.ge_out.at[at], b.sems.at[5 + at, 6]))
            moves.append(copies(pairs, 5 + at))
    rest = [] if first else copies([(x, b.before.at[k]) for k, x in enumerate(b.before_in)], 5 + len(moves))
    for group in (weights, early[0], moves[0], *moves[1:], *early[1:], *late, rest):
        for copy in group:
            copy.start()

    def wait(group):
        for copy in group:
            copy.wait()

    sums = [b.d_first, b.d_b, b.v_e]
    sums += [b.d_outer, b.d_ee, b.link8] if first else [b.d_bn, b.d_an, b.v_n]
    backward_reset(plan, b, tile, sums)
    b.low_e[latent:, :] = jnp.ones((16, tile), BF)
    wait(weights)
    assemble(plan, b.ids[0], [b.pack.at[k] for k in range(plan.fsdp)], b.wa, b.wb, cols=b.cols)
    for k, g in enumerate(places):
        wait(early[k])
        b.gagg[...] = b.gagg_all[k]
        b.gh[...] = b.gh_all[k]
        b.q[...] = jnp.zeros_like(b.q)
        for t in range(tiles):
            at = k * tiles + t
            wait(moves[at])
            lanes = slice(t * tile, (t + 1) * tile)
            kept = (b.z1.at[at], b.xh.at[at], b.iv.at[at])

            def get(lanes, at=at):
                return b.ge[at, :, lanes]

            if first:
                b.link8[0:4, :] = b.link[k, :, lanes]
                b.low_e[0:latent, :] = nn(b.cols[:, 8:16].astype(BF), b.link8[...].astype(BF)).astype(BF)

                def put(lanes, value):
                    b.ge_low[:, lanes] = value.astype(BF)
            else:
                b.low_e[0:latent, :] = b.e[at].astype(BF)

                def put(lanes, value, at=at):
                    b.ge[at, :, lanes] = value

            src = b.src[g : g + 1, lanes]
            dst = b.dst[g : g + 1, lanes]
            backward_edges(plan, b, src, dst, tile, get, kept, b.low_e, put)
            if first:
                b.d_ee[...] += nt(b.ge_low[...], b.link8[...].astype(BF))
            else:
                ends[at].start()
        wait(late[k])
        total = backward_nodes_out(plan, b, b.hb[k])
        if first:
            chosen = jnp.where(b.border[...] == 1, b.x_next[...], b.x_now[...]).astype(BF)
            b.d_outer[:, 0 : b.x_now.shape[0]] += nt(total.astype(BF), chosen)
        else:
            if k == 0:
                wait(rest)
                packs = [b.before.at[k] for k in range(plan.fsdp)]
                assemble(plan, b.ids[0], packs, node_second=b.wbn, node_first=b.wan, cols=b.cols1)
            b.gh_out[k], b.gagg_out[k] = backward_nodes_in(
                plan,
                (b.wan, b.wbn, b.cols1),
                (b.d_an, b.d_bn, b.v_n),
                total,
                b.hb0[k],
                b.aggl[k],
                b.zn[k],
                b.xn[k],
                b.ivn[k],
            )
    if first:
        backward_emit(plan, block, b, b.d_ee[...].T, b.d_outer, (), b.other if places[0] > 0 else None)
    else:
        backward_emit(plan, block, b, None, None, ((b.d_an, b.d_bn, b.v_n),), None)
    wait(ends)


def owner_sum_kernel(plan, block, b):
    total = b.got[0][...].astype(F32)
    for ref in b.got[1:]:
        total = total + ref[...].astype(F32)
    b.total[...] = total
    for k, out in enumerate(b.parts):
        place = jnp.bitwise_xor(b.ids[1], k)
        out[...] = b.total[pl.ds(pl.multiple_of(place * block.piece, 8), block.piece), :].astype(BF)


def adam_math(weight, moment, square, gradient, rate):
    moment_new = beta_one * moment + (1.0 - beta_one) * gradient
    square_new = beta_two * square + (1.0 - beta_two) * gradient * gradient
    direction = (
        moment_new
        * (1.0 / (1.0 - beta_one**STEP))
        / (jnp.sqrt(square_new * (1.0 / (1.0 - beta_two**STEP))) + adam_eps)
    )
    return (moment_new, square_new, weight - rate * (direction + decay_rate * weight))


def apply_update(b, k, index, gradient, rate):
    new = adam_math(b.weight[k][index], b.moment[k][index], b.square[k][index], gradient, rate)
    for ref, value in zip(b.new[k], new):
        ref[index] = value


def by_number(b, numbers, products):
    for group in (b.weight, b.moment, b.square):
        group[:] = [group[numbers.index(k)] if k in numbers else None for k in range(7)]
    b.new = [products[3 * numbers.index(k) : 3 * numbers.index(k) + 3] if k in numbers else None for k in range(7)]


def part_of(ref, block, name):
    start, size = block.at[name]
    return ref[start : start + size, :]


def update_edge(plan, b, ref, block, at):
    apply_update(b, 2, at, part_of(ref, block, EDGE_FIRST), rate_matrix)
    apply_update(b, 3, (at, 0), part_of(ref, block, EDGE_SECOND), rate_matrix)
    rows = part_of(ref, block, ROWS)
    apply_update(b, 5, (at, 0), rows[0:4, 0 : plan.width], rate_vector)
    half = plan.latent // 2
    wide = part_of(ref, block, OUTER)
    return rows, jnp.concatenate([wide[:, 0:half], wide[:, half:]], axis=0)


def update_early_kernel(plan, blocks, numbers, b):
    by_number(b, numbers, b.products)
    width = plan.width
    for source in range(plan.dp):
        for target, block, start in ((b.grads2, blocks[2], 0), (b.grads1, blocks[1], blocks[2].piece)):
            rows = slice(source * block.piece, (source + 1) * block.piece)
            target[rows, :] = b.shared[source, start : start + block.piece, :]
    rows, outer = update_edge(plan, b, b.grads2, blocks[2], 2)
    apply_update(b, 6, Ellipsis, outer[:, 0 : b.weight[6].shape[1]], rate_matrix)
    lane = lax.broadcasted_iota(jnp.int32, (1, plan.latent), 1)
    b.loss[0, 0] = jnp.sum(jnp.where(lane < width, rows[8:9, :], 0.0))
    update_edge(plan, b, b.grads1, blocks[1], 1)
    for r, ref, block, k in ((2, b.grads2, blocks[2], 0), (1, b.grads2, blocks[2], 1), (0, b.grads1, blocks[1], 0)):
        apply_update(b, 4, r, part_of(ref, block, (NODE_FIRST, k)), rate_matrix)
        apply_update(b, 3, (r, 1), part_of(ref, block, (NODE_SECOND, k)), rate_matrix)
        apply_update(b, 5, (r, 1), part_of(ref, block, (ROWS, k))[0:4, 0:width], rate_vector)


def update_late_kernel(plan, block, numbers, b):
    by_number(b, numbers, b.products + b.slots)
    for k, piece in enumerate(b.pieces):
        place = jnp.bitwise_xor(b.ids[1], k)
        b.grads[pl.ds(pl.multiple_of(place * block.piece, 8), block.piece), :] = piece[...]
    rows, outer = update_edge(plan, b, b.grads, block, 0)
    apply_update(b, 0, Ellipsis, outer[:, 0 : b.weight[0].shape[1]], rate_matrix)
    apply_update(b, 1, Ellipsis, rows[8:12, 0 : plan.width], rate_matrix)


def body(plan, *args):
    x_now, x_next, node_counts, border_flag, source_vertex, target_vertex, link_features, level_ids = args[:8]
    weights = args[8:15]
    moments = args[15:22]
    squares = args[22:29]
    encoder, edge_encoder, edge_first, second_layers, node_first, vectors, decoder = weights
    graphs, edge_count = source_vertex.shape
    nodes = x_now.shape[0] // graphs
    channels = x_now.shape[1]
    latent = plan.latent
    tile = EDGE_TILE
    tiles = edge_count // tile
    x_now_t = x_now.T
    x_next_t = x_next.T
    border = border_flag.reshape(1, -1)
    link_t = jnp.transpose(link_features, (0, 2, 1))
    level = level_ids.reshape(-1, 1)
    ids = jnp.stack([lax.axis_index("fsdp"), lax.axis_index("dp")]).astype(jnp.int32)

    sm = pl.BlockSpec(memory_space=pltpu.SMEM)
    sds = jax.ShapeDtypeStruct
    pack_shape = sds((plan.total, latent), BF)
    devices = plan.dp * plan.fsdp

    def across(value, axis, size, mask):
        return lax.ppermute(value, axis, [(j, j ^ mask) for j in range(size)])

    def spread_chain(own, beside):
        got = [own]
        for k in range(1, plan.fsdp):
            source = got[k & (k - 1)]
            if k & (k - 1):
                source, _ = lax.optimization_barrier((source, beside))
            got.append(across(source, "fsdp", plan.fsdp, k & -k))
        return got

    def spread_direct(own, axis, size):
        return [own] + [across(own, axis, size, k) for k in range(1, size)]

    def exchange(parts, axis, size):
        return [parts[0]] + [across(parts[k], axis, size, k) for k in range(1, size)]

    raw = dict(ef=edge_first, sl=second_layers, nf=node_first, vec=vectors)
    start = kernel_call(
        functools.partial(pack_first_kernel, plan),
        "pack_first",
        dict(**raw, ee=edge_encoder, enc=encoder.T),
        dict(pack=pack_shape),
        cost=(1000, 3_000_000),
    )
    rest = kernel_call(
        functools.partial(pack_rest_kernel, plan, graphs),
        "pack_rest",
        dict(counts=(node_counts, sm), **raw, dec=decoder, x_now=x_now_t, x_next=x_next_t, border=border),
        dict(pack=sds((2, plan.total, latent), BF), stats=sds((devices, 8, 128), F32)),
        cost=(1000, 8_000_000),
    )
    pack_first = spread_chain(start.pack, rest.pack)
    pack_rest = spread_direct(rest.pack, "fsdp", plan.fsdp)
    stats = lax.all_to_all(rest.stats, ("dp", "fsdp"), 0, 0, tiled=True)

    ids_spec = pl.BlockSpec((graphs, tile), lambda g, t, *_: (0, t))
    x_spec = pl.BlockSpec((channels, nodes), lambda g, t, *_: (0, g))
    border_spec = pl.BlockSpec((1, nodes), lambda g, t, *_: (0, g))
    link_spec = pl.BlockSpec((1, 4, tile), lambda g, t, *_: (g, 0, t))
    node_spec = pl.BlockSpec((1, latent, nodes), lambda g, t, *_: (g, 0, 0))
    node_row = pl.BlockSpec((1, 1, nodes), lambda g, t, *_: (g, 0, 0))
    edge_spec = pl.BlockSpec((1, latent, tile), lambda g, t, *_: (g * tiles + t, 0, 0))
    edge_row = pl.BlockSpec((1, 1, tile), lambda g, t, *_: (g * tiles + t, 0, 0))

    node_f32 = sds((graphs, latent, nodes), F32)
    node_bf = sds((graphs, latent, nodes), BF)
    node_row_f32 = sds((graphs, 1, nodes), F32)
    edge_f32 = sds((graphs * tiles, latent, tile), F32)
    edge_bf = sds((graphs * tiles, latent, tile), BF)
    edge_row_f32 = sds((graphs * tiles, 1, tile), F32)

    def vmem(shape, kind=F32):
        return pltpu.VMEM(shape, kind)

    weight_scratch = dict(
        wa=vmem((3 * latent, latent), BF),
        wb=vmem((latent, latent), BF),
        wbn=vmem((latent, latent), BF),
        wan=vmem((2 * latent, latent), BF),
        cols=vmem((latent, 16)),
        outer=vmem((latent, latent // 2), BF),
        u=vmem((2 * nodes + latent, tile), BF),
    )
    forward_scratch = dict(
        b_t=vmem((latent, latent), BF),
        pcat=vmem((latent, 2 * nodes + latent), BF),
        new_low=vmem((latent, tile), BF),
        agg=vmem((latent, nodes)),
    )
    edge_sums = dict(
        act=vmem((latent + 16, tile), BF),
        one=vmem((latent, tile), BF),
        two=vmem((latent, tile), BF),
        gh=vmem((latent, nodes)),
        gagg=vmem((latent, nodes), BF),
        q=vmem((latent, 2 * nodes)),
        d_first=vmem((3 * latent + 16, latent)),
        d_b=vmem((latent + 16, latent)),
        v_e=vmem((latent, 256)),
    )
    node_sums = dict(
        d_bn=vmem((latent, latent)),
        d_an=vmem((2 * latent, latent)),
        v_n=vmem((latent, 512)),
    )
    outer_sums = dict(d_outer=vmem((latent, latent // 2)))
    row_flops = 2 * latent * latent * graphs * edge_count
    prefetch = dict(ids=ids)

    zero = kernel_call(
        functools.partial(first_kernel, plan, tiles),
        "first",
        dict(
            pack=list(pack_first),
            src=(source_vertex, ids_spec),
            dst=(target_vertex, ids_spec),
            x_now=(x_now_t, x_spec),
            x_next=(x_next_t, x_spec),
            border=(border, border_spec),
            link=(link_t, link_spec),
        ),
        dict(
            h_out=(node_f32, node_spec),
            hb=(node_bf, node_spec),
            aggl=(node_bf, node_spec),
            zn=(node_bf, node_spec),
            xn=(node_bf, node_spec),
            ivn=(node_row_f32, node_row),
            z1=(edge_bf, edge_spec),
            xh=(edge_bf, edge_spec),
            iv=(edge_row_f32, edge_row),
            e_out=(edge_f32, edge_spec),
        ),
        dict(**weight_scratch, **forward_scratch, link8=vmem((8, tile)), h=vmem((latent, nodes))),
        grid=(graphs, tiles),
        prefetch=prefetch,
        cost=(row_flops * 8, 20_000_000),
    )

    last_at = graphs * tiles - 1

    def early_edge(p, g, t, *_):
        return (jnp.where(p == 0, g * tiles + t, last_at), 0, 0)

    def late_edge(p, g, t, *_):
        return (jnp.where(p == 2, g * tiles + t, 0), 0, 0)

    def early_node(p, g, t, *_):
        return (jnp.where(p == 0, g, graphs - 1), 0, 0)

    def late_node(p, g, t, *_):
        return (jnp.where(p == 2, g, 0), 0, 0)

    def late_x(p, g, t, *_):
        return (0, jnp.where(p == 2, g, 0))

    early_node_spec = pl.BlockSpec((1, latent, nodes), early_node)
    early_edge_spec = pl.BlockSpec((1, latent, tile), early_edge)
    late_node_spec = pl.BlockSpec((1, latent, nodes), late_node)
    tile_ids = pl.BlockSpec((graphs, tile), lambda p, g, t, *_: (0, t))
    late_x_spec = pl.BlockSpec((channels, nodes), late_x)
    blocks = (Block(plan, 0), Block(plan, 1), Block(plan, 2))

    def grad_outs(r):
        return [sds((blocks[r].total, latent), BF)] * plan.fsdp

    all_nodes = (graphs, latent, nodes)
    all_edges = (graphs * tiles, latent, tile)
    mid = kernel_call(
        functools.partial(middle_kernel, plan, blocks[2], graphs, tiles),
        "middle",
        dict(
            pack=list(pack_rest),
            src=(source_vertex, tile_ids),
            dst=(target_vertex, tile_ids),
            h_in=(zero.h_out, early_node_spec),
            e_in=(zero.e_out, early_edge_spec),
            x_now=(x_now_t, late_x_spec),
            x_next=(x_next_t, late_x_spec),
            border=(border, pl.BlockSpec((1, nodes), late_x)),
            level=level,
            stats=stats,
        ),
        dict(
            hb=(node_bf, early_node_spec),
            z1=(edge_bf, early_edge_spec),
            xh=(edge_bf, early_edge_spec),
            iv=(edge_row_f32, pl.BlockSpec((1, 1, tile), early_edge)),
            grad=grad_outs(2),
            gh_out=(node_f32, late_node_spec),
            gagg_out=(node_bf, late_node_spec),
            ge_out=(edge_f32, pl.BlockSpec((1, latent, tile), late_edge)),
            count_out=(sds((1, 1), F32), sm),
        ),
        dict(
            **weight_scratch,
            **forward_scratch,
            **edge_sums,
            **node_sums,
            **outer_sums,
            loss=vmem((8, 128)),
            hb1=vmem(all_nodes, BF),
            aggl1=vmem(all_nodes, BF),
            zn1=vmem(all_nodes),
            xn1=vmem(all_nodes),
            ivn1=vmem((graphs, 1, nodes)),
            wan1=vmem((2 * latent, latent), BF),
            wbn1=vmem((latent, latent), BF),
            cols1=vmem((latent, 16)),
            d_bn1=vmem((latent, latent)),
            d_an1=vmem((2 * latent, latent)),
            v_n1=vmem((latent, 512)),
            hb2=vmem(all_nodes, BF),
            aggl2=vmem(all_nodes, BF),
            zn2=vmem(all_nodes),
            xn2=vmem(all_nodes),
            ivn2=vmem((graphs, 1, nodes)),
            h_all=vmem(all_nodes),
            e_all=vmem(all_edges),
            low2=vmem((graphs * tiles, latent + 16, tile), BF),
            z12=vmem(all_edges, BF),
            xh2=vmem(all_edges, BF),
            iv2=vmem((graphs * tiles, 1, tile)),
            aux=vmem((channels, 256)),
        ),
        grid=(3, graphs, tiles),
        prefetch=dict(ids=ids, counts=node_counts),
        cost=(row_flops * 27, 40_000_000),
    )
    anywhere = pl.BlockSpec(memory_space=pl.ANY)

    def back(r, places, kept, grads, other):
        first = r == 0
        count = len(places)
        node_shape = (count, latent, nodes)
        edge_shape = (count * tiles, latent, tile)

        def any_of(**group):
            return {n: (v, anywhere) for n, v in group.items()}

        ins = dict(
            pack_in=[(v, anywhere) for v in (pack_first if first else pack_rest)],
            src=source_vertex,
            dst=target_vertex,
            **any_of(hb_in=kept.hb, z1_in=kept.z1, xh_in=kept.xh, iv_in=kept.iv),
            **any_of(gh_in=grads.gh_out, gagg_in=grads.gagg_out, ge_in=grads.ge_out),
        )
        outs = dict(grad=grad_outs(r))
        scratch = dict(
            pack=vmem((plan.fsdp, plan.total, latent), BF),
            wa=vmem((3 * latent, latent), BF),
            wb=vmem((latent, latent), BF),
            cols=vmem((latent, 16)),
            u=vmem((2 * nodes, tile), BF),
            low_e=vmem((latent + 16, tile), BF),
            **edge_sums,
            z1=vmem(edge_shape, BF),
            xh=vmem(edge_shape, BF),
            iv=vmem((count * tiles, 1, tile)),
            ge=vmem(edge_shape),
            hb=vmem(node_shape, BF),
            gh_all=vmem(node_shape),
            gagg_all=vmem(node_shape, BF),
            sems=pltpu.SemaphoreType.DMA((6 + count * tiles, 8)),
        )
        if first:
            (g,) = places
            ins.update(
                x_now=(x_now_t, pl.BlockSpec((channels, nodes), lambda *_: (0, g))),
                x_next=(x_next_t, pl.BlockSpec((channels, nodes), lambda *_: (0, g))),
                border=(border, pl.BlockSpec((1, nodes), lambda *_: (0, g))),
                link=(link_t, pl.BlockSpec((1, 4, edge_count), lambda *_: (g, 0, 0))),
            )
            if other is not None:
                ins.update(other=list(other.grad))
            scratch.update(**outer_sums, d_ee=vmem((latent, 8)), link8=vmem((8, tile)))
            scratch.update(ge_low=vmem((latent, tile), BF))
        else:
            ins.update(before_in=[(v, anywhere) for v in pack_first])
            ins.update(any_of(e_in=zero.e_out, hb0_in=zero.hb, aggl_in=zero.aggl))
            ins.update(any_of(zn_in=zero.zn, xn_in=zero.xn, ivn_in=zero.ivn))
            outs.update(
                gh_out=sds(node_shape, F32), gagg_out=sds(node_shape, BF), ge_out=(sds(edge_shape, F32), anywhere)
            )
            scratch.update(
                **node_sums,
                before=vmem((plan.fsdp, plan.total, latent), BF),
                e=vmem(edge_shape),
                hb0=vmem(node_shape, BF),
                aggl=vmem(node_shape, BF),
                zn=vmem(node_shape, BF),
                xn=vmem(node_shape, BF),
                ivn=vmem((count, 1, nodes)),
                wbn=vmem((latent, latent), BF),
                wan=vmem((2 * latent, latent), BF),
                cols1=vmem((latent, 16)),
            )
        return kernel_call(
            functools.partial(back_kernel, plan, blocks[r], first, places, tiles),
            f"back{r}_{places[0]}",
            ins,
            outs,
            scratch,
            grid=(1,),
            prefetch=prefetch,
            cost=(row_flops * 11 * count // graphs, 15_000_000 * count),
        )

    def total_of(parts):
        total = parts[0].astype(F32)
        for part in parts[1:]:
            total = total + part.astype(F32)
        return total

    def exchange_grads(bag):
        return exchange(bag.grad, "fsdp", plan.fsdp)

    def owned(got, r):
        return total_of(got).astype(BF).reshape(plan.dp, blocks[r].piece, latent)

    def reduce_owner(value):
        return lax.all_to_all(value, "dp", 0, 0, tiled=True)

    def share(parts):
        total = jnp.sum(parts.astype(F32), axis=0)
        wide = jnp.broadcast_to(total[None], (plan.dp, *total.shape))
        return lax.all_to_all(wide, "dp", 0, 0, tiled=True)

    def after(bag, *others):
        bag.grad, held = lax.optimization_barrier((bag.grad, others))
        return held

    got2 = exchange_grads(mid)
    one = back(1, tuple(range(graphs)), mid, mid, None)
    owned2 = owned(got2, 2)
    (owned2,) = after(one, owned2)
    got1 = exchange_grads(one)
    last = None
    for g in range(graphs):
        last = back(0, (g,), zero, one, last)
        if g == 0:
            both = jnp.concatenate([owned2, owned(got1, 1)], axis=1)
            (both,) = after(last, both)
            parts = reduce_owner(both)
    (parts,) = after(last, parts)
    got0 = exchange_grads(last)
    shared = share(parts)
    cut = kernel_call(
        functools.partial(owner_sum_kernel, plan, blocks[0]),
        "owner_sum",
        dict(got=got0),
        dict(parts=[sds((blocks[0].piece, latent), BF)] * plan.dp),
        dict(total=vmem((blocks[0].total, latent))),
        prefetch=prefetch,
        cost=(1000, 1_000_000),
    )
    total0, shared = lax.optimization_barrier((total_of(exchange(cut.parts, "dp", plan.dp)), shared))
    pieces = spread_direct(total0, "dp", plan.dp)

    def turned(group):
        return (group[0].T, *group[1:])

    weights, moments, squares = turned(weights), turned(moments), turned(squares)
    numbers = (2, 3, 4, 5, 6)

    def products(numbers):
        return [sds(weights[k].shape, F32) for k in numbers for _ in range(3)]

    early = kernel_call(
        functools.partial(update_early_kernel, plan, blocks, numbers),
        "update_early",
        dict(
            shared=shared,
            weight=[weights[k] for k in numbers],
            moment=[moments[k] for k in numbers],
            square=[squares[k] for k in numbers],
        ),
        dict(products=products(numbers), loss=(sds((1, 1), F32), sm)),
        dict(grads2=vmem((blocks[2].total, latent)), grads1=vmem((blocks[1].total, latent))),
        cost=(1000, 9_000_000),
    )

    def slot(value):
        shape = value.shape
        cut = (1, 1, *shape[2:]) if len(shape) == 4 else (1, *shape[1:])
        return value, pl.BlockSpec(cut, lambda *_: (0,) * len(shape))

    partial = (2, 3, 5)
    alone = (0, 1)
    held = [early.products[3 * numbers.index(k) + i] for k in partial for i in range(3)]

    def pick(group):
        return [group[k] for k in alone] + [slot(group[k]) for k in partial]

    late = kernel_call(
        functools.partial(update_late_kernel, plan, blocks[0], alone + partial),
        "update_late",
        dict(
            pieces=pieces,
            weight=pick(weights),
            moment=pick(moments),
            square=pick(squares),
            held=[(v, anywhere) for v in held],
        ),
        dict(products=products(alone), slots=[slot(v) for v in products(partial)]),
        dict(grads=vmem((blocks[0].total, latent))),
        grid=(1,),
        prefetch=prefetch,
        cost=(1000, 1_000_000),
        alias=("held", "slots"),
    )
    new = [None] * 7
    for k in numbers:
        new[k] = early.products[3 * numbers.index(k) :][:3]
    for k, v in enumerate(alone + partial):
        new[v] = (late.products + late.slots)[3 * k : 3 * k + 3]
    results = [v.T for v in new[0]]
    for k in range(1, 7):
        results += new[k]
    return (early.loss.reshape(()), mid.count_out.reshape(()), *results)


def solution(mesh):
    rows = P(("dp", "fsdp"), None)
    row = P(("dp", "fsdp"))
    weight_specs = (
        P(None, "fsdp"),
        P(None, "fsdp"),
        P(None, "fsdp", None),
        P(None, None, "fsdp", None),
        P(None, "fsdp", None),
        P(None, None, None, "fsdp"),
        P("fsdp", None),
    )
    placed = (rows, rows, row, row, rows, rows, P(("dp", "fsdp"), None, None), P(), *weight_specs * 3)
    out_specs = [P(), P()]
    for spec in weight_specs:
        out_specs += [spec] * 3

    def step(*args):
        plan = Plan(args[10].shape[2], mesh.shape["dp"], mesh.shape["fsdp"])
        return body(plan, *args)

    return jax.shard_map(
        step, mesh=mesh, in_specs=placed, out_specs=tuple(out_specs), check_vma=False
    )
```

```python
import functools

import jax
import jax.numpy as jnp
from jax import lax
from jax.experimental import pallas as pl
from jax.experimental.pallas import tpu as pltpu
from jax.sharding import PartitionSpec as P

VARS = 6
LEVELS = 13
ROUNDS = 3
STEP = 10

norm_eps = 1e-05
stat_eps = 1e-06
beta_one = 0.9
beta_two = 0.999
adam_eps = 1e-08
decay_rate = 0.01
rate_matrix = 0.03
rate_vector = 0.2

EDGE_FIRST, EDGE_SECOND, NODE_FIRST, NODE_SECOND, ROWS, OUTER = range(6)

BF = jnp.bfloat16
F32 = jnp.float32
VMEM_LIMIT = 56 * 1024 * 1024
EDGE_TILE = 1536
CHUNK = 256


def contract(a, b, da, db):
    return lax.dot_general(a, b, (((da,), (db,)), ((), ())), preferred_element_type=F32)


def nn(a, b):
    return contract(a, b, 1, 0)


def nt(a, b):
    return contract(a, b, 1, 1)


def tn(a, b):
    return contract(a, b, 0, 0)


def sigmoid(v):
    return 0.5 * jnp.tanh(0.5 * v) + 0.5


def silu(v):
    half = 0.5 * v
    return half * jnp.tanh(half) + half


def round_up(v, m):
    return (v + m - 1) // m * m


def stacked(sizes):
    offset = 0
    at = {}
    for name, size in sizes:
        at[name] = (offset, size)
        offset += size
    return at, offset


class Plan:
    def __init__(self, latent, dp_size, fsdp_size):
        self.latent = latent
        self.dp = dp_size
        self.fsdp = fsdp_size
        self.width = latent // fsdp_size
        self.half = self.width // 2
        width = self.width
        sizes = (
            (EDGE_FIRST, 3 * width),
            (EDGE_SECOND, width),
            (NODE_SECOND, width),
            (NODE_FIRST, 2 * width),
            (ROWS, 16),
            (OUTER, self.half),
        )
        self.at, self.total = stacked(sizes)


class Block:
    def __init__(self, plan, node_parts):
        width = plan.width
        sizes = [(EDGE_FIRST, 3 * width), (EDGE_SECOND, width), (ROWS, 16), (OUTER, plan.half)]
        for k in range(node_parts):
            sizes += [((NODE_FIRST, k), 2 * width), ((NODE_SECOND, k), width), ((ROWS, k), 16)]
        self.at, self.used = stacked(sizes)
        self.piece = round_up((self.used + plan.dp - 1) // plan.dp, 8)
        self.total = self.piece * plan.dp


def live_row(border, count):
    place = lax.broadcasted_iota(jnp.int32, border.shape, 1)
    return jnp.where((place < count) & (border != 1), 1.0, 0.0).astype(F32)


def group_matrix(rows, cols, flip):
    var = lax.broadcasted_iota(jnp.int32, (rows, cols), 1 if flip else 0)
    chan = lax.broadcasted_iota(jnp.int32, (rows, cols), 0 if flip else 1)
    inside = (chan >= var * LEVELS) & (chan < (var + 1) * LEVELS)
    return jnp.where(inside, 1.0, 0.0).astype(F32)


def exact(a, b):
    return lax.dot_general(
        a, b, (((1,), (0,)), ((), ())), precision=lax.Precision.HIGHEST, preferred_element_type=F32
    )


class Bag:
    pass


def kernel_call(kernel, name, ins, outs, scratch=None, grid=(), prefetch=None, cost=None, alias=None):
    scratch = scratch or {}
    prefetch = prefetch or {}
    whole = pl.BlockSpec(memory_space=pltpu.VMEM)

    def flat(group):
        return [(n, v) for n, vs in group.items() for v in (vs if isinstance(vs, list) else [vs])]

    def fill(groups, values):
        bag = Bag()
        at = 0
        for group in groups:
            for n, vs in group.items():
                count = len(vs) if isinstance(vs, list) else None
                if count is None:
                    setattr(bag, n, values[at])
                    at += 1
                else:
                    setattr(bag, n, list(values[at : at + count]))
                    at += count
        return bag

    def split(item):
        if isinstance(item, tuple):
            return item
        if not grid:
            return item, whole
        rank = len(item.shape)
        return item, pl.BlockSpec(item.shape, lambda *_: (0,) * rank)

    def run(*refs):
        kernel(fill((prefetch, ins, outs, scratch), refs))

    sources = [split(v) for _, v in flat(ins)]
    products = [split(v) for _, v in flat(outs)]
    aliases = {}
    if alias:
        first_in = [n for n, _ in flat(ins)].index(alias[0]) + len(prefetch)
        first_out = [n for n, _ in flat(outs)].index(alias[1])
        aliases = {first_in + k: first_out + k for k in range(len(ins[alias[0]]))}
    result = pl.pallas_call(
        run,
        out_shape=[v for v, _ in products],
        grid_spec=pltpu.PrefetchScalarGridSpec(
            num_scalar_prefetch=len(prefetch),
            grid=grid,
            in_specs=[spec for _, spec in sources],
            out_specs=[spec for _, spec in products],
            scratch_shapes=list(scratch.values()),
        ),
        compiler_params=pltpu.CompilerParams(vmem_limit_bytes=VMEM_LIMIT),
        input_output_aliases=aliases,
        cost_estimate=pl.CostEstimate(flops=cost[0], bytes_accessed=cost[1], transcendentals=0),
        name=name,
    )(*prefetch.values(), *[v for v, _ in sources])
    return fill((outs,), result)


def pack_round(plan, out, r, edge_first, second_layers, node_first, vectors, edge_encoder, outer):
    width = plan.width
    at = plan.at

    def put(name, value):
        start, size = at[name]
        out[start : start + size, :] = value.astype(BF)

    put(EDGE_FIRST, edge_first[r])
    put(EDGE_SECOND, second_layers[r, 0])
    put(NODE_SECOND, second_layers[r, 1])
    put(NODE_FIRST, node_first[r])
    rows = jnp.concatenate([vectors[r, 0], vectors[r, 1]], axis=0)
    if edge_encoder is None:
        low = jnp.zeros((8, width), F32)
    else:
        low = jnp.concatenate([edge_encoder[...], jnp.zeros((4, width), F32)], axis=0)
    rows = jnp.concatenate([rows, low], axis=0)
    rows = jnp.concatenate([rows, jnp.zeros((16, plan.latent - width), F32)], axis=1)
    put(ROWS, rows)
    start, size = at[OUTER]
    if outer is None:
        out[start : start + size, :] = jnp.zeros((size, plan.latent), BF)
    else:
        channels = outer.shape[1]
        wide = jnp.concatenate(
            [outer[...], jnp.zeros((width, plan.latent // 2 - channels), F32)], axis=1
        )
        put(OUTER, jnp.concatenate([wide[: plan.half], wide[plan.half :]], axis=1))


def pack_first_kernel(plan, b):
    pack_round(plan, b.pack, 0, b.ef, b.sl, b.nf, b.vec, b.ee, b.enc)


def merge_stats(stats):
    total = jnp.sum(stats, axis=0)
    count = total[:, 2:3]
    mean = total[:, 0:1] / (count * LEVELS)
    own_count = stats[:, :, 2:3] * LEVELS
    shift = stats[:, :, 0:1] / jnp.maximum(own_count, 1.0) - mean[None]
    spread = jnp.sum(stats[:, :, 1:2] + own_count * shift * shift, axis=0)
    return count, spread


def pack_rest_kernel(plan, graphs, b):
    pack_round(plan, b.pack.at[0], 1, b.ef, b.sl, b.nf, b.vec, None, None)
    pack_round(plan, b.pack.at[1], 2, b.ef, b.sl, b.nf, b.vec, None, b.dec)
    nodes = b.x_now.shape[1] // graphs
    channels = b.x_now.shape[0]
    lives = []
    for g in range(graphs):
        lives.append(live_row(b.border[:, g * nodes : (g + 1) * nodes], b.counts[g]))
    live = jnp.concatenate(lives, axis=1)
    delta = b.x_next[...] - b.x_now[...]
    count = jnp.sum(live)
    sums = jnp.sum(delta * live, axis=1, keepdims=True)
    to_var = group_matrix(8, channels, False)
    to_chan = group_matrix(channels, 8, True)
    var_sum = exact(to_var, jnp.broadcast_to(sums, (channels, 128)))
    mean = var_sum / (jnp.maximum(count, 1.0) * LEVELS)
    centered = (delta - exact(to_chan, mean)[:, 0:1]) * live
    square = jnp.sum(centered * centered, axis=1, keepdims=True)
    var_square = exact(to_var, jnp.broadcast_to(square, (channels, 128)))
    lane = lax.broadcasted_iota(jnp.int32, (8, 128), 1)
    value = jnp.where(lane == 0, var_sum, jnp.where(lane == 1, var_square, count))
    b.stats[...] = jnp.broadcast_to(value[None], b.stats.shape)


def assemble(plan, me, packs, edge_first=None, edge_second=None, node_second=None, node_first=None, cols=None, outer=None):
    width = plan.width
    latent = plan.latent
    total = jnp.zeros((latent, 16), F32)
    rowid = lax.broadcasted_iota(jnp.int32, (latent, width), 0)
    colid = lax.broadcasted_iota(jnp.int32, (latent, width), 1)
    for k, pack in enumerate(packs):
        owner = jnp.bitwise_xor(me, k)

        def put(ref, name, step):
            if ref is not None:
                start, size = plan.at[name]
                ref[pl.ds(pl.multiple_of(owner * step, 16), size), :] = pack[start : start + size, :]

        put(edge_first, EDGE_FIRST, 3 * width)
        put(edge_second, EDGE_SECOND, width)
        put(node_second, NODE_SECOND, width)
        put(node_first, NODE_FIRST, 2 * width)
        start, size = plan.at[ROWS]
        place = jnp.where(rowid == owner * width + colid, 1.0, 0.0).astype(BF)
        total = total + nt(place, pack[start : start + size, 0:width])
        if outer is not None:
            start, size = plan.at[OUTER]
            half = latent // 2
            first = pl.multiple_of(owner * width, 16)
            second = pl.multiple_of(owner * width + plan.half, 16)
            outer[pl.ds(first, size), :] = pack[start : start + size, 0:half]
            outer[pl.ds(second, size), :] = pack[start : start + size, half : 2 * half]
    cols[...] = total


def assemble_all(plan, b, packs, outer):
    assemble(plan, b.ids[0], packs, b.wa, b.wb, b.wbn, b.wan, b.cols, b.outer if outer else None)


def turn_weights(plan, b, nodes):
    latent = plan.latent
    b.b_t[...] = b.wb[...].astype(F32).T.astype(BF)
    b.pcat[:, 2 * nodes :] = b.wa[2 * latent :, :].astype(F32).T.astype(BF)


def fill_tables(u_ref, src, dst, nodes, lanes):
    count = lanes.stop - lanes.start
    place = lax.broadcasted_iota(jnp.int32, (nodes, count), 0).astype(jnp.int16)
    one = jnp.ones((nodes, count), BF)
    zero = jnp.zeros((nodes, count), BF)
    u_ref[0:nodes, lanes] = jnp.where(place == src[:, lanes].astype(jnp.int16), one, zero)
    u_ref[nodes : 2 * nodes, lanes] = jnp.where(place == dst[:, lanes].astype(jnp.int16), one, zero)


def skew(chunks):
    live = []
    waiting = list(chunks)
    while live or waiting:
        if waiting:
            live.append(waiting.pop(0))
        for item in list(reversed(live)):
            if next(item, 1) == 1:
                live.remove(item)


def norm_forward(z2, count):
    mean = jnp.sum(z2, axis=0, keepdims=True) * (1.0 / count)
    centered = z2 - mean
    var = jnp.sum(centered * centered, axis=0, keepdims=True) * (1.0 / count)
    inverse = lax.rsqrt(var + norm_eps)
    return centered * inverse, inverse


def forward_nodes_in(plan, b, state):
    latent = plan.latent
    nodes = state.shape[-1]
    low = state.astype(BF)
    b.pcat[:, 0:nodes] = tn(b.wa[0:latent, :], low).astype(BF)
    b.pcat[:, nodes : 2 * nodes] = tn(b.wa[latent : 2 * latent, :], low).astype(BF)
    b.agg[...] = jnp.zeros_like(b.agg)
    return low


def forward_edges(plan, b, src, dst, tile, get, put, kept):
    nodes = b.agg.shape[-1]
    z1_ref, xh_ref, iv_ref = kept

    def chunk(at):
        lanes = slice(at, at + CHUNK)
        fill_tables(b.u, src, dst, nodes, lanes)
        b.u[2 * nodes :, lanes] = get(lanes).astype(BF)
        yield
        z1 = nn(b.pcat[...], b.u[:, lanes])
        yield
        z1 = z1 + b.cols[:, 0:1]
        active = silu(z1).astype(BF)
        z1_ref[:, lanes] = z1.astype(BF)
        yield
        z2 = nn(b.b_t[...], active)
        yield
        z2 = z2 + b.cols[:, 1:2]
        normed, inverse = norm_forward(z2, plan.latent)
        xh_ref[:, lanes] = normed.astype(BF)
        iv_ref[:, lanes] = inverse
        e = get(lanes) + (normed * b.cols[:, 2:3] + b.cols[:, 3:4])
        if put is not None:
            put(lanes, e)
        b.new_low[:, lanes] = e.astype(BF)
        yield

    skew([chunk(at) for at in range(0, tile, CHUNK)])
    b.agg[...] += nt(b.new_low[...], b.u[nodes : 2 * nodes, :])


def forward_nodes_out(plan, b, state, low):
    latent = plan.latent
    arriving = b.agg[...].astype(BF)
    z1 = tn(b.wan[0:latent, :], low) + tn(b.wan[latent:, :], arriving) + b.cols[:, 4:5]
    active = silu(z1).astype(BF)
    z2 = tn(b.wbn[...], active) + b.cols[:, 5:6]
    normed, inverse = norm_forward(z2, latent)
    return arriving, z1, normed, inverse, state + (normed * b.cols[:, 6:7] + b.cols[:, 7:8])


def norm_backward(grad, gain, normed, inverse, count):
    scaled = grad * gain
    mean = jnp.sum(scaled, axis=0, keepdims=True) * (1.0 / count)
    cross = jnp.sum(scaled * normed, axis=0, keepdims=True) * (1.0 / count)
    return (inverse * (scaled - mean - normed * cross)).astype(BF)


def lane_sum(value):
    total = value[:, 0:128]
    for k in range(1, value.shape[1] // 128):
        total = total + value[:, 128 * k : 128 * (k + 1)]
    return total


def backward_reset(plan, b, tile, refs):
    for ref in refs:
        ref[...] = jnp.zeros_like(ref)
    b.act[plan.latent :, :] = jnp.ones((16, tile), BF)


def backward_nodes_in(plan, weights, sums, grad, low_h, arriving, z1, normed, inverse):
    latent = plan.latent
    wan, wbn, cols = weights
    z1 = z1.astype(F32)
    normed = normed.astype(F32)
    d_an, d_bn, v_n = sums
    v_n[:, 0:128] += lane_sum(grad * normed)
    v_n[:, 128:256] += lane_sum(grad)
    low_two = norm_backward(grad, cols[:, 6:7], normed, inverse, latent)
    gate = sigmoid(z1)
    soft = z1 * gate
    d_bn[...] += nt(soft.astype(BF), low_two)
    d_active = nn(wbn[...], low_two)
    low_one = (d_active * (soft - soft * gate + gate)).astype(BF)
    v_n[:, 256:384] += lane_sum(low_one.astype(F32))
    v_n[:, 384:512] += lane_sum(low_two.astype(F32))
    d_an[0:latent, :] += nt(low_h, low_one)
    d_an[latent:, :] += nt(arriving, low_one)
    return grad + nn(wan[0:latent, :], low_one), nn(wan[latent:, :], low_one).astype(BF)


def backward_edges(plan, b, src, dst, tile, get, kept, low_e, put):
    z1_ref, xh_ref, iv_ref = kept
    latent = plan.latent
    nodes = b.gagg.shape[-1]

    def chunk(at):
        lanes = slice(at, at + CHUNK)
        fill_tables(b.u, src, dst, nodes, lanes)
        yield
        ge = nn(b.gagg[...], b.u[nodes : 2 * nodes, lanes])
        yield
        if get is not None:
            ge = ge + get(lanes)
        normed = xh_ref[:, lanes].astype(F32)
        b.v_e[:, 0:128] += lane_sum(ge * normed)
        b.v_e[:, 128:256] += lane_sum(ge)
        low_two = norm_backward(ge, b.cols[:, 2:3], normed, iv_ref[:, lanes], latent)
        b.two[:, lanes] = low_two
        yield
        d_active = nn(b.wb[...], low_two)
        yield
        z1 = z1_ref[:, lanes].astype(F32)
        gate = sigmoid(z1)
        soft = z1 * gate
        b.act[0:latent, lanes] = soft.astype(BF)
        low_one = (d_active * (soft - soft * gate + gate)).astype(BF)
        b.one[:, lanes] = low_one
        yield
        put(lanes, ge + nn(b.wa[2 * latent :, :], low_one))
        yield

    skew([chunk(at) for at in range(0, tile, CHUNK)])
    b.d_b[...] += nt(b.act[...], b.two[...])
    b.d_first[2 * latent :, :] += nt(low_e[...], b.one[...])
    b.q[...] += nt(b.one[...], b.u[0 : 2 * nodes, :])


def backward_nodes_out(plan, b, low_h):
    latent = plan.latent
    nodes = b.gagg.shape[-1]
    total = b.gh[...]
    for side in range(2):
        sums = b.q[:, side * nodes : (side + 1) * nodes]
        high = sums.astype(BF)
        rest = (sums - high.astype(F32)).astype(BF)
        rows = slice(side * latent, (side + 1) * latent)
        b.d_first[rows, :] += nt(low_h, high) + nt(low_h, rest)
        total = total + nn(b.wa[rows, :], high) + nn(b.wa[rows, :], rest)
    return total


def row_of(cols128):
    return jnp.sum(cols128.T, axis=0, keepdims=True)


def backward_emit(plan, block, b, low, outer, node_sums, before):
    latent = plan.latent
    width = plan.width
    rows = [
        b.d_first[3 * latent : 3 * latent + 1, :],
        b.d_b[latent : latent + 1, :],
        row_of(b.v_e[:, 0:128]),
        row_of(b.v_e[:, 128:256]),
        jnp.zeros((4, latent), F32),
        jnp.zeros((8, latent), F32) if low is None else low,
    ]
    groups = [(ROWS, jnp.concatenate(rows, axis=0).astype(BF))]
    for k, (_, _, v_n) in enumerate(node_sums):
        rows = [
            row_of(v_n[:, 256:384]),
            row_of(v_n[:, 384:512]),
            row_of(v_n[:, 0:128]),
            row_of(v_n[:, 128:256]),
            jnp.zeros((12, latent), F32),
        ]
        groups.append(((ROWS, k), jnp.concatenate(rows, axis=0).astype(BF)))
    rowid = lax.broadcasted_iota(jnp.int32, (latent, latent), 0)
    colid = lax.broadcasted_iota(jnp.int32, (latent, latent), 1)
    for k, out in enumerate(b.grad):
        owner = jnp.bitwise_xor(b.ids[0], k)

        def put(name, value):
            start, size = block.at[name]
            rows = slice(start, start + size)
            if before is not None:
                value = value + before[k][rows, :].astype(F32)
            out[rows, :] = value.astype(BF)

        def take(ref, step):
            return ref[pl.ds(pl.multiple_of(owner * step, 8), step), :]

        put(EDGE_FIRST, take(b.d_first, 3 * width))
        put(EDGE_SECOND, take(b.d_b, width))
        inside = (rowid == owner * width + colid) & (colid < width)
        place = jnp.where(inside, 1.0, 0.0).astype(BF)
        for name, value in groups:
            put(name, nn(value, place))
        if outer is not None:
            own = take(outer, width)
            put(OUTER, jnp.concatenate([own[: plan.half], own[plan.half :]], axis=1))
        else:
            put(OUTER, jnp.zeros((plan.half, latent), F32))
        for k2, (d_an, d_bn, _) in enumerate(node_sums):
            put((NODE_FIRST, k2), take(d_an, 2 * width))
            put((NODE_SECOND, k2), take(d_bn, width))
        if block.total > block.used:
            out[block.used :, :] = jnp.zeros((block.total - block.used, latent), BF)


def split_three(whole, lanes, period, place):
    high = whole.astype(BF).astype(F32)
    mid = (whole - high).astype(BF).astype(F32)
    rest = whole - high - mid
    lane = lax.broadcasted_iota(jnp.int32, (8, lanes), 1) % period - 3 * place
    top = lax.broadcasted_iota(jnp.int32, (8, lanes), 0) == 0
    value = jnp.where(lane == 0, high, jnp.where(lane == 1, mid, jnp.where(lane == 2, rest, 0.0)))
    return jnp.where(top, value, 0.0)


def first_kernel(plan, tiles, b):
    g = pl.program_id(0)
    t = pl.program_id(1)
    nodes = b.h_out.shape[-1]
    tile = b.z1.shape[-1]

    @pl.when((g == 0) & (t == 0))
    def _():
        assemble_all(plan, b, b.pack, True)
        turn_weights(plan, b, nodes)
        b.link8[...] = jnp.zeros_like(b.link8)

    @pl.when(t == 0)
    def _():
        chosen = jnp.where(b.border[...] == 1, b.x_next[...], b.x_now[...]).astype(BF)
        b.h[...] = nn(b.outer[:, 0 : b.x_now.shape[0]], chosen)
        b.hb[0] = forward_nodes_in(plan, b, b.h[...])

    b.link8[0:4, :] = b.link[0]

    def get(lanes):
        return nn(b.cols[:, 8:16].astype(BF), b.link8[:, lanes].astype(BF))

    def put(lanes, value):
        b.e_out[0, :, lanes] = value

    kept = (b.z1.at[0], b.xh.at[0], b.iv.at[0])
    forward_edges(plan, b, b.src[pl.ds(g, 1), :], b.dst[pl.ds(g, 1), :], tile, get, put, kept)

    @pl.when(t == tiles - 1)
    def _():
        state = b.h[...]
        b.aggl[0], z1, normed, b.ivn[0], b.h_out[0] = forward_nodes_out(plan, b, state, state.astype(BF))
        b.zn[0] = z1.astype(BF)
        b.xn[0] = normed.astype(BF)


def middle_kernel(plan, block, graphs, tiles, b):
    p = pl.program_id(0)
    g = pl.program_id(1)
    t = pl.program_id(2)
    nodes = b.gh_out.shape[-1]
    tile = b.z1.shape[-1]
    latent = plan.latent
    channels = b.x_now.shape[0]
    at = g * tiles + t
    start = (g == 0) & (t == 0)
    src = b.src[pl.ds(g, 1), :]
    dst = b.dst[pl.ds(g, 1), :]

    @pl.when((p == 0) & start)
    def _():
        assemble_all(plan, b, [r.at[0] for r in b.pack], False)
        turn_weights(plan, b, nodes)
        b.wan1[...] = b.wan[...]
        b.wbn1[...] = b.wbn[...]
        b.cols1[...] = b.cols[...]
        refs = (b.d_first, b.d_b, b.v_e, b.d_bn, b.d_an, b.v_n, b.d_bn1, b.d_an1, b.v_n1, b.d_outer, b.loss)
        backward_reset(plan, b, tile, refs)
        count, spread = merge_stats(b.stats[...])
        scale = lax.rsqrt(spread / (count * LEVELS) + stat_eps)
        b.aux[:, 0:128] = exact(group_matrix(channels, 8, True), jnp.broadcast_to(scale, (8, 128)))
        b.aux[:, 128:256] = jnp.broadcast_to(count[0:1] * channels, (channels, 128))
        b.count_out[0, 0] = jnp.sum(count[0:1]) * channels

    @pl.when((p == 1) & start)
    def _():
        assemble_all(plan, b, [r.at[1] for r in b.pack], True)
        turn_weights(plan, b, nodes)

    @pl.when((p == 0) & (t == 0))
    def _():
        b.hb[0] = forward_nodes_in(plan, b, b.h_in[0])

    @pl.when(p == 0)
    def _():
        def get(lanes):
            return b.e_in[0, :, lanes]

        def put(lanes, value):
            b.e_all[at, :, lanes] = value

        forward_edges(plan, b, src, dst, tile, get, put, (b.z1.at[0], b.xh.at[0], b.iv.at[0]))

    @pl.when((p == 0) & (t == tiles - 1))
    def _():
        state = b.h_in[0]
        b.hb1[g] = state.astype(BF)
        b.aggl1[g], b.zn1[g], b.xn1[g], b.ivn1[g], b.h_all[g] = forward_nodes_out(plan, b, state, b.hb1[g])

    @pl.when((p == 1) & (t == 0))
    def _():
        b.hb2[g] = forward_nodes_in(plan, b, b.h_all[g])

    @pl.when(p == 1)
    def _():
        b.low2[at, latent:, :] = jnp.ones((16, tile), BF)

        def get(lanes):
            return b.e_all[at, :, lanes]

        forward_edges(plan, b, src, dst, tile, get, None, (b.z12.at[at], b.xh2.at[at], b.iv2.at[at]))
        b.low2[at, 0:latent, :] = b.u[2 * nodes :, :]

    @pl.when((p == 1) & (t == tiles - 1))
    def _():
        b.aggl2[g], b.zn2[g], b.xn2[g], b.ivn2[g], b.h_all[g] = forward_nodes_out(
            plan, b, b.h_all[g], b.hb2[g]
        )

    @pl.when((p == 2) & (t == 0))
    def _():
        final_low = b.h_all[g].astype(BF)
        delta = b.x_next[...] - b.x_now[...]
        scale = b.aux[:, 0:1]
        norm_count = b.aux[:, 128:129]
        predicted = tn(b.outer[...], final_low)[0:channels]
        misfit = (predicted - delta) * scale
        weighting = (b.level[...].astype(F32) + 1.0) / LEVELS * live_row(b.border[...], b.counts[g])
        b.loss[...] += jnp.broadcast_to(jnp.sum(weighting * misfit * misfit), b.loss.shape)
        grad_pred = (2.0 * weighting * misfit * scale / norm_count).astype(BF)
        b.d_outer[:, 0:channels] += nt(final_low, grad_pred)
        grad = nn(b.outer[:, 0:channels], grad_pred)
        b.gh[...], b.gagg[...] = backward_nodes_in(
            plan,
            (b.wan, b.wbn, b.cols),
            (b.d_an, b.d_bn, b.v_n),
            grad,
            b.hb2[g],
            b.aggl2[g],
            b.zn2[g],
            b.xn2[g],
            b.ivn2[g],
        )
        b.q[...] = jnp.zeros_like(b.q)

    @pl.when(p == 2)
    def _():
        def put(lanes, value):
            b.ge_out[0, :, lanes] = value

        kept = (b.z12.at[at], b.xh2.at[at], b.iv2.at[at])
        backward_edges(plan, b, src, dst, tile, None, kept, b.low2.at[at], put)

    @pl.when((p == 2) & (t == tiles - 1))
    def _():
        grad = backward_nodes_out(plan, b, b.hb2[g])
        b.gh_out[0], b.gagg_out[0] = backward_nodes_in(
            plan,
            (b.wan1, b.wbn1, b.cols1),
            (b.d_an1, b.d_bn1, b.v_n1),
            grad,
            b.hb1[g],
            b.aggl1[g],
            b.zn1[g],
            b.xn1[g],
            b.ivn1[g],
        )

    @pl.when((p == 2) & (g == graphs - 1) & (t == tiles - 1))
    def _():
        low = split_three(b.loss[0:1, 0:1], latent, plan.width, b.ids[0])
        sums = ((b.d_an, b.d_bn, b.v_n), (b.d_an1, b.d_bn1, b.v_n1))
        backward_emit(plan, block, b, low, b.d_outer, sums, None)


def back_kernel(plan, block, first, places, tiles, b):
    tile = b.u.shape[-1]
    latent = plan.latent

    def copies(pairs, row):
        return [pltpu.make_async_copy(x, y, b.sems.at[row, k]) for k, (x, y) in enumerate(pairs)]

    picked = b.pack_in if first else [r.at[0] for r in b.pack_in]
    weights = copies([(x, b.pack.at[k]) for k, x in enumerate(picked)], 0)
    early = []
    late = []
    moves = []
    ends = []
    for k, g in enumerate(places):
        own = g if b.gh_in.shape[0] > 1 else 0
        pairs = [(b.gagg_in.at[own], b.gagg_all.at[k]), (b.gh_in.at[own], b.gh_all.at[k])]
        early.append(copies(pairs, 1 + k))
        pairs = [(b.hb_in.at[g], b.hb.at[k])]
        if not first:
            nodes_in = ((b.hb0_in, b.hb0), (b.aggl_in, b.aggl), (b.zn_in, b.zn), (b.xn_in, b.xn), (b.ivn_in, b.ivn))
            pairs += [(x.at[g], y.at[k]) for x, y in nodes_in]
        late.append(copies(pairs, 3 + k))
        for t in range(tiles):
            at = k * tiles + t
            place = g * tiles + t
            source = place if b.ge_in.shape[0] > tiles else t
            pairs = [(b.z1_in.at[place], b.z1.at[at]), (b.xh_in.at[place], b.xh.at[at])]
            pairs += [(b.iv_in.at[place], b.iv.at[at]), (b.ge_in.at[source], b.ge.at[at])]
            if not first:
                pairs.append((b.e_in.at[place], b.e.at[at]))
                ends.append(pltpu.make_async_copy(b.ge.at[at], b.ge_out.at[at], b.sems.at[5 + at, 6]))
            moves.append(copies(pairs, 5 + at))
    rest = [] if first else copies([(x, b.before.at[k]) for k, x in enumerate(b.before_in)], 5 + len(moves))
    for group in (weights, early[0], moves[0], *moves[1:], *early[1:], *late, rest):
        for copy in group:
            copy.start()

    def wait(group):
        for copy in group:
            copy.wait()

    sums = [b.d_first, b.d_b, b.v_e]
    sums += [b.d_outer, b.d_ee, b.link8] if first else [b.d_bn, b.d_an, b.v_n]
    backward_reset(plan, b, tile, sums)
    b.low_e[latent:, :] = jnp.ones((16, tile), BF)
    wait(weights)
    assemble(plan, b.ids[0], [b.pack.at[k] for k in range(plan.fsdp)], b.wa, b.wb, cols=b.cols)
    for k, g in enumerate(places):
        wait(early[k])
        b.gagg[...] = b.gagg_all[k]
        b.gh[...] = b.gh_all[k]
        b.q[...] = jnp.zeros_like(b.q)
        for t in range(tiles):
            at = k * tiles + t
            wait(moves[at])
            lanes = slice(t * tile, (t + 1) * tile)
            kept = (b.z1.at[at], b.xh.at[at], b.iv.at[at])

            def get(lanes, at=at):
                return b.ge[at, :, lanes]

            if first:
                b.link8[0:4, :] = b.link[k, :, lanes]
                b.low_e[0:latent, :] = nn(b.cols[:, 8:16].astype(BF), b.link8[...].astype(BF)).astype(BF)

                def put(lanes, value):
                    b.ge_low[:, lanes] = value.astype(BF)
            else:
                b.low_e[0:latent, :] = b.e[at].astype(BF)

                def put(lanes, value, at=at):
                    b.ge[at, :, lanes] = value

            src = b.src[g : g + 1, lanes]
            dst = b.dst[g : g + 1, lanes]
            backward_edges(plan, b, src, dst, tile, get, kept, b.low_e, put)
            if first:
                b.d_ee[...] += nt(b.ge_low[...], b.link8[...].astype(BF))
            else:
                ends[at].start()
        wait(late[k])
        total = backward_nodes_out(plan, b, b.hb[k])
        if first:
            chosen = jnp.where(b.border[...] == 1, b.x_next[...], b.x_now[...]).astype(BF)
            b.d_outer[:, 0 : b.x_now.shape[0]] += nt(total.astype(BF), chosen)
        else:
            if k == 0:
                wait(rest)
                packs = [b.before.at[k] for k in range(plan.fsdp)]
                assemble(plan, b.ids[0], packs, node_second=b.wbn, node_first=b.wan, cols=b.cols1)
            b.gh_out[k], b.gagg_out[k] = backward_nodes_in(
                plan,
                (b.wan, b.wbn, b.cols1),
                (b.d_an, b.d_bn, b.v_n),
                total,
                b.hb0[k],
                b.aggl[k],
                b.zn[k],
                b.xn[k],
                b.ivn[k],
            )
    if first:
        backward_emit(plan, block, b, b.d_ee[...].T, b.d_outer, (), b.other if places[0] > 0 else None)
    else:
        backward_emit(plan, block, b, None, None, ((b.d_an, b.d_bn, b.v_n),), None)
    wait(ends)


def adam_math(weight, moment, square, gradient, rate):
    moment_new = beta_one * moment + (1.0 - beta_one) * gradient
    square_new = beta_two * square + (1.0 - beta_two) * gradient * gradient
    direction = (
        moment_new
        * (1.0 / (1.0 - beta_one**STEP))
        / (jnp.sqrt(square_new * (1.0 / (1.0 - beta_two**STEP))) + adam_eps)
    )
    return (moment_new, square_new, weight - rate * (direction + decay_rate * weight))


def apply_update(b, k, index, gradient, rate):
    new = adam_math(b.weight[k][index], b.moment[k][index], b.square[k][index], gradient, rate)
    for ref, value in zip(b.new[k], new):
        ref[index] = value


def by_number(b, numbers, products):
    for group in (b.weight, b.moment, b.square):
        group[:] = [group[numbers.index(k)] if k in numbers else None for k in range(7)]
    b.new = [products[3 * numbers.index(k) : 3 * numbers.index(k) + 3] if k in numbers else None for k in range(7)]


def part_of(ref, block, name):
    start, size = block.at[name]
    return ref[start : start + size, :]


def update_edge(plan, b, ref, block, at):
    apply_update(b, 2, at, part_of(ref, block, EDGE_FIRST), rate_matrix)
    apply_update(b, 3, (at, 0), part_of(ref, block, EDGE_SECOND), rate_matrix)
    rows = part_of(ref, block, ROWS)
    apply_update(b, 5, (at, 0), rows[0:4, 0 : plan.width], rate_vector)
    half = plan.latent // 2
    wide = part_of(ref, block, OUTER)
    return rows, jnp.concatenate([wide[:, 0:half], wide[:, half:]], axis=0)


def update_early_kernel(plan, blocks, numbers, b):
    by_number(b, numbers, b.products)
    width = plan.width
    for source in range(plan.dp):
        for target, block, start in ((b.grads2, blocks[2], 0), (b.grads1, blocks[1], blocks[2].piece)):
            rows = slice(source * block.piece, (source + 1) * block.piece)
            target[rows, :] = b.shared[source, start : start + block.piece, :]
    rows, outer = update_edge(plan, b, b.grads2, blocks[2], 2)
    apply_update(b, 6, Ellipsis, outer[:, 0 : b.weight[6].shape[1]], rate_matrix)
    lane = lax.broadcasted_iota(jnp.int32, (1, plan.latent), 1)
    b.loss[0, 0] = jnp.sum(jnp.where(lane < width, rows[8:9, :], 0.0))
    update_edge(plan, b, b.grads1, blocks[1], 1)
    for r, ref, block, k in ((2, b.grads2, blocks[2], 0), (1, b.grads2, blocks[2], 1), (0, b.grads1, blocks[1], 0)):
        apply_update(b, 4, r, part_of(ref, block, (NODE_FIRST, k)), rate_matrix)
        apply_update(b, 3, (r, 1), part_of(ref, block, (NODE_SECOND, k)), rate_matrix)
        apply_update(b, 5, (r, 1), part_of(ref, block, (ROWS, k))[0:4, 0:width], rate_vector)


def update_late_kernel(plan, block, numbers, b):
    by_number(b, numbers, b.products + b.slots)
    rows, outer = update_edge(plan, b, b.grads, block, 0)
    apply_update(b, 0, Ellipsis, outer[:, 0 : b.weight[0].shape[1]], rate_matrix)
    apply_update(b, 1, Ellipsis, rows[8:12, 0 : plan.width], rate_matrix)


def body(plan, *args):
    x_now, x_next, node_counts, border_flag, source_vertex, target_vertex, link_features, level_ids = args[:8]
    weights = args[8:15]
    moments = args[15:22]
    squares = args[22:29]
    encoder, edge_encoder, edge_first, second_layers, node_first, vectors, decoder = weights
    graphs, edge_count = source_vertex.shape
    nodes = x_now.shape[0] // graphs
    channels = x_now.shape[1]
    latent = plan.latent
    tile = EDGE_TILE
    tiles = edge_count // tile
    x_now_t = x_now.T
    x_next_t = x_next.T
    border = border_flag.reshape(1, -1)
    link_t = jnp.transpose(link_features, (0, 2, 1))
    level = level_ids.reshape(-1, 1)
    ids = jnp.stack([lax.axis_index("fsdp"), lax.axis_index("dp")]).astype(jnp.int32)

    sm = pl.BlockSpec(memory_space=pltpu.SMEM)
    sds = jax.ShapeDtypeStruct
    pack_shape = sds((plan.total, latent), BF)
    devices = plan.dp * plan.fsdp

    def across(value, axis, size, mask):
        return lax.ppermute(value, axis, [(j, j ^ mask) for j in range(size)])

    def spread_chain(own, beside):
        got = [own]
        for k in range(1, plan.fsdp):
            source = got[k & (k - 1)]
            if k & (k - 1):
                source, _ = lax.optimization_barrier((source, beside))
            got.append(across(source, "fsdp", plan.fsdp, k & -k))
        return got

    def spread_direct(own, axis, size):
        return [own] + [across(own, axis, size, k) for k in range(1, size)]

    def exchange(parts, axis, size):
        return [parts[0]] + [across(parts[k], axis, size, k) for k in range(1, size)]

    raw = dict(ef=edge_first, sl=second_layers, nf=node_first, vec=vectors)
    start = kernel_call(
        functools.partial(pack_first_kernel, plan),
        "pack_first",
        dict(**raw, ee=edge_encoder, enc=encoder.T),
        dict(pack=pack_shape),
        cost=(1000, 3_000_000),
    )
    rest = kernel_call(
        functools.partial(pack_rest_kernel, plan, graphs),
        "pack_rest",
        dict(counts=(node_counts, sm), **raw, dec=decoder, x_now=x_now_t, x_next=x_next_t, border=border),
        dict(pack=sds((2, plan.total, latent), BF), stats=sds((devices, 8, 128), F32)),
        cost=(1000, 8_000_000),
    )
    pack_first = spread_chain(start.pack, rest.pack)
    pack_rest = spread_direct(rest.pack, "fsdp", plan.fsdp)
    stats = lax.all_to_all(rest.stats, ("dp", "fsdp"), 0, 0, tiled=True)

    ids_spec = pl.BlockSpec((graphs, tile), lambda g, t, *_: (0, t))
    x_spec = pl.BlockSpec((channels, nodes), lambda g, t, *_: (0, g))
    border_spec = pl.BlockSpec((1, nodes), lambda g, t, *_: (0, g))
    link_spec = pl.BlockSpec((1, 4, tile), lambda g, t, *_: (g, 0, t))
    node_spec = pl.BlockSpec((1, latent, nodes), lambda g, t, *_: (g, 0, 0))
    node_row = pl.BlockSpec((1, 1, nodes), lambda g, t, *_: (g, 0, 0))
    edge_spec = pl.BlockSpec((1, latent, tile), lambda g, t, *_: (g * tiles + t, 0, 0))
    edge_row = pl.BlockSpec((1, 1, tile), lambda g, t, *_: (g * tiles + t, 0, 0))

    node_f32 = sds((graphs, latent, nodes), F32)
    node_bf = sds((graphs, latent, nodes), BF)
    node_row_f32 = sds((graphs, 1, nodes), F32)
    edge_f32 = sds((graphs * tiles, latent, tile), F32)
    edge_bf = sds((graphs * tiles, latent, tile), BF)
    edge_row_f32 = sds((graphs * tiles, 1, tile), F32)

    def vmem(shape, kind=F32):
        return pltpu.VMEM(shape, kind)

    weight_scratch = dict(
        wa=vmem((3 * latent, latent), BF),
        wb=vmem((latent, latent), BF),
        wbn=vmem((latent, latent), BF),
        wan=vmem((2 * latent, latent), BF),
        cols=vmem((latent, 16)),
        outer=vmem((latent, latent // 2), BF),
        u=vmem((2 * nodes + latent, tile), BF),
    )
    forward_scratch = dict(
        b_t=vmem((latent, latent), BF),
        pcat=vmem((latent, 2 * nodes + latent), BF),
        new_low=vmem((latent, tile), BF),
        agg=vmem((latent, nodes)),
    )
    edge_sums = dict(
        act=vmem((latent + 16, tile), BF),
        one=vmem((latent, tile), BF),
        two=vmem((latent, tile), BF),
        gh=vmem((latent, nodes)),
        gagg=vmem((latent, nodes), BF),
        q=vmem((latent, 2 * nodes)),
        d_first=vmem((3 * latent + 16, latent)),
        d_b=vmem((latent + 16, latent)),
        v_e=vmem((latent, 256)),
    )
    node_sums = dict(
        d_bn=vmem((latent, latent)),
        d_an=vmem((2 * latent, latent)),
        v_n=vmem((latent, 512)),
    )
    outer_sums = dict(d_outer=vmem((latent, latent // 2)))
    row_flops = 2 * latent * latent * graphs * edge_count
    prefetch = dict(ids=ids)

    zero = kernel_call(
        functools.partial(first_kernel, plan, tiles),
        "first",
        dict(
            pack=list(pack_first),
            src=(source_vertex, ids_spec),
            dst=(target_vertex, ids_spec),
            x_now=(x_now_t, x_spec),
            x_next=(x_next_t, x_spec),
            border=(border, border_spec),
            link=(link_t, link_spec),
        ),
        dict(
            h_out=(node_f32, node_spec),
            hb=(node_bf, node_spec),
            aggl=(node_bf, node_spec),
            zn=(node_bf, node_spec),
            xn=(node_bf, node_spec),
            ivn=(node_row_f32, node_row),
            z1=(edge_bf, edge_spec),
            xh=(edge_bf, edge_spec),
            iv=(edge_row_f32, edge_row),
            e_out=(edge_f32, edge_spec),
        ),
        dict(**weight_scratch, **forward_scratch, link8=vmem((8, tile)), h=vmem((latent, nodes))),
        grid=(graphs, tiles),
        prefetch=prefetch,
        cost=(row_flops * 8, 20_000_000),
    )

    last_at = graphs * tiles - 1

    def early_edge(p, g, t, *_):
        return (jnp.where(p == 0, g * tiles + t, last_at), 0, 0)

    def late_edge(p, g, t, *_):
        return (jnp.where(p == 2, g * tiles + t, 0), 0, 0)

    def early_node(p, g, t, *_):
        return (jnp.where(p == 0, g, graphs - 1), 0, 0)

    def late_node(p, g, t, *_):
        return (jnp.where(p == 2, g, 0), 0, 0)

    def late_x(p, g, t, *_):
        return (0, jnp.where(p == 2, g, 0))

    early_node_spec = pl.BlockSpec((1, latent, nodes), early_node)
    early_edge_spec = pl.BlockSpec((1, latent, tile), early_edge)
    late_node_spec = pl.BlockSpec((1, latent, nodes), late_node)
    tile_ids = pl.BlockSpec((graphs, tile), lambda p, g, t, *_: (0, t))
    late_x_spec = pl.BlockSpec((channels, nodes), late_x)
    blocks = (Block(plan, 0), Block(plan, 1), Block(plan, 2))

    def grad_outs(r):
        return [sds((blocks[r].total, latent), BF)] * plan.fsdp

    all_nodes = (graphs, latent, nodes)
    all_edges = (graphs * tiles, latent, tile)
    mid = kernel_call(
        functools.partial(middle_kernel, plan, blocks[2], graphs, tiles),
        "middle",
        dict(
            pack=list(pack_rest),
            src=(source_vertex, tile_ids),
            dst=(target_vertex, tile_ids),
            h_in=(zero.h_out, early_node_spec),
            e_in=(zero.e_out, early_edge_spec),
            x_now=(x_now_t, late_x_spec),
            x_next=(x_next_t, late_x_spec),
            border=(border, pl.BlockSpec((1, nodes), late_x)),
            level=level,
            stats=stats,
        ),
        dict(
            hb=(node_bf, early_node_spec),
            z1=(edge_bf, early_edge_spec),
            xh=(edge_bf, early_edge_spec),
            iv=(edge_row_f32, pl.BlockSpec((1, 1, tile), early_edge)),
            grad=grad_outs(2),
            gh_out=(node_f32, late_node_spec),
            gagg_out=(node_bf, late_node_spec),
            ge_out=(edge_f32, pl.BlockSpec((1, latent, tile), late_edge)),
            count_out=(sds((1, 1), F32), sm),
        ),
        dict(
            **weight_scratch,
            **forward_scratch,
            **edge_sums,
            **node_sums,
            **outer_sums,
            loss=vmem((8, 128)),
            hb1=vmem(all_nodes, BF),
            aggl1=vmem(all_nodes, BF),
            zn1=vmem(all_nodes),
            xn1=vmem(all_nodes),
            ivn1=vmem((graphs, 1, nodes)),
            wan1=vmem((2 * latent, latent), BF),
            wbn1=vmem((latent, latent), BF),
            cols1=vmem((latent, 16)),
            d_bn1=vmem((latent, latent)),
            d_an1=vmem((2 * latent, latent)),
            v_n1=vmem((latent, 512)),
            hb2=vmem(all_nodes, BF),
            aggl2=vmem(all_nodes, BF),
            zn2=vmem(all_nodes),
            xn2=vmem(all_nodes),
            ivn2=vmem((graphs, 1, nodes)),
            h_all=vmem(all_nodes),
            e_all=vmem(all_edges),
            low2=vmem((graphs * tiles, latent + 16, tile), BF),
            z12=vmem(all_edges, BF),
            xh2=vmem(all_edges, BF),
            iv2=vmem((graphs * tiles, 1, tile)),
            aux=vmem((channels, 256)),
        ),
        grid=(3, graphs, tiles),
        prefetch=dict(ids=ids, counts=node_counts),
        cost=(row_flops * 27, 40_000_000),
    )
    anywhere = pl.BlockSpec(memory_space=pl.ANY)

    def back(r, places, kept, grads, other):
        first = r == 0
        count = len(places)
        node_shape = (count, latent, nodes)
        edge_shape = (count * tiles, latent, tile)

        def any_of(**group):
            return {n: (v, anywhere) for n, v in group.items()}

        ins = dict(
            pack_in=[(v, anywhere) for v in (pack_first if first else pack_rest)],
            src=source_vertex,
            dst=target_vertex,
            **any_of(hb_in=kept.hb, z1_in=kept.z1, xh_in=kept.xh, iv_in=kept.iv),
            **any_of(gh_in=grads.gh_out, gagg_in=grads.gagg_out, ge_in=grads.ge_out),
        )
        outs = dict(grad=grad_outs(r))
        scratch = dict(
            pack=vmem((plan.fsdp, plan.total, latent), BF),
            wa=vmem((3 * latent, latent), BF),
            wb=vmem((latent, latent), BF),
            cols=vmem((latent, 16)),
            u=vmem((2 * nodes, tile), BF),
            low_e=vmem((latent + 16, tile), BF),
            **edge_sums,
            z1=vmem(edge_shape, BF),
            xh=vmem(edge_shape, BF),
            iv=vmem((count * tiles, 1, tile)),
            ge=vmem(edge_shape),
            hb=vmem(node_shape, BF),
            gh_all=vmem(node_shape),
            gagg_all=vmem(node_shape, BF),
            sems=pltpu.SemaphoreType.DMA((6 + count * tiles, 8)),
        )
        if first:
            (g,) = places
            ins.update(
                x_now=(x_now_t, pl.BlockSpec((channels, nodes), lambda *_: (0, g))),
                x_next=(x_next_t, pl.BlockSpec((channels, nodes), lambda *_: (0, g))),
                border=(border, pl.BlockSpec((1, nodes), lambda *_: (0, g))),
                link=(link_t, pl.BlockSpec((1, 4, edge_count), lambda *_: (g, 0, 0))),
            )
            if other is not None:
                ins.update(other=list(other.grad))
            scratch.update(**outer_sums, d_ee=vmem((latent, 8)), link8=vmem((8, tile)))
            scratch.update(ge_low=vmem((latent, tile), BF))
        else:
            ins.update(before_in=[(v, anywhere) for v in pack_first])
            ins.update(any_of(e_in=zero.e_out, hb0_in=zero.hb, aggl_in=zero.aggl))
            ins.update(any_of(zn_in=zero.zn, xn_in=zero.xn, ivn_in=zero.ivn))
            outs.update(
                gh_out=sds(node_shape, F32), gagg_out=sds(node_shape, BF), ge_out=(sds(edge_shape, F32), anywhere)
            )
            scratch.update(
                **node_sums,
                before=vmem((plan.fsdp, plan.total, latent), BF),
                e=vmem(edge_shape),
                hb0=vmem(node_shape, BF),
                aggl=vmem(node_shape, BF),
                zn=vmem(node_shape, BF),
                xn=vmem(node_shape, BF),
                ivn=vmem((count, 1, nodes)),
                wbn=vmem((latent, latent), BF),
                wan=vmem((2 * latent, latent), BF),
                cols1=vmem((latent, 16)),
            )
        return kernel_call(
            functools.partial(back_kernel, plan, blocks[r], first, places, tiles),
            f"back{r}_{places[0]}",
            ins,
            outs,
            scratch,
            grid=(1,),
            prefetch=prefetch,
            cost=(row_flops * 11 * count // graphs, 15_000_000 * count),
        )

    def total_of(parts):
        total = parts[0].astype(F32)
        for part in parts[1:]:
            total = total + part.astype(F32)
        return total

    def exchange_grads(bag):
        return exchange(bag.grad, "fsdp", plan.fsdp)

    def owned(got, r):
        return total_of(got).astype(BF).reshape(plan.dp, blocks[r].piece, latent)

    def reduce_owner(value):
        return lax.all_to_all(value, "dp", 0, 0, tiled=True)

    def share(parts):
        total = jnp.sum(parts.astype(F32), axis=0)
        wide = jnp.broadcast_to(total[None], (plan.dp, *total.shape))
        return lax.all_to_all(wide, "dp", 0, 0, tiled=True)

    def share_scaled(parts):
        total = jnp.sum(parts.astype(F32), axis=0)
        count = total.shape[0]
        top = jnp.max(jnp.abs(total), axis=1, keepdims=True)
        power = jnp.clip(jnp.ceil(jnp.log2(jnp.maximum(top, 1e-30))), -100.0, 100.0) - 14.0
        value = (total * jnp.exp2(-power)).astype(jnp.float16)
        row = lax.broadcasted_iota(jnp.int32, (count, latent), 0)
        lane = lax.broadcasted_iota(jnp.int32, (count, latent), 1)
        powers = jnp.sum(jnp.where(row == lane, power, 0.0), axis=0, keepdims=True)
        powers = jnp.broadcast_to(powers, (8, latent)).astype(jnp.float16)
        wide = jnp.broadcast_to(jnp.concatenate([value, powers], axis=0)[None], (plan.dp, count + 8, latent))
        got = lax.all_to_all(wide, "dp", 0, 0, tiled=True)
        powers = got[:, count : count + 1, :].astype(F32)
        scale = jnp.exp2(jnp.sum(jnp.where((row == lane)[None], powers, 0.0), axis=2, keepdims=True))
        return got[:, :count, :].astype(F32) * scale

    def after(bag, *others):
        bag.grad, held = lax.optimization_barrier((bag.grad, others))
        return held

    got2 = exchange_grads(mid)
    one = back(1, tuple(range(graphs)), mid, mid, None)
    owned2 = owned(got2, 2)
    (owned2,) = after(one, owned2)
    got1 = exchange_grads(one)
    last = None
    for g in range(graphs):
        last = back(0, (g,), zero, one, last)
        if g == 0:
            both = jnp.concatenate([owned2, owned(got1, 1)], axis=1)
            (both,) = after(last, both)
            parts = reduce_owner(both)
    (parts,) = after(last, parts)
    got0 = exchange_grads(last)
    shared = share_scaled(parts)
    owned0, shared = lax.optimization_barrier((owned(got0, 0), shared))
    whole0 = share(reduce_owner(owned0))

    def turned(group):
        return (group[0].T, *group[1:])

    weights, moments, squares = turned(weights), turned(moments), turned(squares)
    numbers = (2, 3, 4, 5, 6)

    def products(numbers):
        return [sds(weights[k].shape, F32) for k in numbers for _ in range(3)]

    early = kernel_call(
        functools.partial(update_early_kernel, plan, blocks, numbers),
        "update_early",
        dict(
            shared=shared,
            weight=[weights[k] for k in numbers],
            moment=[moments[k] for k in numbers],
            square=[squares[k] for k in numbers],
        ),
        dict(products=products(numbers), loss=(sds((1, 1), F32), sm)),
        dict(grads2=vmem((blocks[2].total, latent)), grads1=vmem((blocks[1].total, latent))),
        cost=(1000, 9_000_000),
    )

    def slot(value):
        shape = value.shape
        cut = (1, 1, *shape[2:]) if len(shape) == 4 else (1, *shape[1:])
        return value, pl.BlockSpec(cut, lambda *_: (0,) * len(shape))

    partial = (2, 3, 5)
    alone = (0, 1)
    held = [early.products[3 * numbers.index(k) + i] for k in partial for i in range(3)]

    def pick(group):
        return [group[k] for k in alone] + [slot(group[k]) for k in partial]

    late = kernel_call(
        functools.partial(update_late_kernel, plan, blocks[0], alone + partial),
        "update_late",
        dict(
            grads=whole0.reshape(blocks[0].total, latent),
            weight=pick(weights),
            moment=pick(moments),
            square=pick(squares),
            held=[(v, anywhere) for v in held],
        ),
        dict(products=products(alone), slots=[slot(v) for v in products(partial)]),
        grid=(1,),
        cost=(1000, 1_000_000),
        alias=("held", "slots"),
    )
    new = [None] * 7
    for k in numbers:
        new[k] = early.products[3 * numbers.index(k) :][:3]
    for k, v in enumerate(alone + partial):
        new[v] = (late.products + late.slots)[3 * k : 3 * k + 3]
    results = [v.T for v in new[0]]
    for k in range(1, 7):
        results += new[k]
    return (early.loss.reshape(()), mid.count_out.reshape(()), *results)


def solution(mesh):
    rows = P(("dp", "fsdp"), None)
    row = P(("dp", "fsdp"))
    weight_specs = (
        P(None, "fsdp"),
        P(None, "fsdp"),
        P(None, "fsdp", None),
        P(None, None, "fsdp", None),
        P(None, "fsdp", None),
        P(None, None, None, "fsdp"),
        P("fsdp", None),
    )
    placed = (rows, rows, row, row, rows, rows, P(("dp", "fsdp"), None, None), P(), *weight_specs * 3)
    out_specs = [P(), P()]
    for spec in weight_specs:
        out_specs += [spec] * 3

    def step(*args):
        plan = Plan(args[10].shape[2], mesh.shape["dp"], mesh.shape["fsdp"])
        return body(plan, *args)

    return jax.shard_map(
        step, mesh=mesh, in_specs=placed, out_specs=tuple(out_specs), check_vma=False
    )
```

```python
import functools

import jax
import jax.numpy as jnp
from jax import lax
from jax.experimental import pallas as pl
from jax.experimental.pallas import tpu as pltpu
from jax.sharding import PartitionSpec as P

VARS = 6
LEVELS = 13
ROUNDS = 3
STEP = 10

norm_eps = 1e-05
stat_eps = 1e-06
beta_one = 0.9
beta_two = 0.999
adam_eps = 1e-08
decay_rate = 0.01
rate_matrix = 0.03
rate_vector = 0.2

EDGE_FIRST, EDGE_SECOND, NODE_FIRST, NODE_SECOND, ROWS, OUTER = range(6)

BF = jnp.bfloat16
F32 = jnp.float32
VMEM_LIMIT = 60 * 1024 * 1024
EDGE_TILE = 1536
CHUNK = 256


def contract(a, b, da, db):
    return lax.dot_general(a, b, (((da,), (db,)), ((), ())), preferred_element_type=F32)


def nn(a, b):
    return contract(a, b, 1, 0)


def nt(a, b):
    return contract(a, b, 1, 1)


def tn(a, b):
    return contract(a, b, 0, 0)


def sigmoid(v):
    return 0.5 * jnp.tanh(0.5 * v) + 0.5


def silu(v):
    half = 0.5 * v
    return half * jnp.tanh(half) + half


def round_up(v, m):
    return (v + m - 1) // m * m


def stacked(sizes):
    offset = 0
    at = {}
    for name, size in sizes:
        at[name] = (offset, size)
        offset += size
    return at, offset


class Plan:
    def __init__(self, latent, dp_size, fsdp_size):
        self.latent = latent
        self.dp = dp_size
        self.fsdp = fsdp_size
        self.width = latent // fsdp_size
        self.half = self.width // 2
        width = self.width
        sizes = (
            (EDGE_FIRST, 3 * width),
            (EDGE_SECOND, width),
            (NODE_SECOND, width),
            (NODE_FIRST, 2 * width),
            (ROWS, 16),
            (OUTER, self.half),
        )
        self.at, self.total = stacked(sizes)


class Block:
    def __init__(self, plan, node_parts):
        width = plan.width
        sizes = [(EDGE_FIRST, 3 * width), (EDGE_SECOND, width), (ROWS, 16), (OUTER, plan.half)]
        for k in range(node_parts):
            sizes += [((NODE_FIRST, k), 2 * width), ((NODE_SECOND, k), width), ((ROWS, k), 16)]
        self.at, self.used = stacked(sizes)
        self.piece = round_up((self.used + plan.dp - 1) // plan.dp, 8)
        self.total = self.piece * plan.dp


def live_row(border, count):
    place = lax.broadcasted_iota(jnp.int32, border.shape, 1)
    return jnp.where((place < count) & (border != 1), 1.0, 0.0).astype(F32)


def group_matrix(rows, cols, flip):
    var = lax.broadcasted_iota(jnp.int32, (rows, cols), 1 if flip else 0)
    chan = lax.broadcasted_iota(jnp.int32, (rows, cols), 0 if flip else 1)
    inside = (chan >= var * LEVELS) & (chan < (var + 1) * LEVELS)
    return jnp.where(inside, 1.0, 0.0).astype(F32)


def exact(a, b):
    return lax.dot_general(
        a, b, (((1,), (0,)), ((), ())), precision=lax.Precision.HIGHEST, preferred_element_type=F32
    )


class Bag:
    pass


def kernel_call(kernel, name, ins, outs, scratch=None, grid=(), prefetch=None, cost=None, alias=None):
    scratch = scratch or {}
    prefetch = prefetch or {}
    whole = pl.BlockSpec(memory_space=pltpu.VMEM)

    def flat(group):
        return [(n, v) for n, vs in group.items() for v in (vs if isinstance(vs, list) else [vs])]

    def fill(groups, values):
        bag = Bag()
        at = 0
        for group in groups:
            for n, vs in group.items():
                count = len(vs) if isinstance(vs, list) else None
                if count is None:
                    setattr(bag, n, values[at])
                    at += 1
                else:
                    setattr(bag, n, list(values[at : at + count]))
                    at += count
        return bag

    def split(item):
        if isinstance(item, tuple):
            return item
        if not grid:
            return item, whole
        rank = len(item.shape)
        return item, pl.BlockSpec(item.shape, lambda *_: (0,) * rank)

    def run(*refs):
        kernel(fill((prefetch, ins, outs, scratch), refs))

    sources = [split(v) for _, v in flat(ins)]
    products = [split(v) for _, v in flat(outs)]
    aliases = {}
    if alias:
        first_in = [n for n, _ in flat(ins)].index(alias[0]) + len(prefetch)
        first_out = [n for n, _ in flat(outs)].index(alias[1])
        aliases = {first_in + k: first_out + k for k in range(len(ins[alias[0]]))}
    result = pl.pallas_call(
        run,
        out_shape=[v for v, _ in products],
        grid_spec=pltpu.PrefetchScalarGridSpec(
            num_scalar_prefetch=len(prefetch),
            grid=grid,
            in_specs=[spec for _, spec in sources],
            out_specs=[spec for _, spec in products],
            scratch_shapes=list(scratch.values()),
        ),
        compiler_params=pltpu.CompilerParams(vmem_limit_bytes=VMEM_LIMIT),
        input_output_aliases=aliases,
        cost_estimate=pl.CostEstimate(flops=cost[0], bytes_accessed=cost[1], transcendentals=0),
        name=name,
    )(*prefetch.values(), *[v for v, _ in sources])
    return fill((outs,), result)


def pack_round(plan, out, r, edge_first, second_layers, node_first, vectors, edge_encoder, outer):
    width = plan.width
    at = plan.at

    def put(name, value):
        start, size = at[name]
        out[start : start + size, :] = value.astype(BF)

    put(EDGE_FIRST, edge_first[r])
    put(EDGE_SECOND, second_layers[r, 0])
    put(NODE_SECOND, second_layers[r, 1])
    put(NODE_FIRST, node_first[r])
    rows = jnp.concatenate([vectors[r, 0], vectors[r, 1]], axis=0)
    if edge_encoder is None:
        low = jnp.zeros((8, width), F32)
    else:
        low = jnp.concatenate([edge_encoder[...], jnp.zeros((4, width), F32)], axis=0)
    rows = jnp.concatenate([rows, low], axis=0)
    rows = jnp.concatenate([rows, jnp.zeros((16, plan.latent - width), F32)], axis=1)
    put(ROWS, rows)
    start, size = at[OUTER]
    if outer is None:
        out[start : start + size, :] = jnp.zeros((size, plan.latent), BF)
    else:
        channels = outer.shape[1]
        wide = jnp.concatenate(
            [outer[...], jnp.zeros((width, plan.latent // 2 - channels), F32)], axis=1
        )
        put(OUTER, jnp.concatenate([wide[: plan.half], wide[plan.half :]], axis=1))


def pack_first_kernel(plan, b):
    pack_round(plan, b.pack, 0, b.ef, b.sl, b.nf, b.vec, b.ee, b.enc)


def merge_stats(stats):
    total = jnp.sum(stats, axis=0)
    count = total[:, 2:3]
    mean = total[:, 0:1] / (count * LEVELS)
    own_count = stats[:, :, 2:3] * LEVELS
    shift = stats[:, :, 0:1] / jnp.maximum(own_count, 1.0) - mean[None]
    spread = jnp.sum(stats[:, :, 1:2] + own_count * shift * shift, axis=0)
    return count, spread


def pack_rest_kernel(plan, graphs, b):
    pack_round(plan, b.pack.at[0], 1, b.ef, b.sl, b.nf, b.vec, None, None)
    pack_round(plan, b.pack.at[1], 2, b.ef, b.sl, b.nf, b.vec, None, b.dec)
    nodes = b.x_now.shape[1] // graphs
    channels = b.x_now.shape[0]
    lives = []
    for g in range(graphs):
        lives.append(live_row(b.border[:, g * nodes : (g + 1) * nodes], b.counts[g]))
    live = jnp.concatenate(lives, axis=1)
    delta = b.x_next[...] - b.x_now[...]
    count = jnp.sum(live)
    sums = jnp.sum(delta * live, axis=1, keepdims=True)
    to_var = group_matrix(8, channels, False)
    to_chan = group_matrix(channels, 8, True)
    var_sum = exact(to_var, jnp.broadcast_to(sums, (channels, 128)))
    mean = var_sum / (jnp.maximum(count, 1.0) * LEVELS)
    centered = (delta - exact(to_chan, mean)[:, 0:1]) * live
    square = jnp.sum(centered * centered, axis=1, keepdims=True)
    var_square = exact(to_var, jnp.broadcast_to(square, (channels, 128)))
    lane = lax.broadcasted_iota(jnp.int32, (8, 128), 1)
    value = jnp.where(lane == 0, var_sum, jnp.where(lane == 1, var_square, count))
    b.stats[...] = jnp.broadcast_to(value[None], b.stats.shape)


def assemble(plan, me, packs, edge_first=None, edge_second=None, node_second=None, node_first=None, cols=None, outer=None):
    width = plan.width
    latent = plan.latent
    total = jnp.zeros((latent, 16), F32)
    rowid = lax.broadcasted_iota(jnp.int32, (latent, width), 0)
    colid = lax.broadcasted_iota(jnp.int32, (latent, width), 1)
    for k, pack in enumerate(packs):
        owner = jnp.bitwise_xor(me, k)

        def put(ref, name, step):
            if ref is not None:
                start, size = plan.at[name]
                ref[pl.ds(pl.multiple_of(owner * step, 16), size), :] = pack[start : start + size, :]

        put(edge_first, EDGE_FIRST, 3 * width)
        put(edge_second, EDGE_SECOND, width)
        put(node_second, NODE_SECOND, width)
        put(node_first, NODE_FIRST, 2 * width)
        start, size = plan.at[ROWS]
        place = jnp.where(rowid == owner * width + colid, 1.0, 0.0).astype(BF)
        total = total + nt(place, pack[start : start + size, 0:width])
        if outer is not None:
            start, size = plan.at[OUTER]
            half = latent // 2
            first = pl.multiple_of(owner * width, 16)
            second = pl.multiple_of(owner * width + plan.half, 16)
            outer[pl.ds(first, size), :] = pack[start : start + size, 0:half]
            outer[pl.ds(second, size), :] = pack[start : start + size, half : 2 * half]
    cols[...] = total


def assemble_all(plan, b, packs, outer):
    assemble(plan, b.ids[0], packs, b.wa, b.wb, b.wbn, b.wan, b.cols, b.outer if outer else None)


def turn_weights(plan, b, nodes):
    latent = plan.latent
    b.b_t[...] = b.wb[...].astype(F32).T.astype(BF)
    b.pcat[:, 2 * nodes :] = b.wa[2 * latent :, :].astype(F32).T.astype(BF)


def fill_tables(u_ref, src, dst, nodes, lanes):
    count = lanes.stop - lanes.start
    place = lax.broadcasted_iota(jnp.int32, (nodes, count), 0).astype(jnp.int16)
    one = jnp.ones((nodes, count), BF)
    zero = jnp.zeros((nodes, count), BF)
    u_ref[0:nodes, lanes] = jnp.where(place == src[:, lanes].astype(jnp.int16), one, zero)
    u_ref[nodes : 2 * nodes, lanes] = jnp.where(place == dst[:, lanes].astype(jnp.int16), one, zero)


def skew(chunks):
    live = []
    waiting = list(chunks)
    while live or waiting:
        if waiting:
            live.append(waiting.pop(0))
        for item in list(reversed(live)):
            if next(item, 1) == 1:
                live.remove(item)


def norm_forward(z2, count):
    mean = jnp.sum(z2, axis=0, keepdims=True) * (1.0 / count)
    centered = z2 - mean
    var = jnp.sum(centered * centered, axis=0, keepdims=True) * (1.0 / count)
    inverse = lax.rsqrt(var + norm_eps)
    return centered * inverse, inverse


def forward_nodes_in(plan, b, state):
    latent = plan.latent
    nodes = state.shape[-1]
    low = state.astype(BF)
    b.pcat[:, 0:nodes] = tn(b.wa[0:latent, :], low).astype(BF)
    b.pcat[:, nodes : 2 * nodes] = tn(b.wa[latent : 2 * latent, :], low).astype(BF)
    b.agg[...] = jnp.zeros_like(b.agg)
    return low


def forward_edges(plan, b, src, dst, tile, get, put, kept):
    nodes = b.agg.shape[-1]
    z1_ref, xh_ref, iv_ref = kept

    def chunk(at):
        lanes = slice(at, at + CHUNK)
        fill_tables(b.u, src, dst, nodes, lanes)
        b.u[2 * nodes :, lanes] = get(lanes).astype(BF)
        yield
        z1 = nn(b.pcat[...], b.u[:, lanes])
        yield
        z1 = z1 + b.cols[:, 0:1]
        active = silu(z1).astype(BF)
        z1_ref[:, lanes] = z1.astype(BF)
        yield
        z2 = nn(b.b_t[...], active)
        yield
        z2 = z2 + b.cols[:, 1:2]
        normed, inverse = norm_forward(z2, plan.latent)
        xh_ref[:, lanes] = normed.astype(BF)
        iv_ref[:, lanes] = inverse
        e = get(lanes) + (normed * b.cols[:, 2:3] + b.cols[:, 3:4])
        if put is not None:
            put(lanes, e)
        b.new_low[:, lanes] = e.astype(BF)
        yield

    skew([chunk(at) for at in range(0, tile, CHUNK)])
    b.agg[...] += nt(b.new_low[...], b.u[nodes : 2 * nodes, :])


def forward_nodes_out(plan, b, state, low, arriving):
    latent = plan.latent
    z1 = tn(b.wan[0:latent, :], low) + tn(b.wan[latent:, :], arriving) + b.cols[:, 4:5]
    active = silu(z1).astype(BF)
    z2 = tn(b.wbn[...], active) + b.cols[:, 5:6]
    normed, inverse = norm_forward(z2, latent)
    return z1, normed, inverse, state + (normed * b.cols[:, 6:7] + b.cols[:, 7:8])


def norm_backward(grad, gain, normed, inverse, count):
    scaled = grad * gain
    mean = jnp.sum(scaled, axis=0, keepdims=True) * (1.0 / count)
    cross = jnp.sum(scaled * normed, axis=0, keepdims=True) * (1.0 / count)
    return (inverse * (scaled - mean - normed * cross)).astype(BF)


def lane_sum(value):
    total = value[:, 0:128]
    for k in range(1, value.shape[1] // 128):
        total = total + value[:, 128 * k : 128 * (k + 1)]
    return total


def backward_reset(plan, b, tile, refs):
    for ref in refs:
        ref[...] = jnp.zeros_like(ref)
    b.act[plan.latent :, :] = jnp.ones((16, tile), BF)


def backward_nodes_in(plan, weights, sums, grad, low_h, arriving, z1, normed, inverse):
    latent = plan.latent
    wan, wbn, cols = weights
    z1 = z1.astype(F32)
    normed = normed.astype(F32)
    d_an, d_bn, v_n = sums
    v_n[:, 0:128] += lane_sum(grad * normed)
    v_n[:, 128:256] += lane_sum(grad)
    low_two = norm_backward(grad, cols[:, 6:7], normed, inverse, latent)
    gate = sigmoid(z1)
    soft = z1 * gate
    d_bn[...] += nt(soft.astype(BF), low_two)
    d_active = nn(wbn[...], low_two)
    low_one = (d_active * (soft - soft * gate + gate)).astype(BF)
    v_n[:, 256:384] += lane_sum(low_one.astype(F32))
    v_n[:, 384:512] += lane_sum(low_two.astype(F32))
    d_an[0:latent, :] += nt(low_h, low_one)
    d_an[latent:, :] += nt(arriving, low_one)
    return grad + nn(wan[0:latent, :], low_one), nn(wan[latent:, :], low_one).astype(BF)


def backward_edges(plan, b, src, dst, tile, get, kept, low_e, put):
    z1_ref, xh_ref, iv_ref = kept
    latent = plan.latent
    nodes = b.gagg.shape[-1]

    def chunk(at):
        lanes = slice(at, at + CHUNK)
        fill_tables(b.u, src, dst, nodes, lanes)
        yield
        ge = nn(b.gagg[...], b.u[nodes : 2 * nodes, lanes])
        yield
        if get is not None:
            ge = ge + get(lanes)
        normed = xh_ref[:, lanes].astype(F32)
        b.v_e[:, 0:128] += lane_sum(ge * normed)
        b.v_e[:, 128:256] += lane_sum(ge)
        low_two = norm_backward(ge, b.cols[:, 2:3], normed, iv_ref[:, lanes], latent)
        b.two[:, lanes] = low_two
        yield
        d_active = nn(b.wb[...], low_two)
        yield
        z1 = z1_ref[:, lanes].astype(F32)
        gate = sigmoid(z1)
        soft = z1 * gate
        b.act[0:latent, lanes] = soft.astype(BF)
        low_one = (d_active * (soft - soft * gate + gate)).astype(BF)
        b.one[:, lanes] = low_one
        yield
        put(lanes, ge + nn(b.wa[2 * latent :, :], low_one))
        yield

    skew([chunk(at) for at in range(0, tile, CHUNK)])
    b.d_b[...] += nt(b.act[...], b.two[...])
    b.d_first[2 * latent :, :] += nt(low_e[...], b.one[...])
    b.q[...] += nt(b.one[...], b.u[0 : 2 * nodes, :])


def backward_nodes_out(plan, b, low_h):
    latent = plan.latent
    nodes = b.gagg.shape[-1]
    total = b.gh[...]
    for side in range(2):
        sums = b.q[:, side * nodes : (side + 1) * nodes]
        high = sums.astype(BF)
        rows = slice(side * latent, (side + 1) * latent)
        b.d_first[rows, :] += nt(low_h, high)
        total = total + nn(b.wa[rows, :], high)
    return total


def row_of(cols128):
    return jnp.sum(cols128.T, axis=0, keepdims=True)


def backward_emit(plan, block, b, low, outer, node_sums, before):
    latent = plan.latent
    width = plan.width
    rows = [
        b.d_first[3 * latent : 3 * latent + 1, :],
        b.d_b[latent : latent + 1, :],
        row_of(b.v_e[:, 0:128]),
        row_of(b.v_e[:, 128:256]),
        jnp.zeros((4, latent), F32),
        jnp.zeros((8, latent), F32) if low is None else low,
    ]
    groups = [(ROWS, jnp.concatenate(rows, axis=0).astype(BF))]
    for k, (_, _, v_n) in enumerate(node_sums):
        rows = [
            row_of(v_n[:, 256:384]),
            row_of(v_n[:, 384:512]),
            row_of(v_n[:, 0:128]),
            row_of(v_n[:, 128:256]),
            jnp.zeros((12, latent), F32),
        ]
        groups.append(((ROWS, k), jnp.concatenate(rows, axis=0).astype(BF)))
    rowid = lax.broadcasted_iota(jnp.int32, (latent, latent), 0)
    colid = lax.broadcasted_iota(jnp.int32, (latent, latent), 1)
    for k, out in enumerate(b.grad):
        owner = jnp.bitwise_xor(b.ids[0], k)

        def put(name, value):
            start, size = block.at[name]
            rows = slice(start, start + size)
            if before is not None:
                value = value + before[k][rows, :].astype(F32)
            out[rows, :] = value.astype(BF)

        def take(ref, step):
            return ref[pl.ds(pl.multiple_of(owner * step, 8), step), :]

        put(EDGE_FIRST, take(b.d_first, 3 * width))
        put(EDGE_SECOND, take(b.d_b, width))
        inside = (rowid == owner * width + colid) & (colid < width)
        place = jnp.where(inside, 1.0, 0.0).astype(BF)
        for name, value in groups:
            put(name, nn(value, place))
        if outer is not None:
            own = take(outer, width)
            put(OUTER, jnp.concatenate([own[: plan.half], own[plan.half :]], axis=1))
        else:
            put(OUTER, jnp.zeros((plan.half, latent), F32))
        for k2, (d_an, d_bn, _) in enumerate(node_sums):
            put((NODE_FIRST, k2), take(d_an, 2 * width))
            put((NODE_SECOND, k2), take(d_bn, width))
        if block.total > block.used:
            out[block.used :, :] = jnp.zeros((block.total - block.used, latent), BF)


def split_three(whole, lanes, period, place):
    high = whole.astype(BF).astype(F32)
    mid = (whole - high).astype(BF).astype(F32)
    rest = whole - high - mid
    lane = lax.broadcasted_iota(jnp.int32, (8, lanes), 1) % period - 3 * place
    top = lax.broadcasted_iota(jnp.int32, (8, lanes), 0) == 0
    value = jnp.where(lane == 0, high, jnp.where(lane == 1, mid, jnp.where(lane == 2, rest, 0.0)))
    return jnp.where(top, value, 0.0)


def first_kernel(plan, tiles, b):
    g = pl.program_id(0)
    t = pl.program_id(1)
    nodes = b.h_out.shape[-1]
    tile = b.z1.shape[-1]

    @pl.when((g == 0) & (t == 0))
    def _():
        assemble_all(plan, b, b.pack, True)
        turn_weights(plan, b, nodes)
        b.link8[...] = jnp.zeros_like(b.link8)

    @pl.when(t == 0)
    def _():
        chosen = jnp.where(b.border[...] == 1, b.x_next[...], b.x_now[...]).astype(BF)
        b.h[...] = nn(b.outer[:, 0 : b.x_now.shape[0]], chosen)
        b.hb[0] = forward_nodes_in(plan, b, b.h[...])

    b.link8[0:4, :] = b.link[0]

    def get(lanes):
        return nn(b.cols[:, 8:16].astype(BF), b.link8[:, lanes].astype(BF))

    def put(lanes, value):
        b.e_out[0, :, lanes] = value

    kept = (b.z1.at[0], b.xh.at[0], b.iv.at[0])
    forward_edges(plan, b, b.src[pl.ds(g, 1), :], b.dst[pl.ds(g, 1), :], tile, get, put, kept)

    @pl.when(t == tiles - 1)
    def _():
        state = b.h[...]
        b.aggl[0] = b.agg[...].astype(BF)
        z1, normed, b.ivn[0], b.h_out[0] = forward_nodes_out(plan, b, state, state.astype(BF), b.aggl[0])
        b.zn[0] = z1.astype(BF)
        b.xn[0] = normed.astype(BF)


def middle_kernel(plan, block, graphs, tiles, b):
    p = pl.program_id(0)
    g = pl.program_id(1)
    t = pl.program_id(2)
    nodes = b.gh_out.shape[-1]
    tile = b.z1.shape[-1]
    latent = plan.latent
    channels = b.x_now.shape[0]
    at = g * tiles + t
    start = (g == 0) & (t == 0)
    src = b.src[pl.ds(g, 1), :]
    dst = b.dst[pl.ds(g, 1), :]

    @pl.when((p == 0) & start)
    def _():
        assemble_all(plan, b, [r.at[0] for r in b.pack], False)
        turn_weights(plan, b, nodes)
        b.wan1[...] = b.wan[...]
        b.wbn1[...] = b.wbn[...]
        b.cols1[...] = b.cols[...]
        refs = (b.d_first, b.d_b, b.v_e, b.d_bn, b.d_an, b.v_n, b.d_bn1, b.d_an1, b.v_n1, b.d_outer, b.loss)
        backward_reset(plan, b, tile, refs)
        count, spread = merge_stats(b.stats[...])
        scale = lax.rsqrt(spread / (count * LEVELS) + stat_eps)
        b.aux[:, 0:128] = exact(group_matrix(channels, 8, True), jnp.broadcast_to(scale, (8, 128)))
        b.aux[:, 128:256] = jnp.broadcast_to(count[0:1] * channels, (channels, 128))
        b.count_out[0, 0] = jnp.sum(count[0:1]) * channels

    @pl.when((p == 1) & start)
    def _():
        assemble_all(plan, b, [r.at[1] for r in b.pack], True)
        turn_weights(plan, b, nodes)

    ends = (g == graphs - 1) & (t == tiles - 1)

    def joined(ref):
        return jnp.concatenate([ref[k] for k in range(graphs)], axis=1)

    def part(value, k):
        return value[:, k * nodes : (k + 1) * nodes]

    @pl.when((p == 0) & (t == 0))
    def _():
        b.h_all[g] = b.h_in[0]
        low = forward_nodes_in(plan, b, b.h_in[0])
        b.hb[0] = low
        b.hb1[g] = low

    @pl.when(p == 0)
    def _():
        def get(lanes):
            return b.e_in[0, :, lanes]

        def put(lanes, value):
            b.e_all[at, :, lanes] = value

        forward_edges(plan, b, src, dst, tile, get, put, (b.z1.at[0], b.xh.at[0], b.iv.at[0]))

    @pl.when((p == 0) & (t == tiles - 1))
    def _():
        b.aggl1[g] = b.agg[...].astype(BF)

    @pl.when((p == 0) & ends)
    def _():
        z1, normed, inverse, state = forward_nodes_out(plan, b, joined(b.h_all), joined(b.hb1), joined(b.aggl1))
        for k in range(graphs):
            b.zn1[k] = part(z1, k).astype(BF)
            b.xn1[k] = part(normed, k).astype(BF)
            b.ivn1[k] = part(inverse, k)
            b.h_all[k] = part(state, k)

    @pl.when((p == 1) & (t == 0))
    def _():
        b.hb2[g] = forward_nodes_in(plan, b, b.h_all[g])

    @pl.when(p == 1)
    def _():
        b.low2[at, latent:, :] = jnp.ones((16, tile), BF)

        def get(lanes):
            return b.e_all[at, :, lanes]

        forward_edges(plan, b, src, dst, tile, get, None, (b.z12.at[at], b.xh2.at[at], b.iv2.at[at]))
        b.low2[at, 0:latent, :] = b.u[2 * nodes :, :]

    @pl.when((p == 1) & (t == tiles - 1))
    def _():
        b.aggl2[g] = b.agg[...].astype(BF)

    @pl.when((p == 1) & ends)
    def _():
        z1, normed, inverse, state = forward_nodes_out(plan, b, joined(b.h_all), joined(b.hb2), joined(b.aggl2))
        final_low = state.astype(BF)
        delta = b.x_next[...] - b.x_now[...]
        scale = b.aux[:, 0:1]
        norm_count = b.aux[:, 128:129]
        predicted = tn(b.outer[...], final_low)[0:channels]
        misfit = (predicted - delta) * scale
        lives = [live_row(part(b.border, k), b.counts[k]) for k in range(graphs)]
        weighting = (b.level[...].astype(F32) + 1.0) / LEVELS * jnp.concatenate(lives, axis=1)
        b.loss[...] += jnp.broadcast_to(jnp.sum(weighting * misfit * misfit), b.loss.shape)
        grad_pred = (2.0 * weighting * misfit * scale / norm_count).astype(BF)
        b.d_outer[:, 0:channels] += nt(final_low, grad_pred)
        grad, arriving = backward_nodes_in(
            plan,
            (b.wan, b.wbn, b.cols),
            (b.d_an, b.d_bn, b.v_n),
            nn(b.outer[:, 0:channels], grad_pred),
            joined(b.hb2),
            joined(b.aggl2),
            z1,
            normed,
            inverse,
        )
        for k in range(graphs):
            b.h_all[k] = part(grad, k)
            b.aggl2[k] = part(arriving, k)

    @pl.when((p == 2) & (t == 0))
    def _():
        b.gh[...] = b.h_all[g]
        b.gagg[...] = b.aggl2[g]
        b.q[...] = jnp.zeros_like(b.q)

    @pl.when(p == 2)
    def _():
        def put(lanes, value):
            b.ge_out[0, :, lanes] = value

        kept = (b.z12.at[at], b.xh2.at[at], b.iv2.at[at])
        backward_edges(plan, b, src, dst, tile, None, kept, b.low2.at[at], put)

    @pl.when((p == 2) & (t == tiles - 1))
    def _():
        b.h_all[g] = backward_nodes_out(plan, b, b.hb2[g])

    @pl.when((p == 2) & ends)
    def _():
        grad, arriving = backward_nodes_in(
            plan,
            (b.wan1, b.wbn1, b.cols1),
            (b.d_an1, b.d_bn1, b.v_n1),
            joined(b.h_all),
            joined(b.hb1),
            joined(b.aggl1),
            joined(b.zn1),
            joined(b.xn1),
            joined(b.ivn1),
        )
        for k in range(graphs):
            b.gh_out[k] = part(grad, k)
            b.gagg_out[k] = part(arriving, k)
        low = split_three(b.loss[0:1, 0:1], latent, plan.width, b.ids[0])
        sums = ((b.d_an, b.d_bn, b.v_n), (b.d_an1, b.d_bn1, b.v_n1))
        backward_emit(plan, block, b, low, b.d_outer, sums, None)


def back_kernel(plan, block, first, places, tiles, b):
    tile = b.u.shape[-1]
    latent = plan.latent

    def copies(pairs, row):
        return [pltpu.make_async_copy(x, y, b.sems.at[row, k]) for k, (x, y) in enumerate(pairs)]

    picked = b.pack_in if first else [r.at[0] for r in b.pack_in]
    weights = copies([(x, b.pack.at[k]) for k, x in enumerate(picked)], 0)
    early = []
    late = []
    moves = []
    ends = []
    for k, g in enumerate(places):
        own = g if b.gh_in.shape[0] > 1 else 0
        pairs = [(b.gagg_in.at[own], b.gagg_all.at[k]), (b.gh_in.at[own], b.gh_all.at[k])]
        early.append(copies(pairs, 1 + k))
        pairs = [(b.hb_in.at[g], b.hb.at[k])]
        if not first:
            nodes_in = ((b.hb0_in, b.hb0), (b.aggl_in, b.aggl), (b.zn_in, b.zn), (b.xn_in, b.xn), (b.ivn_in, b.ivn))
            pairs += [(x.at[g], y.at[k]) for x, y in nodes_in]
        late.append(copies(pairs, 3 + k))
        for t in range(tiles):
            at = k * tiles + t
            place = g * tiles + t
            source = place if b.ge_in.shape[0] > tiles else t
            pairs = [(b.z1_in.at[place], b.z1.at[at]), (b.xh_in.at[place], b.xh.at[at])]
            pairs += [(b.iv_in.at[place], b.iv.at[at]), (b.ge_in.at[source], b.ge.at[at])]
            if not first:
                pairs.append((b.e_in.at[place], b.e.at[at]))
                ends.append(pltpu.make_async_copy(b.ge.at[at], b.ge_out.at[at], b.sems.at[5 + at, 6]))
            moves.append(copies(pairs, 5 + at))
    rest = [] if first else copies([(x, b.before.at[k]) for k, x in enumerate(b.before_in)], 5 + len(moves))
    for group in (weights, early[0], moves[0], *moves[1:], *early[1:], *late, rest):
        for copy in group:
            copy.start()

    def wait(group):
        for copy in group:
            copy.wait()

    sums = [b.d_first, b.d_b, b.v_e]
    sums += [b.d_outer, b.d_ee, b.link8] if first else [b.d_bn, b.d_an, b.v_n]
    backward_reset(plan, b, tile, sums)
    b.low_e[latent:, :] = jnp.ones((16, tile), BF)
    wait(weights)
    assemble(plan, b.ids[0], [b.pack.at[k] for k in range(plan.fsdp)], b.wa, b.wb, cols=b.cols)
    for k, g in enumerate(places):
        wait(early[k])
        b.gagg[...] = b.gagg_all[k]
        b.gh[...] = b.gh_all[k]
        b.q[...] = jnp.zeros_like(b.q)
        for t in range(tiles):
            at = k * tiles + t
            wait(moves[at])
            lanes = slice(t * tile, (t + 1) * tile)
            kept = (b.z1.at[at], b.xh.at[at], b.iv.at[at])

            def get(lanes, at=at):
                return b.ge[at, :, lanes]

            if first:
                b.link8[0:4, :] = b.link[k, :, lanes]
                b.low_e[0:latent, :] = nn(b.cols[:, 8:16].astype(BF), b.link8[...].astype(BF)).astype(BF)

                def put(lanes, value):
                    b.ge_low[:, lanes] = value.astype(BF)
            else:
                b.low_e[0:latent, :] = b.e[at].astype(BF)

                def put(lanes, value, at=at):
                    b.ge[at, :, lanes] = value

            src = b.src[g : g + 1, lanes]
            dst = b.dst[g : g + 1, lanes]
            backward_edges(plan, b, src, dst, tile, get, kept, b.low_e, put)
            if first:
                b.d_ee[...] += nt(b.ge_low[...], b.link8[...].astype(BF))
            else:
                ends[at].start()
        wait(late[k])
        total = backward_nodes_out(plan, b, b.hb[k])
        if first:
            chosen = jnp.where(b.border[...] == 1, b.x_next[...], b.x_now[...]).astype(BF)
            b.d_outer[:, 0 : b.x_now.shape[0]] += nt(total.astype(BF), chosen)
        else:
            if k == 0:
                wait(rest)
                packs = [b.before.at[k] for k in range(plan.fsdp)]
                assemble(plan, b.ids[0], packs, node_second=b.wbn, node_first=b.wan, cols=b.cols1)
            b.gh_out[k], b.gagg_out[k] = backward_nodes_in(
                plan,
                (b.wan, b.wbn, b.cols1),
                (b.d_an, b.d_bn, b.v_n),
                total,
                b.hb0[k],
                b.aggl[k],
                b.zn[k],
                b.xn[k],
                b.ivn[k],
            )
    if first:
        backward_emit(plan, block, b, b.d_ee[...].T, b.d_outer, (), b.other if places[0] > 0 else None)
    else:
        backward_emit(plan, block, b, None, None, ((b.d_an, b.d_bn, b.v_n),), None)
    wait(ends)


def adam_math(weight, moment, square, gradient, rate):
    moment_new = beta_one * moment + (1.0 - beta_one) * gradient
    square_new = beta_two * square + (1.0 - beta_two) * gradient * gradient
    direction = (
        moment_new
        * (1.0 / (1.0 - beta_one**STEP))
        / (jnp.sqrt(square_new * (1.0 / (1.0 - beta_two**STEP))) + adam_eps)
    )
    return (moment_new, square_new, weight - rate * (direction + decay_rate * weight))


def apply_update(b, k, index, gradient, rate):
    new = adam_math(b.weight[k][index], b.moment[k][index], b.square[k][index], gradient, rate)
    for ref, value in zip(b.new[k], new):
        ref[index] = value


def by_number(b, numbers, products):
    for group in (b.weight, b.moment, b.square):
        group[:] = [group[numbers.index(k)] if k in numbers else None for k in range(7)]
    b.new = [products[3 * numbers.index(k) : 3 * numbers.index(k) + 3] if k in numbers else None for k in range(7)]


def part_of(ref, block, name):
    start, size = block.at[name]
    return ref[start : start + size, :]


def update_edge(plan, b, ref, block, at):
    apply_update(b, 2, at, part_of(ref, block, EDGE_FIRST), rate_matrix)
    apply_update(b, 3, (at, 0), part_of(ref, block, EDGE_SECOND), rate_matrix)
    rows = part_of(ref, block, ROWS)
    apply_update(b, 5, (at, 0), rows[0:4, 0 : plan.width], rate_vector)
    half = plan.latent // 2
    wide = part_of(ref, block, OUTER)
    return rows, jnp.concatenate([wide[:, 0:half], wide[:, half:]], axis=0)


def update_early_kernel(plan, blocks, numbers, b):
    by_number(b, numbers, b.products)
    width = plan.width
    for source in range(plan.dp):
        for target, block, start in ((b.grads2, blocks[2], 0), (b.grads1, blocks[1], blocks[2].piece)):
            rows = slice(source * block.piece, (source + 1) * block.piece)
            target[rows, :] = b.shared[source, start : start + block.piece, :]
    rows, outer = update_edge(plan, b, b.grads2, blocks[2], 2)
    apply_update(b, 6, Ellipsis, outer[:, 0 : b.weight[6].shape[1]], rate_matrix)
    lane = lax.broadcasted_iota(jnp.int32, (1, plan.latent), 1)
    b.loss[0, 0] = jnp.sum(jnp.where(lane < width, rows[8:9, :], 0.0))
    update_edge(plan, b, b.grads1, blocks[1], 1)
    for r, ref, block, k in ((2, b.grads2, blocks[2], 0), (1, b.grads2, blocks[2], 1), (0, b.grads1, blocks[1], 0)):
        apply_update(b, 4, r, part_of(ref, block, (NODE_FIRST, k)), rate_matrix)
        apply_update(b, 3, (r, 1), part_of(ref, block, (NODE_SECOND, k)), rate_matrix)
        apply_update(b, 5, (r, 1), part_of(ref, block, (ROWS, k))[0:4, 0:width], rate_vector)


def update_late_kernel(plan, block, numbers, b):
    by_number(b, numbers, b.products + b.slots)
    rows, outer = update_edge(plan, b, b.grads, block, 0)
    apply_update(b, 0, Ellipsis, outer[:, 0 : b.weight[0].shape[1]], rate_matrix)
    apply_update(b, 1, Ellipsis, rows[8:12, 0 : plan.width], rate_matrix)


def body(plan, *args):
    x_now, x_next, node_counts, border_flag, source_vertex, target_vertex, link_features, level_ids = args[:8]
    weights = args[8:15]
    moments = args[15:22]
    squares = args[22:29]
    encoder, edge_encoder, edge_first, second_layers, node_first, vectors, decoder = weights
    graphs, edge_count = source_vertex.shape
    nodes = x_now.shape[0] // graphs
    channels = x_now.shape[1]
    latent = plan.latent
    tile = EDGE_TILE
    tiles = edge_count // tile
    x_now_t = x_now.T
    x_next_t = x_next.T
    border = border_flag.reshape(1, -1)
    link_t = jnp.transpose(link_features, (0, 2, 1))
    level = level_ids.reshape(-1, 1)
    ids = jnp.stack([lax.axis_index("fsdp"), lax.axis_index("dp")]).astype(jnp.int32)

    sm = pl.BlockSpec(memory_space=pltpu.SMEM)
    sds = jax.ShapeDtypeStruct
    pack_shape = sds((plan.total, latent), BF)
    devices = plan.dp * plan.fsdp

    def across(value, axis, size, mask):
        return lax.ppermute(value, axis, [(j, j ^ mask) for j in range(size)])

    def spread_chain(own, beside):
        got = [own]
        for k in range(1, plan.fsdp):
            source = got[k & (k - 1)]
            if k & (k - 1):
                source, _ = lax.optimization_barrier((source, beside))
            got.append(across(source, "fsdp", plan.fsdp, k & -k))
        return got

    def spread_direct(own, axis, size):
        return [own] + [across(own, axis, size, k) for k in range(1, size)]

    def exchange(parts, axis, size):
        return [parts[0]] + [across(parts[k], axis, size, k) for k in range(1, size)]

    raw = dict(ef=edge_first, sl=second_layers, nf=node_first, vec=vectors)
    start = kernel_call(
        functools.partial(pack_first_kernel, plan),
        "pack_first",
        dict(**raw, ee=edge_encoder, enc=encoder.T),
        dict(pack=pack_shape),
        cost=(1000, 3_000_000),
    )
    rest = kernel_call(
        functools.partial(pack_rest_kernel, plan, graphs),
        "pack_rest",
        dict(counts=(node_counts, sm), **raw, dec=decoder, x_now=x_now_t, x_next=x_next_t, border=border),
        dict(pack=sds((2, plan.total, latent), BF), stats=sds((devices, 8, 128), F32)),
        cost=(1000, 8_000_000),
    )
    pack_first = spread_chain(start.pack, rest.pack)
    pack_rest = spread_direct(rest.pack, "fsdp", plan.fsdp)
    stats = lax.all_to_all(rest.stats, ("dp", "fsdp"), 0, 0, tiled=True)

    ids_spec = pl.BlockSpec((graphs, tile), lambda g, t, *_: (0, t))
    x_spec = pl.BlockSpec((channels, nodes), lambda g, t, *_: (0, g))
    border_spec = pl.BlockSpec((1, nodes), lambda g, t, *_: (0, g))
    link_spec = pl.BlockSpec((1, 4, tile), lambda g, t, *_: (g, 0, t))
    node_spec = pl.BlockSpec((1, latent, nodes), lambda g, t, *_: (g, 0, 0))
    node_row = pl.BlockSpec((1, 1, nodes), lambda g, t, *_: (g, 0, 0))
    edge_spec = pl.BlockSpec((1, latent, tile), lambda g, t, *_: (g * tiles + t, 0, 0))
    edge_row = pl.BlockSpec((1, 1, tile), lambda g, t, *_: (g * tiles + t, 0, 0))

    node_f32 = sds((graphs, latent, nodes), F32)
    node_bf = sds((graphs, latent, nodes), BF)
    node_row_f32 = sds((graphs, 1, nodes), F32)
    edge_f32 = sds((graphs * tiles, latent, tile), F32)
    edge_bf = sds((graphs * tiles, latent, tile), BF)
    edge_row_f32 = sds((graphs * tiles, 1, tile), F32)

    def vmem(shape, kind=F32):
        return pltpu.VMEM(shape, kind)

    weight_scratch = dict(
        wa=vmem((3 * latent, latent), BF),
        wb=vmem((latent, latent), BF),
        wbn=vmem((latent, latent), BF),
        wan=vmem((2 * latent, latent), BF),
        cols=vmem((latent, 16)),
        outer=vmem((latent, latent // 2), BF),
        u=vmem((2 * nodes + latent, tile), BF),
    )
    forward_scratch = dict(
        b_t=vmem((latent, latent), BF),
        pcat=vmem((latent, 2 * nodes + latent), BF),
        new_low=vmem((latent, tile), BF),
        agg=vmem((latent, nodes)),
    )
    edge_sums = dict(
        act=vmem((latent + 16, tile), BF),
        one=vmem((latent, tile), BF),
        two=vmem((latent, tile), BF),
        gh=vmem((latent, nodes)),
        gagg=vmem((latent, nodes), BF),
        q=vmem((latent, 2 * nodes)),
        d_first=vmem((3 * latent + 16, latent)),
        d_b=vmem((latent + 16, latent)),
        v_e=vmem((latent, 256)),
    )
    node_sums = dict(
        d_bn=vmem((latent, latent)),
        d_an=vmem((2 * latent, latent)),
        v_n=vmem((latent, 512)),
    )
    outer_sums = dict(d_outer=vmem((latent, latent // 2)))
    row_flops = 2 * latent * latent * graphs * edge_count
    prefetch = dict(ids=ids)

    zero = kernel_call(
        functools.partial(first_kernel, plan, tiles),
        "first",
        dict(
            pack=list(pack_first),
            src=(source_vertex, ids_spec),
            dst=(target_vertex, ids_spec),
            x_now=(x_now_t, x_spec),
            x_next=(x_next_t, x_spec),
            border=(border, border_spec),
            link=(link_t, link_spec),
        ),
        dict(
            h_out=(node_f32, node_spec),
            hb=(node_bf, node_spec),
            aggl=(node_bf, node_spec),
            zn=(node_bf, node_spec),
            xn=(node_bf, node_spec),
            ivn=(node_row_f32, node_row),
            z1=(edge_bf, edge_spec),
            xh=(edge_bf, edge_spec),
            iv=(edge_row_f32, edge_row),
            e_out=(edge_f32, edge_spec),
        ),
        dict(**weight_scratch, **forward_scratch, link8=vmem((8, tile)), h=vmem((latent, nodes))),
        grid=(graphs, tiles),
        prefetch=prefetch,
        cost=(row_flops * 8, 20_000_000),
    )

    last_at = graphs * tiles - 1

    def early_edge(p, g, t, *_):
        return (jnp.where(p == 0, g * tiles + t, last_at), 0, 0)

    def late_edge(p, g, t, *_):
        return (jnp.where(p == 2, g * tiles + t, 0), 0, 0)

    def early_node(p, g, t, *_):
        return (jnp.where(p == 0, g, graphs - 1), 0, 0)

    early_node_spec = pl.BlockSpec((1, latent, nodes), early_node)
    early_edge_spec = pl.BlockSpec((1, latent, tile), early_edge)
    tile_ids = pl.BlockSpec((graphs, tile), lambda p, g, t, *_: (0, t))
    blocks = (Block(plan, 0), Block(plan, 1), Block(plan, 2))

    def grad_outs(r):
        return [sds((blocks[r].total, latent), BF)] * plan.fsdp

    all_nodes = (graphs, latent, nodes)
    all_edges = (graphs * tiles, latent, tile)
    mid = kernel_call(
        functools.partial(middle_kernel, plan, blocks[2], graphs, tiles),
        "middle",
        dict(
            pack=list(pack_rest),
            src=(source_vertex, tile_ids),
            dst=(target_vertex, tile_ids),
            h_in=(zero.h_out, early_node_spec),
            e_in=(zero.e_out, early_edge_spec),
            x_now=x_now_t,
            x_next=x_next_t,
            border=border,
            level=level,
            stats=stats,
        ),
        dict(
            hb=(node_bf, early_node_spec),
            z1=(edge_bf, early_edge_spec),
            xh=(edge_bf, early_edge_spec),
            iv=(edge_row_f32, pl.BlockSpec((1, 1, tile), early_edge)),
            grad=grad_outs(2),
            gh_out=node_f32,
            gagg_out=node_bf,
            ge_out=(edge_f32, pl.BlockSpec((1, latent, tile), late_edge)),
            count_out=(sds((1, 1), F32), sm),
        ),
        dict(
            **weight_scratch,
            **forward_scratch,
            **edge_sums,
            **node_sums,
            **outer_sums,
            loss=vmem((8, 128)),
            hb1=vmem(all_nodes, BF),
            aggl1=vmem(all_nodes, BF),
            zn1=vmem(all_nodes, BF),
            xn1=vmem(all_nodes, BF),
            ivn1=vmem((graphs, 1, nodes)),
            wan1=vmem((2 * latent, latent), BF),
            wbn1=vmem((latent, latent), BF),
            cols1=vmem((latent, 16)),
            d_bn1=vmem((latent, latent)),
            d_an1=vmem((2 * latent, latent)),
            v_n1=vmem((latent, 512)),
            hb2=vmem(all_nodes, BF),
            aggl2=vmem(all_nodes, BF),
            h_all=vmem(all_nodes),
            e_all=vmem(all_edges),
            low2=vmem((graphs * tiles, latent + 16, tile), BF),
            z12=vmem(all_edges, BF),
            xh2=vmem(all_edges, BF),
            iv2=vmem((graphs * tiles, 1, tile)),
            aux=vmem((channels, 256)),
        ),
        grid=(3, graphs, tiles),
        prefetch=dict(ids=ids, counts=node_counts),
        cost=(row_flops * 27, 40_000_000),
    )
    anywhere = pl.BlockSpec(memory_space=pl.ANY)

    def back(r, places, kept, grads, other):
        first = r == 0
        count = len(places)
        node_shape = (count, latent, nodes)
        edge_shape = (count * tiles, latent, tile)

        def any_of(**group):
            return {n: (v, anywhere) for n, v in group.items()}

        ins = dict(
            pack_in=[(v, anywhere) for v in (pack_first if first else pack_rest)],
            src=source_vertex,
            dst=target_vertex,
            **any_of(hb_in=kept.hb, z1_in=kept.z1, xh_in=kept.xh, iv_in=kept.iv),
            **any_of(gh_in=grads.gh_out, gagg_in=grads.gagg_out, ge_in=grads.ge_out),
        )
        outs = dict(grad=grad_outs(r))
        scratch = dict(
            pack=vmem((plan.fsdp, plan.total, latent), BF),
            wa=vmem((3 * latent, latent), BF),
            wb=vmem((latent, latent), BF),
            cols=vmem((latent, 16)),
            u=vmem((2 * nodes, tile), BF),
            low_e=vmem((latent + 16, tile), BF),
            **edge_sums,
            z1=vmem(edge_shape, BF),
            xh=vmem(edge_shape, BF),
            iv=vmem((count * tiles, 1, tile)),
            ge=vmem(edge_shape),
            hb=vmem(node_shape, BF),
            gh_all=vmem(node_shape),
            gagg_all=vmem(node_shape, BF),
            sems=pltpu.SemaphoreType.DMA((6 + count * tiles, 8)),
        )
        if first:
            (g,) = places
            ins.update(
                x_now=(x_now_t, pl.BlockSpec((channels, nodes), lambda *_: (0, g))),
                x_next=(x_next_t, pl.BlockSpec((channels, nodes), lambda *_: (0, g))),
                border=(border, pl.BlockSpec((1, nodes), lambda *_: (0, g))),
                link=(link_t, pl.BlockSpec((1, 4, edge_count), lambda *_: (g, 0, 0))),
            )
            if other is not None:
                ins.update(other=list(other.grad))
            scratch.update(**outer_sums, d_ee=vmem((latent, 8)), link8=vmem((8, tile)))
            scratch.update(ge_low=vmem((latent, tile), BF))
        else:
            ins.update(before_in=[(v, anywhere) for v in pack_first])
            ins.update(any_of(e_in=zero.e_out, hb0_in=zero.hb, aggl_in=zero.aggl))
            ins.update(any_of(zn_in=zero.zn, xn_in=zero.xn, ivn_in=zero.ivn))
            outs.update(
                gh_out=sds(node_shape, F32), gagg_out=sds(node_shape, BF), ge_out=(sds(edge_shape, F32), anywhere)
            )
            scratch.update(
                **node_sums,
                before=vmem((plan.fsdp, plan.total, latent), BF),
                e=vmem(edge_shape),
                hb0=vmem(node_shape, BF),
                aggl=vmem(node_shape, BF),
                zn=vmem(node_shape, BF),
                xn=vmem(node_shape, BF),
                ivn=vmem((count, 1, nodes)),
                wbn=vmem((latent, latent), BF),
                wan=vmem((2 * latent, latent), BF),
                cols1=vmem((latent, 16)),
            )
        return kernel_call(
            functools.partial(back_kernel, plan, blocks[r], first, places, tiles),
            f"back{r}_{places[0]}",
            ins,
            outs,
            scratch,
            grid=(1,),
            prefetch=prefetch,
            cost=(row_flops * 11 * count // graphs, 15_000_000 * count),
        )

    def total_of(parts):
        total = parts[0].astype(F32)
        for part in parts[1:]:
            total = total + part.astype(F32)
        return total

    def exchange_grads(bag):
        return exchange(bag.grad, "fsdp", plan.fsdp)

    def owned(got, r):
        return total_of(got).astype(BF).reshape(plan.dp, blocks[r].piece, latent)

    def reduce_owner(value):
        return lax.all_to_all(value, "dp", 0, 0, tiled=True)

    def share(parts):
        total = jnp.sum(parts.astype(F32), axis=0)
        wide = jnp.broadcast_to(total[None], (plan.dp, *total.shape))
        return lax.all_to_all(wide, "dp", 0, 0, tiled=True)

    def share_scaled(parts):
        total = jnp.sum(parts.astype(F32), axis=0)
        count = total.shape[0]
        top = jnp.max(jnp.abs(total), axis=1, keepdims=True)
        power = jnp.clip(jnp.ceil(jnp.log2(jnp.maximum(top, 1e-30))), -100.0, 100.0) - 14.0
        value = (total * jnp.exp2(-power)).astype(jnp.float16)
        row = lax.broadcasted_iota(jnp.int32, (count, latent), 0)
        lane = lax.broadcasted_iota(jnp.int32, (count, latent), 1)
        powers = jnp.sum(jnp.where(row == lane, power, 0.0), axis=0, keepdims=True)
        powers = jnp.broadcast_to(powers, (8, latent)).astype(jnp.float16)
        wide = jnp.broadcast_to(jnp.concatenate([value, powers], axis=0)[None], (plan.dp, count + 8, latent))
        got = lax.all_to_all(wide, "dp", 0, 0, tiled=True)
        powers = got[:, count : count + 1, :].astype(F32)
        scale = jnp.exp2(jnp.sum(jnp.where((row == lane)[None], powers, 0.0), axis=2, keepdims=True))
        return got[:, :count, :].astype(F32) * scale

    def after(bag, *others):
        bag.grad, held = lax.optimization_barrier((bag.grad, others))
        return held

    got2 = exchange_grads(mid)
    one = back(1, tuple(range(graphs)), mid, mid, None)
    owned2 = owned(got2, 2)
    (owned2,) = after(one, owned2)
    got1 = exchange_grads(one)
    last = None
    for g in range(graphs):
        last = back(0, (g,), zero, one, last)
        if g == 0:
            both = jnp.concatenate([owned2, owned(got1, 1)], axis=1)
            (both,) = after(last, both)
            parts = reduce_owner(both)
    (parts,) = after(last, parts)
    got0 = exchange_grads(last)
    shared = share_scaled(parts)
    owned0, shared = lax.optimization_barrier((owned(got0, 0), shared))
    whole0 = share(reduce_owner(owned0))

    def turned(group):
        return (group[0].T, *group[1:])

    weights, moments, squares = turned(weights), turned(moments), turned(squares)
    numbers = (2, 3, 4, 5, 6)

    def products(numbers):
        return [sds(weights[k].shape, F32) for k in numbers for _ in range(3)]

    early = kernel_call(
        functools.partial(update_early_kernel, plan, blocks, numbers),
        "update_early",
        dict(
            shared=shared,
            weight=[weights[k] for k in numbers],
            moment=[moments[k] for k in numbers],
            square=[squares[k] for k in numbers],
        ),
        dict(products=products(numbers), loss=(sds((1, 1), F32), sm)),
        dict(grads2=vmem((blocks[2].total, latent)), grads1=vmem((blocks[1].total, latent))),
        cost=(1000, 9_000_000),
    )

    def slot(value):
        shape = value.shape
        cut = (1, 1, *shape[2:]) if len(shape) == 4 else (1, *shape[1:])
        return value, pl.BlockSpec(cut, lambda *_: (0,) * len(shape))

    partial = (2, 3, 5)
    alone = (0, 1)
    held = [early.products[3 * numbers.index(k) + i] for k in partial for i in range(3)]

    def pick(group):
        return [group[k] for k in alone] + [slot(group[k]) for k in partial]

    late = kernel_call(
        functools.partial(update_late_kernel, plan, blocks[0], alone + partial),
        "update_late",
        dict(
            grads=whole0.reshape(blocks[0].total, latent),
            weight=pick(weights),
            moment=pick(moments),
            square=pick(squares),
            held=[(v, anywhere) for v in held],
        ),
        dict(products=products(alone), slots=[slot(v) for v in products(partial)]),
        grid=(1,),
        cost=(1000, 1_000_000),
        alias=("held", "slots"),
    )
    new = [None] * 7
    for k in numbers:
        new[k] = early.products[3 * numbers.index(k) :][:3]
    for k, v in enumerate(alone + partial):
        new[v] = (late.products + late.slots)[3 * k : 3 * k + 3]
    results = [v.T for v in new[0]]
    for k in range(1, 7):
        results += new[k]
    return (early.loss.reshape(()), mid.count_out.reshape(()), *results)


def solution(mesh):
    rows = P(("dp", "fsdp"), None)
    row = P(("dp", "fsdp"))
    weight_specs = (
        P(None, "fsdp"),
        P(None, "fsdp"),
        P(None, "fsdp", None),
        P(None, None, "fsdp", None),
        P(None, "fsdp", None),
        P(None, None, None, "fsdp"),
        P("fsdp", None),
    )
    placed = (rows, rows, row, row, rows, rows, P(("dp", "fsdp"), None, None), P(), *weight_specs * 3)
    out_specs = [P(), P()]
    for spec in weight_specs:
        out_specs += [spec] * 3

    def step(*args):
        plan = Plan(args[10].shape[2], mesh.shape["dp"], mesh.shape["fsdp"])
        return body(plan, *args)

    return jax.shard_map(
        step, mesh=mesh, in_specs=placed, out_specs=tuple(out_specs), check_vma=False
    )
```

```python
import functools

import jax
import jax.numpy as jnp
from jax import lax
from jax.experimental import pallas as pl
from jax.experimental.pallas import tpu as pltpu
from jax.sharding import PartitionSpec as P

VARS = 6
LEVELS = 13
ROUNDS = 3
STEP = 10

norm_eps = 1e-05
stat_eps = 1e-06
beta_one = 0.9
beta_two = 0.999
adam_eps = 1e-08
decay_rate = 0.01
rate_matrix = 0.03
rate_vector = 0.2

EDGE_FIRST, EDGE_SECOND, NODE_FIRST, NODE_SECOND, ROWS, OUTER = range(6)

BF = jnp.bfloat16
F32 = jnp.float32
VMEM_LIMIT = 60 * 1024 * 1024
EDGE_TILE = 1536
CHUNK = 256


def contract(a, b, da, db):
    return lax.dot_general(a, b, (((da,), (db,)), ((), ())), preferred_element_type=F32)


def nn(a, b):
    return contract(a, b, 1, 0)


def nt(a, b):
    return contract(a, b, 1, 1)


def tn(a, b):
    return contract(a, b, 0, 0)


def sigmoid(v):
    return 0.5 * jnp.tanh(0.5 * v) + 0.5


def silu(v):
    half = 0.5 * v
    return half * jnp.tanh(half) + half


def round_up(v, m):
    return (v + m - 1) // m * m


def stacked(sizes):
    offset = 0
    at = {}
    for name, size in sizes:
        at[name] = (offset, size)
        offset += size
    return at, offset


class Plan:
    def __init__(self, latent, dp_size, fsdp_size):
        self.latent = latent
        self.dp = dp_size
        self.fsdp = fsdp_size
        self.width = latent // fsdp_size
        self.half = self.width // 2
        width = self.width
        sizes = (
            (EDGE_FIRST, 3 * width),
            (EDGE_SECOND, width),
            (NODE_SECOND, width),
            (NODE_FIRST, 2 * width),
            (ROWS, 16),
            (OUTER, self.half),
        )
        self.at, self.total = stacked(sizes)


class Block:
    def __init__(self, plan, node_parts):
        width = plan.width
        sizes = [(EDGE_FIRST, 3 * width), (EDGE_SECOND, width), (ROWS, 16), (OUTER, plan.half)]
        for k in range(node_parts):
            sizes += [((NODE_FIRST, k), 2 * width), ((NODE_SECOND, k), width), ((ROWS, k), 16)]
        self.at, self.used = stacked(sizes)
        self.piece = round_up((self.used + plan.dp - 1) // plan.dp, 8)
        self.total = self.piece * plan.dp


def live_row(border, count):
    place = lax.broadcasted_iota(jnp.int32, border.shape, 1)
    return jnp.where((place < count) & (border != 1), 1.0, 0.0).astype(F32)


def group_matrix(rows, cols, flip):
    var = lax.broadcasted_iota(jnp.int32, (rows, cols), 1 if flip else 0)
    chan = lax.broadcasted_iota(jnp.int32, (rows, cols), 0 if flip else 1)
    inside = (chan >= var * LEVELS) & (chan < (var + 1) * LEVELS)
    return jnp.where(inside, 1.0, 0.0).astype(F32)


def exact(a, b):
    return lax.dot_general(
        a, b, (((1,), (0,)), ((), ())), precision=lax.Precision.HIGHEST, preferred_element_type=F32
    )


class Bag:
    pass


def kernel_call(kernel, name, ins, outs, scratch=None, grid=(), prefetch=None, cost=None, alias=None):
    scratch = scratch or {}
    prefetch = prefetch or {}
    whole = pl.BlockSpec(memory_space=pltpu.VMEM)

    def flat(group):
        return [(n, v) for n, vs in group.items() for v in (vs if isinstance(vs, list) else [vs])]

    def fill(groups, values):
        bag = Bag()
        at = 0
        for group in groups:
            for n, vs in group.items():
                count = len(vs) if isinstance(vs, list) else None
                if count is None:
                    setattr(bag, n, values[at])
                    at += 1
                else:
                    setattr(bag, n, list(values[at : at + count]))
                    at += count
        return bag

    def split(item):
        if isinstance(item, tuple):
            return item
        if not grid:
            return item, whole
        rank = len(item.shape)
        return item, pl.BlockSpec(item.shape, lambda *_: (0,) * rank)

    def run(*refs):
        kernel(fill((prefetch, ins, outs, scratch), refs))

    sources = [split(v) for _, v in flat(ins)]
    products = [split(v) for _, v in flat(outs)]
    aliases = {}
    if alias:
        first_in = [n for n, _ in flat(ins)].index(alias[0]) + len(prefetch)
        first_out = [n for n, _ in flat(outs)].index(alias[1])
        aliases = {first_in + k: first_out + k for k in range(len(ins[alias[0]]))}
    result = pl.pallas_call(
        run,
        out_shape=[v for v, _ in products],
        grid_spec=pltpu.PrefetchScalarGridSpec(
            num_scalar_prefetch=len(prefetch),
            grid=grid,
            in_specs=[spec for _, spec in sources],
            out_specs=[spec for _, spec in products],
            scratch_shapes=list(scratch.values()),
        ),
        compiler_params=pltpu.CompilerParams(vmem_limit_bytes=VMEM_LIMIT),
        input_output_aliases=aliases,
        cost_estimate=pl.CostEstimate(flops=cost[0], bytes_accessed=cost[1], transcendentals=0),
        name=name,
    )(*prefetch.values(), *[v for v, _ in sources])
    return fill((outs,), result)


def pack_round(plan, out, r, edge_first, second_layers, node_first, vectors, edge_encoder, outer):
    width = plan.width
    at = plan.at

    def put(name, value):
        start, size = at[name]
        out[start : start + size, :] = value.astype(BF)

    put(EDGE_FIRST, edge_first[r])
    put(EDGE_SECOND, second_layers[r, 0])
    put(NODE_SECOND, second_layers[r, 1])
    put(NODE_FIRST, node_first[r])
    rows = jnp.concatenate([vectors[r, 0], vectors[r, 1]], axis=0)
    if edge_encoder is None:
        low = jnp.zeros((8, width), F32)
    else:
        low = jnp.concatenate([edge_encoder[...], jnp.zeros((4, width), F32)], axis=0)
    rows = jnp.concatenate([rows, low], axis=0)
    rows = jnp.concatenate([rows, jnp.zeros((16, plan.latent - width), F32)], axis=1)
    put(ROWS, rows)
    start, size = at[OUTER]
    if outer is None:
        out[start : start + size, :] = jnp.zeros((size, plan.latent), BF)
    else:
        channels = outer.shape[1]
        wide = jnp.concatenate(
            [outer[...], jnp.zeros((width, plan.latent // 2 - channels), F32)], axis=1
        )
        put(OUTER, jnp.concatenate([wide[: plan.half], wide[plan.half :]], axis=1))


def pack_first_kernel(plan, b):
    pack_round(plan, b.pack, 0, b.ef, b.sl, b.nf, b.vec, b.ee, b.enc)


def merge_stats(stats):
    total = jnp.sum(stats, axis=0)
    count = total[:, 2:3]
    mean = total[:, 0:1] / (count * LEVELS)
    own_count = stats[:, :, 2:3] * LEVELS
    shift = stats[:, :, 0:1] / jnp.maximum(own_count, 1.0) - mean[None]
    spread = jnp.sum(stats[:, :, 1:2] + own_count * shift * shift, axis=0)
    return count, spread


def pack_rest_kernel(plan, graphs, b):
    pack_round(plan, b.pack.at[0], 1, b.ef, b.sl, b.nf, b.vec, None, None)
    pack_round(plan, b.pack.at[1], 2, b.ef, b.sl, b.nf, b.vec, None, b.dec)
    nodes = b.x_now.shape[1] // graphs
    channels = b.x_now.shape[0]
    lives = []
    for g in range(graphs):
        lives.append(live_row(b.border[:, g * nodes : (g + 1) * nodes], b.counts[g]))
    live = jnp.concatenate(lives, axis=1)
    delta = b.x_next[...] - b.x_now[...]
    count = jnp.sum(live)
    sums = jnp.sum(delta * live, axis=1, keepdims=True)
    to_var = group_matrix(8, channels, False)
    to_chan = group_matrix(channels, 8, True)
    var_sum = exact(to_var, jnp.broadcast_to(sums, (channels, 128)))
    mean = var_sum / (jnp.maximum(count, 1.0) * LEVELS)
    centered = (delta - exact(to_chan, mean)[:, 0:1]) * live
    square = jnp.sum(centered * centered, axis=1, keepdims=True)
    var_square = exact(to_var, jnp.broadcast_to(square, (channels, 128)))
    lane = lax.broadcasted_iota(jnp.int32, (8, 128), 1)
    value = jnp.where(lane == 0, var_sum, jnp.where(lane == 1, var_square, count))
    b.stats[...] = jnp.broadcast_to(value[None], b.stats.shape)


def assemble(plan, me, packs, edge_first=None, edge_second=None, node_second=None, node_first=None, cols=None, outer=None):
    width = plan.width
    latent = plan.latent
    total = jnp.zeros((latent, 16), F32)
    rowid = lax.broadcasted_iota(jnp.int32, (latent, width), 0)
    colid = lax.broadcasted_iota(jnp.int32, (latent, width), 1)
    for k, pack in enumerate(packs):
        owner = jnp.bitwise_xor(me, k)

        def put(ref, name, step):
            if ref is not None:
                start, size = plan.at[name]
                ref[pl.ds(pl.multiple_of(owner * step, 16), size), :] = pack[start : start + size, :]

        put(edge_first, EDGE_FIRST, 3 * width)
        put(edge_second, EDGE_SECOND, width)
        put(node_second, NODE_SECOND, width)
        put(node_first, NODE_FIRST, 2 * width)
        start, size = plan.at[ROWS]
        place = jnp.where(rowid == owner * width + colid, 1.0, 0.0).astype(BF)
        total = total + nt(place, pack[start : start + size, 0:width])
        if outer is not None:
            start, size = plan.at[OUTER]
            half = latent // 2
            first = pl.multiple_of(owner * width, 16)
            second = pl.multiple_of(owner * width + plan.half, 16)
            outer[pl.ds(first, size), :] = pack[start : start + size, 0:half]
            outer[pl.ds(second, size), :] = pack[start : start + size, half : 2 * half]
    cols[...] = total


def assemble_all(plan, b, packs, outer):
    assemble(plan, b.ids[0], packs, b.wa, b.wb, b.wbn, b.wan, b.cols, b.outer if outer else None)


def turn_weights(plan, b, nodes):
    latent = plan.latent
    b.b_t[...] = b.wb[...].astype(F32).T.astype(BF)
    b.pcat[:, 2 * nodes :] = b.wa[2 * latent :, :].astype(F32).T.astype(BF)


def fill_tables(u_ref, src, dst, nodes, lanes):
    count = lanes.stop - lanes.start
    place = lax.broadcasted_iota(jnp.int32, (nodes, count), 0).astype(jnp.int16)
    one = jnp.ones((nodes, count), BF)
    zero = jnp.zeros((nodes, count), BF)
    u_ref[0:nodes, lanes] = jnp.where(place == src[:, lanes].astype(jnp.int16), one, zero)
    u_ref[nodes : 2 * nodes, lanes] = jnp.where(place == dst[:, lanes].astype(jnp.int16), one, zero)


def skew(chunks):
    live = []
    waiting = list(chunks)
    while live or waiting:
        if waiting:
            live.append(waiting.pop(0))
        for item in list(reversed(live)):
            if next(item, 1) == 1:
                live.remove(item)


def norm_forward(z2, count):
    mean = jnp.sum(z2, axis=0, keepdims=True) * (1.0 / count)
    centered = z2 - mean
    var = jnp.sum(centered * centered, axis=0, keepdims=True) * (1.0 / count)
    inverse = lax.rsqrt(var + norm_eps)
    return centered * inverse, inverse


def forward_nodes_in(plan, b, state):
    latent = plan.latent
    nodes = state.shape[-1]
    low = state.astype(BF)
    b.pcat[:, 0:nodes] = tn(b.wa[0:latent, :], low).astype(BF)
    b.pcat[:, nodes : 2 * nodes] = tn(b.wa[latent : 2 * latent, :], low).astype(BF)
    b.agg[...] = jnp.zeros_like(b.agg)
    return low


def forward_edges(plan, b, src, dst, tile, get, put, kept):
    nodes = b.agg.shape[-1]
    z1_ref, xh_ref, iv_ref = kept

    def chunk(at):
        lanes = slice(at, at + CHUNK)
        fill_tables(b.u, src, dst, nodes, lanes)
        b.u[2 * nodes :, lanes] = get(lanes).astype(BF)
        yield
        z1 = nn(b.pcat[...], b.u[:, lanes])
        yield
        z1 = z1 + b.cols[:, 0:1]
        active = silu(z1).astype(BF)
        z1_ref[:, lanes] = z1.astype(BF)
        yield
        z2 = nn(b.b_t[...], active)
        yield
        z2 = z2 + b.cols[:, 1:2]
        normed, inverse = norm_forward(z2, plan.latent)
        xh_ref[:, lanes] = normed.astype(BF)
        iv_ref[:, lanes] = inverse
        e = get(lanes) + (normed * b.cols[:, 2:3] + b.cols[:, 3:4])
        if put is not None:
            put(lanes, e)
        b.new_low[:, lanes] = e.astype(BF)
        yield

    skew([chunk(at) for at in range(0, tile, CHUNK)])
    b.agg[...] += nt(b.new_low[...], b.u[nodes : 2 * nodes, :])


def forward_nodes_out(plan, b, state, low, arriving):
    latent = plan.latent
    z1 = tn(b.wan[0:latent, :], low) + tn(b.wan[latent:, :], arriving) + b.cols[:, 4:5]
    active = silu(z1).astype(BF)
    z2 = tn(b.wbn[...], active) + b.cols[:, 5:6]
    normed, inverse = norm_forward(z2, latent)
    return z1, normed, inverse, state + (normed * b.cols[:, 6:7] + b.cols[:, 7:8])


def norm_backward(grad, gain, normed, inverse, count):
    scaled = grad * gain
    mean = jnp.sum(scaled, axis=0, keepdims=True) * (1.0 / count)
    cross = jnp.sum(scaled * normed, axis=0, keepdims=True) * (1.0 / count)
    return (inverse * (scaled - mean - normed * cross)).astype(BF)


def lane_sum(value):
    total = value[:, 0:128]
    for k in range(1, value.shape[1] // 128):
        total = total + value[:, 128 * k : 128 * (k + 1)]
    return total


def backward_reset(plan, b, tile, refs):
    for ref in refs:
        ref[...] = jnp.zeros_like(ref)
    b.act[plan.latent :, :] = jnp.ones((16, tile), BF)


def backward_nodes_in(plan, weights, sums, grad, low_h, arriving, z1, normed, inverse):
    latent = plan.latent
    wan, wbn, cols = weights
    z1 = z1.astype(F32)
    normed = normed.astype(F32)
    d_an, d_bn, v_n = sums
    v_n[:, 0:128] += lane_sum(grad * normed)
    v_n[:, 128:256] += lane_sum(grad)
    low_two = norm_backward(grad, cols[:, 6:7], normed, inverse, latent)
    gate = sigmoid(z1)
    soft = z1 * gate
    d_bn[...] += nt(soft.astype(BF), low_two)
    d_active = nn(wbn[...], low_two)
    low_one = (d_active * (soft - soft * gate + gate)).astype(BF)
    v_n[:, 256:384] += lane_sum(low_one.astype(F32))
    v_n[:, 384:512] += lane_sum(low_two.astype(F32))
    d_an[0:latent, :] += nt(low_h, low_one)
    d_an[latent:, :] += nt(arriving, low_one)
    return grad + nn(wan[0:latent, :], low_one), nn(wan[latent:, :], low_one).astype(BF)


def backward_edges(plan, b, src, dst, tile, get, kept, low_e, put):
    z1_ref, xh_ref, iv_ref = kept
    latent = plan.latent
    nodes = b.gagg.shape[-1]

    def chunk(at):
        lanes = slice(at, at + CHUNK)
        fill_tables(b.u, src, dst, nodes, lanes)
        yield
        ge = nn(b.gagg[...], b.u[nodes : 2 * nodes, lanes])
        yield
        if get is not None:
            ge = ge + get(lanes)
        normed = xh_ref[:, lanes].astype(F32)
        b.v_e[:, 0:128] += lane_sum(ge * normed)
        b.v_e[:, 128:256] += lane_sum(ge)
        low_two = norm_backward(ge, b.cols[:, 2:3], normed, iv_ref[:, lanes], latent)
        b.two[:, lanes] = low_two
        yield
        d_active = nn(b.wb[...], low_two)
        yield
        z1 = z1_ref[:, lanes].astype(F32)
        gate = sigmoid(z1)
        soft = z1 * gate
        b.act[0:latent, lanes] = soft.astype(BF)
        low_one = (d_active * (soft - soft * gate + gate)).astype(BF)
        b.one[:, lanes] = low_one
        yield
        put(lanes, ge + nn(b.wa[2 * latent :, :], low_one))
        yield

    skew([chunk(at) for at in range(0, tile, CHUNK)])
    b.d_b[...] += nt(b.act[...], b.two[...])
    b.d_first[2 * latent :, :] += nt(low_e[...], b.one[...])
    b.q[...] += nt(b.one[...], b.u[0 : 2 * nodes, :])


def backward_nodes_out(plan, b, low_h):
    latent = plan.latent
    nodes = b.gagg.shape[-1]
    total = b.gh[...]
    for side in range(2):
        sums = b.q[:, side * nodes : (side + 1) * nodes]
        high = sums.astype(BF)
        rows = slice(side * latent, (side + 1) * latent)
        b.d_first[rows, :] += nt(low_h, high)
        total = total + nn(b.wa[rows, :], high)
    return total


def row_of(cols128):
    return jnp.sum(cols128.T, axis=0, keepdims=True)


def backward_emit(plan, block, b, low, outer, node_sums, before):
    latent = plan.latent
    width = plan.width
    rows = [
        b.d_first[3 * latent : 3 * latent + 1, :],
        b.d_b[latent : latent + 1, :],
        row_of(b.v_e[:, 0:128]),
        row_of(b.v_e[:, 128:256]),
        jnp.zeros((4, latent), F32),
        jnp.zeros((8, latent), F32) if low is None else low,
    ]
    groups = [(ROWS, jnp.concatenate(rows, axis=0).astype(BF))]
    for k, (_, _, v_n) in enumerate(node_sums):
        rows = [
            row_of(v_n[:, 256:384]),
            row_of(v_n[:, 384:512]),
            row_of(v_n[:, 0:128]),
            row_of(v_n[:, 128:256]),
            jnp.zeros((12, latent), F32),
        ]
        groups.append(((ROWS, k), jnp.concatenate(rows, axis=0).astype(BF)))
    rowid = lax.broadcasted_iota(jnp.int32, (latent, latent), 0)
    colid = lax.broadcasted_iota(jnp.int32, (latent, latent), 1)
    for k, out in enumerate(b.grad):
        owner = jnp.bitwise_xor(b.ids[0], k)

        def put(name, value):
            start, size = block.at[name]
            rows = slice(start, start + size)
            if before is not None:
                value = value + before[k][rows, :].astype(F32)
            out[rows, :] = value.astype(BF)

        def take(ref, step):
            return ref[pl.ds(pl.multiple_of(owner * step, 8), step), :]

        put(EDGE_FIRST, take(b.d_first, 3 * width))
        put(EDGE_SECOND, take(b.d_b, width))
        inside = (rowid == owner * width + colid) & (colid < width)
        place = jnp.where(inside, 1.0, 0.0).astype(BF)
        for name, value in groups:
            put(name, nn(value, place))
        if outer is not None:
            own = take(outer, width)
            put(OUTER, jnp.concatenate([own[: plan.half], own[plan.half :]], axis=1))
        else:
            put(OUTER, jnp.zeros((plan.half, latent), F32))
        for k2, (d_an, d_bn, _) in enumerate(node_sums):
            put((NODE_FIRST, k2), take(d_an, 2 * width))
            put((NODE_SECOND, k2), take(d_bn, width))
        if block.total > block.used:
            out[block.used :, :] = jnp.zeros((block.total - block.used, latent), BF)


def split_three(whole, lanes, period, place):
    high = whole.astype(BF).astype(F32)
    mid = (whole - high).astype(BF).astype(F32)
    rest = whole - high - mid
    lane = lax.broadcasted_iota(jnp.int32, (8, lanes), 1) % period - 3 * place
    top = lax.broadcasted_iota(jnp.int32, (8, lanes), 0) == 0
    value = jnp.where(lane == 0, high, jnp.where(lane == 1, mid, jnp.where(lane == 2, rest, 0.0)))
    return jnp.where(top, value, 0.0)


def first_kernel(plan, tiles, b):
    g = pl.program_id(0)
    t = pl.program_id(1)
    nodes = b.h_out.shape[-1]
    tile = b.z1.shape[-1]

    @pl.when((g == 0) & (t == 0))
    def _():
        assemble_all(plan, b, b.pack, True)
        turn_weights(plan, b, nodes)
        b.link8[...] = jnp.zeros_like(b.link8)

    @pl.when(t == 0)
    def _():
        chosen = jnp.where(b.border[...] == 1, b.x_next[...], b.x_now[...]).astype(BF)
        b.h[...] = nn(b.outer[:, 0 : b.x_now.shape[0]], chosen)
        b.hb[0] = forward_nodes_in(plan, b, b.h[...])

    b.link8[0:4, :] = b.link[0]

    def get(lanes):
        return nn(b.cols[:, 8:16].astype(BF), b.link8[:, lanes].astype(BF))

    def put(lanes, value):
        b.e_out[0, :, lanes] = value

    kept = (b.z1.at[0], b.xh.at[0], b.iv.at[0])
    forward_edges(plan, b, b.src[pl.ds(g, 1), :], b.dst[pl.ds(g, 1), :], tile, get, put, kept)

    @pl.when(t == tiles - 1)
    def _():
        state = b.h[...]
        b.aggl[0] = b.agg[...].astype(BF)
        z1, normed, b.ivn[0], b.h_out[0] = forward_nodes_out(plan, b, state, state.astype(BF), b.aggl[0])
        b.zn[0] = z1.astype(BF)
        b.xn[0] = normed.astype(BF)


def middle_kernel(plan, block, graphs, tiles, b):
    p = pl.program_id(0)
    g = pl.program_id(1)
    t = pl.program_id(2)
    nodes = b.gh_out.shape[-1]
    tile = b.z1.shape[-1]
    latent = plan.latent
    channels = b.x_now.shape[0]
    at = g * tiles + t
    start = (g == 0) & (t == 0)
    src = b.src[pl.ds(g, 1), :]
    dst = b.dst[pl.ds(g, 1), :]

    @pl.when((p == 0) & start)
    def _():
        assemble_all(plan, b, [r.at[0] for r in b.pack], False)
        turn_weights(plan, b, nodes)
        b.wan1[...] = b.wan[...]
        b.wbn1[...] = b.wbn[...]
        b.cols1[...] = b.cols[...]
        refs = (b.d_first, b.d_b, b.v_e, b.d_bn, b.d_an, b.v_n, b.d_bn1, b.d_an1, b.v_n1, b.d_outer, b.loss)
        backward_reset(plan, b, tile, refs)
        count, spread = merge_stats(b.stats[...])
        scale = lax.rsqrt(spread / (count * LEVELS) + stat_eps)
        b.aux[:, 0:128] = exact(group_matrix(channels, 8, True), jnp.broadcast_to(scale, (8, 128)))
        b.aux[:, 128:256] = jnp.broadcast_to(count[0:1] * channels, (channels, 128))
        b.count_out[0, 0] = jnp.sum(count[0:1]) * channels

    @pl.when((p == 1) & start)
    def _():
        assemble_all(plan, b, [r.at[1] for r in b.pack], True)
        turn_weights(plan, b, nodes)

    ends = (g == graphs - 1) & (t == tiles - 1)

    def joined(ref):
        return jnp.concatenate([ref[k] for k in range(graphs)], axis=1)

    def part(value, k):
        return value[:, k * nodes : (k + 1) * nodes]

    @pl.when((p == 0) & (t == 0))
    def _():
        b.h_all[g] = b.h_in[0]
        low = forward_nodes_in(plan, b, b.h_in[0])
        b.hb[0] = low
        b.hb1[g] = low

    @pl.when(p == 0)
    def _():
        def get(lanes):
            return b.e_in[0, :, lanes]

        def put(lanes, value):
            b.e_all[at, :, lanes] = value

        forward_edges(plan, b, src, dst, tile, get, put, (b.z1.at[0], b.xh.at[0], b.iv.at[0]))

    @pl.when((p == 0) & (t == tiles - 1))
    def _():
        b.aggl1[g] = b.agg[...].astype(BF)

    @pl.when((p == 0) & ends)
    def _():
        z1, normed, inverse, state = forward_nodes_out(plan, b, joined(b.h_all), joined(b.hb1), joined(b.aggl1))
        for k in range(graphs):
            b.zn1[k] = part(z1, k).astype(BF)
            b.xn1[k] = part(normed, k).astype(BF)
            b.ivn1[k] = part(inverse, k)
            b.h_all[k] = part(state, k)

    @pl.when((p == 1) & (t == 0))
    def _():
        b.hb2[g] = forward_nodes_in(plan, b, b.h_all[g])

    @pl.when(p == 1)
    def _():
        b.low2[at, latent:, :] = jnp.ones((16, tile), BF)

        def get(lanes):
            return b.e_all[at, :, lanes]

        forward_edges(plan, b, src, dst, tile, get, None, (b.z12.at[at], b.xh2.at[at], b.iv2.at[at]))
        b.low2[at, 0:latent, :] = b.u[2 * nodes :, :]

    @pl.when((p == 1) & (t == tiles - 1))
    def _():
        b.aggl2[g] = b.agg[...].astype(BF)

    @pl.when((p == 1) & ends)
    def _():
        z1, normed, inverse, state = forward_nodes_out(plan, b, joined(b.h_all), joined(b.hb2), joined(b.aggl2))
        final_low = state.astype(BF)
        delta = b.x_next[...] - b.x_now[...]
        scale = b.aux[:, 0:1]
        norm_count = b.aux[:, 128:129]
        predicted = tn(b.outer[...], final_low)[0:channels]
        misfit = (predicted - delta) * scale
        lives = [live_row(part(b.border, k), b.counts[k]) for k in range(graphs)]
        level = jnp.broadcast_to(b.level[...].astype(F32), (8, channels)).T[:, 0:1]
        weighting = (level + 1.0) / LEVELS * jnp.concatenate(lives, axis=1)
        b.loss[...] += jnp.broadcast_to(jnp.sum(weighting * misfit * misfit), b.loss.shape)
        grad_pred = (2.0 * weighting * misfit * scale / norm_count).astype(BF)
        b.d_outer[:, 0:channels] += nt(final_low, grad_pred)
        grad, arriving = backward_nodes_in(
            plan,
            (b.wan, b.wbn, b.cols),
            (b.d_an, b.d_bn, b.v_n),
            nn(b.outer[:, 0:channels], grad_pred),
            joined(b.hb2),
            joined(b.aggl2),
            z1,
            normed,
            inverse,
        )
        for k in range(graphs):
            b.h_all[k] = part(grad, k)
            b.aggl2[k] = part(arriving, k)

    @pl.when((p == 2) & (t == 0))
    def _():
        b.gh[...] = b.h_all[g]
        b.gagg[...] = b.aggl2[g]
        b.q[...] = jnp.zeros_like(b.q)

    @pl.when(p == 2)
    def _():
        def put(lanes, value):
            b.ge_out[0, :, lanes] = value

        kept = (b.z12.at[at], b.xh2.at[at], b.iv2.at[at])
        backward_edges(plan, b, src, dst, tile, None, kept, b.low2.at[at], put)

    @pl.when((p == 2) & (t == tiles - 1))
    def _():
        b.h_all[g] = backward_nodes_out(plan, b, b.hb2[g])

    @pl.when((p == 2) & ends)
    def _():
        grad, arriving = backward_nodes_in(
            plan,
            (b.wan1, b.wbn1, b.cols1),
            (b.d_an1, b.d_bn1, b.v_n1),
            joined(b.h_all),
            joined(b.hb1),
            joined(b.aggl1),
            joined(b.zn1),
            joined(b.xn1),
            joined(b.ivn1),
        )
        for k in range(graphs):
            b.gh_out[k] = part(grad, k)
            b.gagg_out[k] = part(arriving, k)
        low = split_three(b.loss[0:1, 0:1], latent, plan.width, b.ids[0])
        sums = ((b.d_an, b.d_bn, b.v_n), (b.d_an1, b.d_bn1, b.v_n1))
        backward_emit(plan, block, b, low, b.d_outer, sums, None)


def back_kernel(plan, block, first, places, tiles, b):
    tile = b.u.shape[-1]
    latent = plan.latent

    def copies(pairs, row):
        return [pltpu.make_async_copy(x, y, b.sems.at[row, k]) for k, (x, y) in enumerate(pairs)]

    picked = b.pack_in if first else [r.at[0] for r in b.pack_in]
    weights = copies([(x, b.pack.at[k]) for k, x in enumerate(picked)], 0)
    early = []
    late = []
    moves = []
    ends = []
    for k, g in enumerate(places):
        own = g if b.gh_in.shape[0] > 1 else 0
        pairs = [(b.gagg_in.at[own], b.gagg_all.at[k]), (b.gh_in.at[own], b.gh_all.at[k])]
        early.append(copies(pairs, 1 + k))
        pairs = [(b.hb_in.at[g], b.hb.at[k])]
        if not first:
            nodes_in = ((b.hb0_in, b.hb0), (b.aggl_in, b.aggl), (b.zn_in, b.zn), (b.xn_in, b.xn), (b.ivn_in, b.ivn))
            pairs += [(x.at[g], y.at[k]) for x, y in nodes_in]
        late.append(copies(pairs, 3 + k))
        for t in range(tiles):
            at = k * tiles + t
            place = g * tiles + t
            source = place if b.ge_in.shape[0] > tiles else t
            pairs = [(b.z1_in.at[place], b.z1.at[at]), (b.xh_in.at[place], b.xh.at[at])]
            pairs += [(b.iv_in.at[place], b.iv.at[at]), (b.ge_in.at[source], b.ge.at[at])]
            if not first:
                pairs.append((b.e_in.at[place], b.e.at[at]))
                ends.append(pltpu.make_async_copy(b.ge.at[at], b.ge_out.at[at], b.sems.at[5 + at, 6]))
            moves.append(copies(pairs, 5 + at))
    rest = [] if first else copies([(x, b.before.at[k]) for k, x in enumerate(b.before_in)], 5 + len(moves))
    for group in (weights, early[0], moves[0], *moves[1:], *early[1:], *late, rest):
        for copy in group:
            copy.start()

    def wait(group):
        for copy in group:
            copy.wait()

    sums = [b.d_first, b.d_b, b.v_e]
    sums += [b.d_outer, b.d_ee, b.link8] if first else [b.d_bn, b.d_an, b.v_n]
    backward_reset(plan, b, tile, sums)
    b.low_e[latent:, :] = jnp.ones((16, tile), BF)
    wait(weights)
    assemble(plan, b.ids[0], [b.pack.at[k] for k in range(plan.fsdp)], b.wa, b.wb, cols=b.cols)
    for k, g in enumerate(places):
        wait(early[k])
        b.gagg[...] = b.gagg_all[k]
        b.gh[...] = b.gh_all[k]
        b.q[...] = jnp.zeros_like(b.q)
        for t in range(tiles):
            at = k * tiles + t
            wait(moves[at])
            lanes = slice(t * tile, (t + 1) * tile)
            kept = (b.z1.at[at], b.xh.at[at], b.iv.at[at])

            def get(lanes, at=at):
                return b.ge[at, :, lanes]

            if first:
                b.link8[0:4, :] = b.link[k, :, lanes]
                b.low_e[0:latent, :] = nn(b.cols[:, 8:16].astype(BF), b.link8[...].astype(BF)).astype(BF)

                def put(lanes, value):
                    b.ge_low[:, lanes] = value.astype(BF)
            else:
                b.low_e[0:latent, :] = b.e[at].astype(BF)

                def put(lanes, value, at=at):
                    b.ge[at, :, lanes] = value

            src = b.src[g : g + 1, lanes]
            dst = b.dst[g : g + 1, lanes]
            backward_edges(plan, b, src, dst, tile, get, kept, b.low_e, put)
            if first:
                b.d_ee[...] += nt(b.ge_low[...], b.link8[...].astype(BF))
            else:
                ends[at].start()
        wait(late[k])
        total = backward_nodes_out(plan, b, b.hb[k])
        if first:
            chosen = jnp.where(b.border[...] == 1, b.x_next[...], b.x_now[...]).astype(BF)
            b.d_outer[:, 0 : b.x_now.shape[0]] += nt(total.astype(BF), chosen)
        else:
            if k == 0:
                wait(rest)
                packs = [b.before.at[k] for k in range(plan.fsdp)]
                assemble(plan, b.ids[0], packs, node_second=b.wbn, node_first=b.wan, cols=b.cols1)
            b.gh_out[k], b.gagg_out[k] = backward_nodes_in(
                plan,
                (b.wan, b.wbn, b.cols1),
                (b.d_an, b.d_bn, b.v_n),
                total,
                b.hb0[k],
                b.aggl[k],
                b.zn[k],
                b.xn[k],
                b.ivn[k],
            )
    if first:
        backward_emit(plan, block, b, b.d_ee[...].T, b.d_outer, (), b.other if places[0] > 0 else None)
    else:
        backward_emit(plan, block, b, None, None, ((b.d_an, b.d_bn, b.v_n),), None)
    wait(ends)


def adam_math(weight, moment, square, gradient, rate):
    moment_new = beta_one * moment + (1.0 - beta_one) * gradient
    square_new = beta_two * square + (1.0 - beta_two) * gradient * gradient
    direction = (
        moment_new
        * (1.0 / (1.0 - beta_one**STEP))
        / (jnp.sqrt(square_new * (1.0 / (1.0 - beta_two**STEP))) + adam_eps)
    )
    return (moment_new, square_new, weight - rate * (direction + decay_rate * weight))


def apply_update(b, k, index, gradient, rate):
    new = adam_math(b.weight[k][index], b.moment[k][index], b.square[k][index], gradient, rate)
    for ref, value in zip(b.new[k], new):
        ref[index] = value


def by_number(b, numbers, products):
    for group in (b.weight, b.moment, b.square):
        group[:] = [group[numbers.index(k)] if k in numbers else None for k in range(7)]
    b.new = [products[3 * numbers.index(k) : 3 * numbers.index(k) + 3] if k in numbers else None for k in range(7)]


def part_of(ref, block, name):
    start, size = block.at[name]
    return ref[start : start + size, :]


def update_edge(plan, b, ref, block, at):
    apply_update(b, 2, at, part_of(ref, block, EDGE_FIRST), rate_matrix)
    apply_update(b, 3, (at, 0), part_of(ref, block, EDGE_SECOND), rate_matrix)
    rows = part_of(ref, block, ROWS)
    apply_update(b, 5, (at, 0), rows[0:4, 0 : plan.width], rate_vector)
    half = plan.latent // 2
    wide = part_of(ref, block, OUTER)
    return rows, jnp.concatenate([wide[:, 0:half], wide[:, half:]], axis=0)


def update_early_kernel(plan, blocks, numbers, b):
    by_number(b, numbers, b.products)
    width = plan.width
    for source in range(plan.dp):
        for target, block, start in ((b.grads2, blocks[2], 0), (b.grads1, blocks[1], blocks[2].piece)):
            rows = slice(source * block.piece, (source + 1) * block.piece)
            target[rows, :] = b.shared[source, start : start + block.piece, :]
    rows, outer = update_edge(plan, b, b.grads2, blocks[2], 2)
    apply_update(b, 6, Ellipsis, outer[:, 0 : b.weight[6].shape[1]], rate_matrix)
    lane = lax.broadcasted_iota(jnp.int32, (1, plan.latent), 1)
    b.loss[0, 0] = jnp.sum(jnp.where(lane < width, rows[8:9, :], 0.0))
    update_edge(plan, b, b.grads1, blocks[1], 1)
    for r, ref, block, k in ((2, b.grads2, blocks[2], 0), (1, b.grads2, blocks[2], 1), (0, b.grads1, blocks[1], 0)):
        apply_update(b, 4, r, part_of(ref, block, (NODE_FIRST, k)), rate_matrix)
        apply_update(b, 3, (r, 1), part_of(ref, block, (NODE_SECOND, k)), rate_matrix)
        apply_update(b, 5, (r, 1), part_of(ref, block, (ROWS, k))[0:4, 0:width], rate_vector)


def update_late_kernel(plan, block, numbers, b):
    by_number(b, numbers, b.products + b.slots)
    rows, outer = update_edge(plan, b, b.grads, block, 0)
    apply_update(b, 0, Ellipsis, outer[:, 0 : b.weight[0].shape[1]], rate_matrix)
    apply_update(b, 1, Ellipsis, rows[8:12, 0 : plan.width], rate_matrix)


def body(plan, *args):
    x_now, x_next, node_counts, border_flag, source_vertex, target_vertex, link_features, level_ids = args[:8]
    weights = args[8:15]
    moments = args[15:22]
    squares = args[22:29]
    encoder, edge_encoder, edge_first, second_layers, node_first, vectors, decoder = weights
    graphs, edge_count = source_vertex.shape
    nodes = x_now.shape[0] // graphs
    channels = x_now.shape[1]
    latent = plan.latent
    tile = EDGE_TILE
    tiles = edge_count // tile
    x_now_t = x_now.T
    x_next_t = x_next.T
    border = border_flag.reshape(1, -1)
    link_t = jnp.transpose(link_features, (0, 2, 1))
    level = level_ids.reshape(1, -1)
    ids = jnp.stack([lax.axis_index("fsdp"), lax.axis_index("dp")]).astype(jnp.int32)

    sm = pl.BlockSpec(memory_space=pltpu.SMEM)
    sds = jax.ShapeDtypeStruct
    pack_shape = sds((plan.total, latent), BF)
    devices = plan.dp * plan.fsdp

    def across(value, axis, size, mask):
        return lax.ppermute(value, axis, [(j, j ^ mask) for j in range(size)])

    def spread_chain(own, beside):
        got = [own]
        for k in range(1, plan.fsdp):
            source = got[k & (k - 1)]
            if k & (k - 1):
                source, beside = lax.optimization_barrier((source, beside))
            got.append(across(source, "fsdp", plan.fsdp, k & -k))
        return got, beside

    def spread_direct(own, axis, size):
        return [own] + [across(own, axis, size, k) for k in range(1, size)]

    def exchange(parts, axis, size):
        return [parts[0]] + [across(parts[k], axis, size, k) for k in range(1, size)]

    raw = dict(ef=edge_first, sl=second_layers, nf=node_first, vec=vectors)
    start = kernel_call(
        functools.partial(pack_first_kernel, plan),
        "pack_first",
        dict(**raw, ee=edge_encoder, enc=encoder.T),
        dict(pack=pack_shape),
        cost=(1000, 3_000_000),
    )
    rest = kernel_call(
        functools.partial(pack_rest_kernel, plan, graphs),
        "pack_rest",
        dict(counts=(node_counts, sm), **raw, dec=decoder, x_now=x_now_t, x_next=x_next_t, border=border),
        dict(pack=sds((2, plan.total, latent), BF), stats=sds((devices, 8, 128), F32)),
        cost=(1000, 8_000_000),
    )
    pack_first, (_, ids, level) = spread_chain(start.pack, (rest.pack, ids, level))
    pack_rest = spread_direct(rest.pack, "fsdp", plan.fsdp)
    stats = lax.all_to_all(rest.stats, ("dp", "fsdp"), 0, 0, tiled=True)

    ids_spec = pl.BlockSpec((graphs, tile), lambda g, t, *_: (0, t))
    x_spec = pl.BlockSpec((channels, nodes), lambda g, t, *_: (0, g))
    border_spec = pl.BlockSpec((1, nodes), lambda g, t, *_: (0, g))
    link_spec = pl.BlockSpec((1, 4, tile), lambda g, t, *_: (g, 0, t))
    node_spec = pl.BlockSpec((1, latent, nodes), lambda g, t, *_: (g, 0, 0))
    node_row = pl.BlockSpec((1, 1, nodes), lambda g, t, *_: (g, 0, 0))
    edge_spec = pl.BlockSpec((1, latent, tile), lambda g, t, *_: (g * tiles + t, 0, 0))
    edge_row = pl.BlockSpec((1, 1, tile), lambda g, t, *_: (g * tiles + t, 0, 0))

    node_f32 = sds((graphs, latent, nodes), F32)
    node_bf = sds((graphs, latent, nodes), BF)
    node_row_f32 = sds((graphs, 1, nodes), F32)
    edge_f32 = sds((graphs * tiles, latent, tile), F32)
    edge_bf = sds((graphs * tiles, latent, tile), BF)
    edge_row_f32 = sds((graphs * tiles, 1, tile), F32)

    def vmem(shape, kind=F32):
        return pltpu.VMEM(shape, kind)

    weight_scratch = dict(
        wa=vmem((3 * latent, latent), BF),
        wb=vmem((latent, latent), BF),
        wbn=vmem((latent, latent), BF),
        wan=vmem((2 * latent, latent), BF),
        cols=vmem((latent, 16)),
        outer=vmem((latent, latent // 2), BF),
        u=vmem((2 * nodes + latent, tile), BF),
    )
    forward_scratch = dict(
        b_t=vmem((latent, latent), BF),
        pcat=vmem((latent, 2 * nodes + latent), BF),
        new_low=vmem((latent, tile), BF),
        agg=vmem((latent, nodes)),
    )
    edge_sums = dict(
        act=vmem((latent + 16, tile), BF),
        one=vmem((latent, tile), BF),
        two=vmem((latent, tile), BF),
        gh=vmem((latent, nodes)),
        gagg=vmem((latent, nodes), BF),
        q=vmem((latent, 2 * nodes)),
        d_first=vmem((3 * latent + 16, latent)),
        d_b=vmem((latent + 16, latent)),
        v_e=vmem((latent, 256)),
    )
    node_sums = dict(
        d_bn=vmem((latent, latent)),
        d_an=vmem((2 * latent, latent)),
        v_n=vmem((latent, 512)),
    )
    outer_sums = dict(d_outer=vmem((latent, latent // 2)))
    row_flops = 2 * latent * latent * graphs * edge_count
    prefetch = dict(ids=ids)

    zero = kernel_call(
        functools.partial(first_kernel, plan, tiles),
        "first",
        dict(
            pack=list(pack_first),
            src=(source_vertex, ids_spec),
            dst=(target_vertex, ids_spec),
            x_now=(x_now_t, x_spec),
            x_next=(x_next_t, x_spec),
            border=(border, border_spec),
            link=(link_t, link_spec),
        ),
        dict(
            h_out=(node_f32, node_spec),
            hb=(node_bf, node_spec),
            aggl=(node_bf, node_spec),
            zn=(node_bf, node_spec),
            xn=(node_bf, node_spec),
            ivn=(node_row_f32, node_row),
            z1=(edge_bf, edge_spec),
            xh=(edge_bf, edge_spec),
            iv=(edge_row_f32, edge_row),
            e_out=(edge_f32, edge_spec),
        ),
        dict(**weight_scratch, **forward_scratch, link8=vmem((8, tile)), h=vmem((latent, nodes))),
        grid=(graphs, tiles),
        prefetch=prefetch,
        cost=(row_flops * 8, 20_000_000),
    )

    last_at = graphs * tiles - 1

    def early_edge(p, g, t, *_):
        return (jnp.where(p == 0, g * tiles + t, last_at), 0, 0)

    def late_edge(p, g, t, *_):
        return (jnp.where(p == 2, g * tiles + t, 0), 0, 0)

    def early_node(p, g, t, *_):
        return (jnp.where(p == 0, g, graphs - 1), 0, 0)

    early_node_spec = pl.BlockSpec((1, latent, nodes), early_node)
    early_edge_spec = pl.BlockSpec((1, latent, tile), early_edge)
    tile_ids = pl.BlockSpec((graphs, tile), lambda p, g, t, *_: (0, t))
    blocks = (Block(plan, 0), Block(plan, 1), Block(plan, 2))

    def grad_outs(r):
        return [sds((blocks[r].total, latent), BF)] * plan.fsdp

    all_nodes = (graphs, latent, nodes)
    all_edges = (graphs * tiles, latent, tile)
    mid = kernel_call(
        functools.partial(middle_kernel, plan, blocks[2], graphs, tiles),
        "middle",
        dict(
            pack=list(pack_rest),
            src=(source_vertex, tile_ids),
            dst=(target_vertex, tile_ids),
            h_in=(zero.h_out, early_node_spec),
            e_in=(zero.e_out, early_edge_spec),
            x_now=x_now_t,
            x_next=x_next_t,
            border=border,
            level=level,
            stats=stats,
        ),
        dict(
            hb=(node_bf, early_node_spec),
            z1=(edge_bf, early_edge_spec),
            xh=(edge_bf, early_edge_spec),
            iv=(edge_row_f32, pl.BlockSpec((1, 1, tile), early_edge)),
            grad=grad_outs(2),
            gh_out=node_f32,
            gagg_out=node_bf,
            ge_out=(edge_f32, pl.BlockSpec((1, latent, tile), late_edge)),
            count_out=(sds((1, 1), F32), sm),
        ),
        dict(
            **weight_scratch,
            **forward_scratch,
            **edge_sums,
            **node_sums,
            **outer_sums,
            loss=vmem((8, 128)),
            hb1=vmem(all_nodes, BF),
            aggl1=vmem(all_nodes, BF),
            zn1=vmem(all_nodes, BF),
            xn1=vmem(all_nodes, BF),
            ivn1=vmem((graphs, 1, nodes)),
            wan1=vmem((2 * latent, latent), BF),
            wbn1=vmem((latent, latent), BF),
            cols1=vmem((latent, 16)),
            d_bn1=vmem((latent, latent)),
            d_an1=vmem((2 * latent, latent)),
            v_n1=vmem((latent, 512)),
            hb2=vmem(all_nodes, BF),
            aggl2=vmem(all_nodes, BF),
            h_all=vmem(all_nodes),
            e_all=vmem(all_edges),
            low2=vmem((graphs * tiles, latent + 16, tile), BF),
            z12=vmem(all_edges, BF),
            xh2=vmem(all_edges, BF),
            iv2=vmem((graphs * tiles, 1, tile)),
            aux=vmem((channels, 256)),
        ),
        grid=(3, graphs, tiles),
        prefetch=dict(ids=ids, counts=node_counts),
        cost=(row_flops * 27, 40_000_000),
    )
    anywhere = pl.BlockSpec(memory_space=pl.ANY)

    def back(r, places, kept, grads, other):
        first = r == 0
        count = len(places)
        node_shape = (count, latent, nodes)
        edge_shape = (count * tiles, latent, tile)

        def any_of(**group):
            return {n: (v, anywhere) for n, v in group.items()}

        ins = dict(
            pack_in=[(v, anywhere) for v in (pack_first if first else pack_rest)],
            src=source_vertex,
            dst=target_vertex,
            **any_of(hb_in=kept.hb, z1_in=kept.z1, xh_in=kept.xh, iv_in=kept.iv),
            **any_of(gh_in=grads.gh_out, gagg_in=grads.gagg_out, ge_in=grads.ge_out),
        )
        outs = dict(grad=grad_outs(r))
        scratch = dict(
            pack=vmem((plan.fsdp, plan.total, latent), BF),
            wa=vmem((3 * latent, latent), BF),
            wb=vmem((latent, latent), BF),
            cols=vmem((latent, 16)),
            u=vmem((2 * nodes, tile), BF),
            low_e=vmem((latent + 16, tile), BF),
            **edge_sums,
            z1=vmem(edge_shape, BF),
            xh=vmem(edge_shape, BF),
            iv=vmem((count * tiles, 1, tile)),
            ge=vmem(edge_shape),
            hb=vmem(node_shape, BF),
            gh_all=vmem(node_shape),
            gagg_all=vmem(node_shape, BF),
            sems=pltpu.SemaphoreType.DMA((6 + count * tiles, 8)),
        )
        if first:
            (g,) = places
            ins.update(
                x_now=(x_now_t, pl.BlockSpec((channels, nodes), lambda *_: (0, g))),
                x_next=(x_next_t, pl.BlockSpec((channels, nodes), lambda *_: (0, g))),
                border=(border, pl.BlockSpec((1, nodes), lambda *_: (0, g))),
                link=(link_t, pl.BlockSpec((1, 4, edge_count), lambda *_: (g, 0, 0))),
            )
            if other is not None:
                ins.update(other=list(other.grad))
            scratch.update(**outer_sums, d_ee=vmem((latent, 8)), link8=vmem((8, tile)))
            scratch.update(ge_low=vmem((latent, tile), BF))
        else:
            ins.update(before_in=[(v, anywhere) for v in pack_first])
            ins.update(any_of(e_in=zero.e_out, hb0_in=zero.hb, aggl_in=zero.aggl))
            ins.update(any_of(zn_in=zero.zn, xn_in=zero.xn, ivn_in=zero.ivn))
            outs.update(
                gh_out=sds(node_shape, F32), gagg_out=sds(node_shape, BF), ge_out=(sds(edge_shape, F32), anywhere)
            )
            scratch.update(
                **node_sums,
                before=vmem((plan.fsdp, plan.total, latent), BF),
                e=vmem(edge_shape),
                hb0=vmem(node_shape, BF),
                aggl=vmem(node_shape, BF),
                zn=vmem(node_shape, BF),
                xn=vmem(node_shape, BF),
                ivn=vmem((count, 1, nodes)),
                wbn=vmem((latent, latent), BF),
                wan=vmem((2 * latent, latent), BF),
                cols1=vmem((latent, 16)),
            )
        return kernel_call(
            functools.partial(back_kernel, plan, blocks[r], first, places, tiles),
            f"back{r}_{places[0]}",
            ins,
            outs,
            scratch,
            grid=(1,),
            prefetch=prefetch,
            cost=(row_flops * 11 * count // graphs, 15_000_000 * count),
        )

    def total_of(parts):
        total = parts[0].astype(F32)
        for part in parts[1:]:
            total = total + part.astype(F32)
        return total

    def exchange_grads(bag):
        return exchange(bag.grad, "fsdp", plan.fsdp)

    def owned(got, r):
        return total_of(got).astype(BF).reshape(plan.dp, blocks[r].piece, latent)

    def reduce_owner(value):
        return lax.all_to_all(value, "dp", 0, 0, tiled=True)

    def share(parts):
        total = jnp.sum(parts.astype(F32), axis=0)
        wide = jnp.broadcast_to(total[None], (plan.dp, *total.shape))
        return lax.all_to_all(wide, "dp", 0, 0, tiled=True)

    def share_scaled(parts):
        total = jnp.sum(parts.astype(F32), axis=0)
        count = total.shape[0]
        top = jnp.max(jnp.abs(total), axis=1, keepdims=True)
        power = jnp.clip(jnp.ceil(jnp.log2(jnp.maximum(top, 1e-30))), -100.0, 100.0) - 14.0
        value = (total * jnp.exp2(-power)).astype(jnp.float16)
        row = lax.broadcasted_iota(jnp.int32, (count, latent), 0)
        lane = lax.broadcasted_iota(jnp.int32, (count, latent), 1)
        powers = jnp.sum(jnp.where(row == lane, power, 0.0), axis=0, keepdims=True)
        powers = jnp.broadcast_to(powers, (8, latent)).astype(jnp.float16)
        wide = jnp.broadcast_to(jnp.concatenate([value, powers], axis=0)[None], (plan.dp, count + 8, latent))
        got = lax.all_to_all(wide, "dp", 0, 0, tiled=True)
        powers = got[:, count : count + 1, :].astype(F32)
        scale = jnp.exp2(jnp.sum(jnp.where((row == lane)[None], powers, 0.0), axis=2, keepdims=True))
        return got[:, :count, :].astype(F32) * scale

    def after(bag, *others):
        bag.grad, held = lax.optimization_barrier((bag.grad, others))
        return held

    got2 = exchange_grads(mid)
    one = back(1, tuple(range(graphs)), mid, mid, None)
    owned2 = owned(got2, 2)
    (owned2,) = after(one, owned2)
    got1 = exchange_grads(one)
    last = None
    for g in range(graphs):
        last = back(0, (g,), zero, one, last)
        if g == 0:
            both = jnp.concatenate([owned2, owned(got1, 1)], axis=1)
            (both,) = after(last, both)
            parts = reduce_owner(both)
    (parts,) = after(last, parts)
    got0 = exchange_grads(last)
    shared = share_scaled(parts)
    owned0, shared = lax.optimization_barrier((owned(got0, 0), shared))
    whole0 = share_scaled(reduce_owner(owned0))

    def turned(group):
        return (group[0].T, *group[1:])

    weights, moments, squares = turned(weights), turned(moments), turned(squares)
    numbers = (2, 3, 4, 5, 6)

    def products(numbers):
        return [sds(weights[k].shape, F32) for k in numbers for _ in range(3)]

    early = kernel_call(
        functools.partial(update_early_kernel, plan, blocks, numbers),
        "update_early",
        dict(
            shared=shared,
            weight=[weights[k] for k in numbers],
            moment=[moments[k] for k in numbers],
            square=[squares[k] for k in numbers],
        ),
        dict(products=products(numbers), loss=(sds((1, 1), F32), sm)),
        dict(grads2=vmem((blocks[2].total, latent)), grads1=vmem((blocks[1].total, latent))),
        cost=(1000, 9_000_000),
    )

    def slot(value):
        shape = value.shape
        cut = (1, 1, *shape[2:]) if len(shape) == 4 else (1, *shape[1:])
        return value, pl.BlockSpec(cut, lambda *_: (0,) * len(shape))

    partial = (2, 3, 5)
    alone = (0, 1)
    held = [early.products[3 * numbers.index(k) + i] for k in partial for i in range(3)]

    def pick(group):
        return [group[k] for k in alone] + [slot(group[k]) for k in partial]

    late = kernel_call(
        functools.partial(update_late_kernel, plan, blocks[0], alone + partial),
        "update_late",
        dict(
            grads=whole0.reshape(blocks[0].total, latent),
            weight=pick(weights),
            moment=pick(moments),
            square=pick(squares),
            held=[(v, anywhere) for v in held],
        ),
        dict(products=products(alone), slots=[slot(v) for v in products(partial)]),
        grid=(1,),
        cost=(1000, 1_000_000),
        alias=("held", "slots"),
    )
    new = [None] * 7
    for k in numbers:
        new[k] = early.products[3 * numbers.index(k) :][:3]
    for k, v in enumerate(alone + partial):
        new[v] = (late.products + late.slots)[3 * k : 3 * k + 3]
    results = [v.T for v in new[0]]
    for k in range(1, 7):
        results += new[k]
    return (early.loss.reshape(()), mid.count_out.reshape(()), *results)


def solution(mesh):
    rows = P(("dp", "fsdp"), None)
    row = P(("dp", "fsdp"))
    weight_specs = (
        P(None, "fsdp"),
        P(None, "fsdp"),
        P(None, "fsdp", None),
        P(None, None, "fsdp", None),
        P(None, "fsdp", None),
        P(None, None, None, "fsdp"),
        P("fsdp", None),
    )
    placed = (rows, rows, row, row, rows, rows, P(("dp", "fsdp"), None, None), P(), *weight_specs * 3)
    out_specs = [P(), P()]
    for spec in weight_specs:
        out_specs += [spec] * 3

    def step(*args):
        plan = Plan(args[10].shape[2], mesh.shape["dp"], mesh.shape["fsdp"])
        return body(plan, *args)

    return jax.shard_map(
        step, mesh=mesh, in_specs=placed, out_specs=tuple(out_specs), check_vma=False
    )
```
